32 devices in a mesh: members: 2 (over x), tiles: 16 (over z, y, core).
Axes of the slice: x: 2, y: 2, z: 4, core: 2. Of those that a mesh axis runs over, the one named last changes fastest.
Arguments:
- atm_state: float32 [256, 3072], P(('members', 'tiles')), parts along dimension 0, may hold values from -6 to 6
- atm_kappa: float32 [3072], replicated, may hold values from 0.05 to 0.2
- forcing: bfloat16 [8, 256, 3072], P(None, ('members', 'tiles')), parts along dimension 1, may hold values from -6 to 6
- flux_gain: float32 [8], replicated, may hold values from 0.5 to 1.5
- remap_weight: bfloat16 [4096, 128, 128], P('tiles'), may hold values from -0.5 to 0.5
- remap_source: int32 [4096], P('tiles'), may hold values from 0 to 191
- remap_owner: int32 [4096, 1], P('tiles'), may hold values from 0 to 15; in each aligned block of 256 rows (0 to 255, 256 to 511, ...) at most 32 rows name the same one
- remap_dest: int32 [4096], P('tiles'), may hold values from 0 to 447
- ocean_state: float32 [512, 3584], P(('members', 'tiles')), parts along dimension 0, may hold values from -6 to 6
- ocean_nu: float32 [3584], replicated, may hold values from 0.05 to 0.2
- flux_coef: float32 [8], replicated, may hold values from 0.05 to 0.3
Outputs:
- atm_next: float32 [256, 3072], P(('members', 'tiles')), parts along dimension 0
- ocean_next: float32 [512, 3584], P(('members', 'tiles')), parts along dimension 0
- atm_feedback: float32 [256, 3072], P(('members', 'tiles')), parts along dimension 0
The draws below stay inside these ranges and needn't reach their ends.
There are 2 independent parts, one for each index of `members`. The reference program is written for one: setup_inputs(seed, part) draws one part's arguments, and reference() takes and returns one part's arrays. A program takes and returns all parts, laid end to end along the dimension named above; an argument that names none is the same for every part. Nothing has to cross between parts.
Inputs may be any that keep to these rules, and one draw needn't show every extreme that they name: `remap_owner`: among the 256 blocks of one device no owner is named more than 32 times, a bound that some block reaches.
All inputs are finite; a program needn't handle non-finite values.
Results may differ from the reference program's by a relative error of at most 0.0085.
Values may be sent and summed in bfloat16 or wider, within the bound.
No kernel may reach another device: no remote copies, remote signals or barrier semaphores. Data moves between devices by JAX's collectives and lax.ppermute only.
A program may use at most 64 MiB of HBM per device.

```python
import math
import jax
import jax.numpy as jnp
import numpy as np
from jax import lax

AY = 3072
OY = 3584
NFLUX = 8
TILE = 128
BLK_DEV = 256
CAP = 32
ATILES_DEV = 192
OTILES_DEV = 448
AX = 128
OX = 256
BLOCKS = 4096
N_TILES = 16


def with_ends(result, rng, low, top_value):
    dims = result.shape
    index_at = [jax.random.randint(jax.random.fold_in(rng, axis), (), 0, dims[axis]) for axis in range(len(dims))]
    result = result.at[tuple(index_at)].set(low)
    longest = dims.index(max(dims))
    index_at[longest] = (index_at[longest] + 1) % dims[longest]
    return result.at[tuple(index_at)].set(top_value)


def levels(key, extent, split, smallest, top_value):
    level = 1.0
    for dim, blocks in split:
        heights = jax.random.uniform(jax.random.fold_in(jax.random.fold_in(key, 6), dim), (blocks,), jnp.float32, smallest / len(split), top_value / len(split))
        level = level * jnp.repeat(jnp.exp(heights), extent[dim] // blocks).reshape((-1,) + (1,) * (len(extent) - 1 - dim))
    return level


def deal_out(key, own, number, rows, number_of, top, most, skew):
    order = jax.random.permutation(key, number_of)
    crowded, common = shares(number_of, rows * top, most, skew, True), shares(number_of, rows * top, most, skew, False)
    places = jnp.arange(number_of)

    def named(tallies, rotation):
        used = int((tallies > 0).sum())
        fixed = max(1, used // 4)
        passed = fixed + (places - fixed + rotation * (used - fixed)) % max(1, number_of - fixed)
        return jnp.zeros((number_of,), jnp.int32).at[order[jnp.where(places < fixed, places, passed)]].set(jnp.asarray(tallies, jnp.int32))

    tallies = jnp.where(number % 4 == 0, named(crowded, number // 4), named(common, number - number // 4 - 1))
    mixed = jax.random.permutation(jax.random.fold_in(own, 3), number_of)
    source_of, receiver = mixed[0:number_of // 2 * 2:2], mixed[1:number_of // 2 * 2:2]
    margin = jnp.minimum(tallies[source_of] - 1, most - tallies[receiver]) // 2
    margin = jnp.where((source_of == order[0]) | (receiver == order[0]) | (tallies[receiver] == 0), 0, jnp.maximum(margin, 0))
    passed = jax.random.randint(jax.random.fold_in(own, 4), (number_of // 2,), 0, 1 << 20) % (margin + 1)
    tallies = tallies.at[source_of].add(-passed).at[receiver].add(passed)
    items = jnp.searchsorted(jnp.cumsum(tallies), jnp.arange(rows * top), side="right").astype(jnp.int32)
    table = items.reshape(top, rows).T
    table = table[jax.random.permutation(jax.random.fold_in(own, 1), rows)]
    rotation = jax.random.randint(jax.random.fold_in(own, 2), (rows, 1), 0, top)
    return jnp.take_along_axis(table, (jnp.arange(top)[None, :] + rotation) % top, axis=1)


def shares(amount, total, bound, slope, full):
    portions = [(1 << 20) // math.isqrt(standing ** slope) + 1 for standing in range(1, amount + 1)]
    largest = bound if full else min(bound, max(-(-total // amount), total * portions[0] // sum(portions)))
    least = 1 if total - largest >= amount - 1 else 0
    counts, spare = [largest] + [least] * (amount - 1), total - largest - least * (amount - 1)
    while spare > 0:
        movable = [i for i in range(1, amount) if counts[i] < largest] or [i for i in range(1, amount) if counts[i] < bound]
        pool, left = sum([portions[i] for i in movable]), spare
        for i in movable:
            extra = min(bound - counts[i], max(1, left * portions[i] // pool), spare)
            counts[i] = counts[i] + extra
            spare = spare - extra
    return np.array(counts)


def scatter_about(key, shape, width, bound, cuts=(), kind=jnp.bfloat16):
    drawn = width * jax.random.normal(key, shape, jnp.float32)
    if cuts:
        drawn = drawn * levels(key, shape, cuts, -0.22, 0.18)
    return jnp.clip(drawn, -bound, bound).astype(kind)


def setup_inputs(seed: int = 0, part: int = 0) -> dict:
    splits = jax.random.split(jax.random.key(seed), 12)
    own_keys = jax.random.split(jax.random.fold_in(splits[11], part), 12)
    atm_state = scatter_about(own_keys[0], (AX, AY), 1.0, 6.0, ((0, 16),), jnp.float32)
    atm_kappa = jnp.clip(jnp.exp(jax.random.uniform(splits[1], (AY,), jnp.float32, math.log(0.05), math.log(0.2))), 0.05, 0.2)
    forcing = scatter_about(own_keys[2], (NFLUX, AX, AY), 1.0, 6.0, ((1, 16),))
    flux_gain = jnp.clip(jax.random.uniform(splits[3], (NFLUX,), jnp.float32, 0.5, 1.5), 0.5, 1.5)
    remap_weight = scatter_about(splits[4], (BLOCKS, TILE, TILE), TILE ** -0.5, 0.5, ((0, 16),))
    remap_source = with_ends(jax.random.randint(splits[5], (BLOCKS,), 0, ATILES_DEV), jax.random.fold_in(splits[5], 1), 0, ATILES_DEV - 1).astype(jnp.int32)
    remap_owner_keys = jax.random.split(jax.random.fold_in(splits[6], 1), BLOCKS // BLK_DEV)
    remap_owner_turns = jax.random.permutation(jax.random.fold_in(splits[6], 3), BLOCKS // BLK_DEV)
    remap_owner = jax.vmap(lambda own, number: deal_out(jax.random.fold_in(splits[6], 2), own, number, BLK_DEV, N_TILES, 1, CAP, 2))(remap_owner_keys, remap_owner_turns).reshape((BLOCKS, 1))
    remap_dest = with_ends(jax.random.randint(splits[7], (BLOCKS,), 0, OTILES_DEV), jax.random.fold_in(splits[7], 1), 0, OTILES_DEV - 1).astype(jnp.int32)
    ocean_state = scatter_about(own_keys[8], (OX, OY), 1.0, 6.0, ((0, 16),), jnp.float32)
    ocean_nu = jnp.clip(jnp.exp(jax.random.uniform(splits[9], (OY,), jnp.float32, math.log(0.05), math.log(0.2))), 0.05, 0.2)
    flux_coef = jnp.clip(jax.random.uniform(splits[10], (NFLUX,), jnp.float32, 0.05, 0.3), 0.05, 0.3)
    return {"atm_state": atm_state, "atm_kappa": atm_kappa, "forcing": forcing, "flux_gain": flux_gain, "remap_weight": remap_weight, "remap_source": remap_source, "remap_owner": remap_owner, "remap_dest": remap_dest, "ocean_state": ocean_state, "ocean_nu": ocean_nu, "flux_coef": flux_coef}


def atm_step(atmos, kappa_row):
    laplace = jnp.roll(atmos, 1, 0) + jnp.roll(atmos, -1, 0) + jnp.roll(atmos, 1, 1) + jnp.roll(atmos, -1, 1) - 4.0 * atmos
    return atmos + kappa_row[None, :] * laplace


def ocean_step(ocean, nu_row, drive_sum):
    upper = jnp.concatenate([ocean[1:], ocean[-1:, ::-1]], 0)
    lower = jnp.concatenate([jnp.zeros((1, ocean.shape[1]), jnp.float32), ocean[:-1]], 0)
    laplace = lower + upper + jnp.roll(ocean, 1, 1) + jnp.roll(ocean, -1, 1) - 4.0 * ocean
    return ocean + nu_row[None, :] * laplace + drive_sum


def reference(atm_state, atm_kappa, forcing, flux_gain, remap_weight, remap_source, remap_owner, remap_dest, ocean_state, ocean_nu, flux_coef):
    atmos = atm_state
    for section in range(2):
        atmos = atm_step(atmos, atm_kappa)
    fluxes = (forcing.astype(jnp.float32) + flux_gain[:, None, None] * atmos[None]).astype(jnp.bfloat16)
    flux_tiles = fluxes.reshape(NFLUX, N_TILES * ATILES_DEV, TILE)
    devices = jnp.arange(BLOCKS, dtype=jnp.int32) // BLK_DEV
    src_global = devices * ATILES_DEV + remap_source
    dst_global = remap_owner[:, 0] * OTILES_DEV + remap_dest

    def forward(carry, device):
        start = device * BLK_DEV
        weights = lax.dynamic_slice_in_dim(remap_weight, start, BLK_DEV, 0)
        sources = lax.dynamic_slice_in_dim(src_global, start, BLK_DEV, 0)
        targets = lax.dynamic_slice_in_dim(dst_global, start, BLK_DEV, 0)
        pieces = jnp.take(flux_tiles, sources, axis=1)
        contribution = jnp.einsum('kbi,bij->bkj', pieces.astype(jnp.float32), weights.astype(jnp.float32), precision=lax.Precision.HIGHEST)
        return carry.at[targets].add(contribution), None

    ocean_flux, _ = lax.scan(forward, jnp.zeros((N_TILES * OTILES_DEV, NFLUX, TILE), jnp.float32), jnp.arange(N_TILES, dtype=jnp.int32))
    flux_field = ocean_flux.transpose(1, 0, 2).reshape(NFLUX, OX, OY)
    drive_sum = jnp.tensordot(flux_coef, flux_field, axes=1)
    ocean = ocean_state
    for section in range(2):
        ocean = ocean_step(ocean, ocean_nu, drive_sum)
    sea_tiles = ocean.reshape(N_TILES * OTILES_DEV, TILE)
    returned = jnp.take(sea_tiles, dst_global, axis=0).astype(jnp.bfloat16)

    def backward(carry, device):
        start = device * BLK_DEV
        weights = lax.dynamic_slice_in_dim(remap_weight, start, BLK_DEV, 0)
        sources = lax.dynamic_slice_in_dim(src_global, start, BLK_DEV, 0)
        values = lax.dynamic_slice_in_dim(returned, start, BLK_DEV, 0)
        came_back = jnp.einsum('bij,bj->bi', weights.astype(jnp.float32), values.astype(jnp.float32), precision=lax.Precision.HIGHEST)
        return carry.at[sources].add(came_back), None

    feedback, _ = lax.scan(backward, jnp.zeros((N_TILES * ATILES_DEV, TILE), jnp.float32), jnp.arange(N_TILES, dtype=jnp.int32))
    return atmos, ocean, feedback.reshape(AX, AY)
```

```python
import functools

import jax
import jax.numpy as jnp
from jax import lax
from jax.experimental import pallas as pl
from jax.experimental.pallas import tpu as pltpu
from jax.sharding import PartitionSpec as P

LANE = 128
EDGE = 32
CHUNK = 8
F32 = jnp.float32
BF16 = jnp.bfloat16
VMEM = pl.BlockSpec(memory_space=pltpu.VMEM)
SMEM = pl.BlockSpec(memory_space=pltpu.SMEM)


def iota(shape, dim):
    return lax.broadcasted_iota(jnp.int32, shape, dim)


def dot(a, b):
    return lax.dot_general(a, b, (((1,), (0,)), ((), ())), preferred_element_type=F32)


def dot_nt(a, b):
    return lax.dot_general(a, b, (((1,), (1,)), ((), ())), preferred_element_type=F32)


def onehot(mask):
    return jnp.where(mask, 1.0, 0.0).astype(BF16)


def routing_kernel(
    ntiles, main, ocean_rows, row_tiles, me_ref, src_col, src_row, own_col, own_row, dst_row,
    pick_ref, back_ref, slots_ref, sort_ref, ids_ref,
):
    blocks = own_row.shape[1]
    rows = main + 2 * EDGE
    per_lane = LANE // main
    owner = own_row[...]
    row_of, col_of = dst_row[...] // row_tiles, dst_row[...] % row_tiles
    owner_c = own_col[...]
    match_c = owner_c == iota((blocks, LANE), 1)
    below = onehot(iota((blocks, blocks), 1) < iota((blocks, blocks), 0))
    rank_c = jnp.sum(
        jnp.where(match_c, dot(below, onehot(match_c)), 0.0), axis=1, keepdims=True
    ).astype(jnp.int32)
    match_r = owner == iota((ntiles, blocks), 0)
    above = onehot(iota((blocks, blocks), 0) < iota((blocks, blocks), 1))
    rank_r = jnp.sum(
        jnp.where(match_r, dot(onehot(match_r), above), 0.0), axis=0, keepdims=True
    ).astype(jnp.int32)
    pick_ref[...] = onehot(src_col[...] == iota(pick_ref.shape, 1))
    back_ref[...] = onehot(src_row[...] == iota(back_ref.shape, 0))
    sort_ref[...] = onehot(owner_c * main + rank_c == iota(sort_ref.shape, 1))
    own_slot = owner * rows + rank_r
    low = (row_of == ocean_rows - 1) & (owner < ntiles - 1)
    low_slot = jnp.where(low, (owner + 1) * rows + main + col_of, -1)
    high = (row_of == 0) & (owner > 0)
    high_slot = jnp.where(high, (owner - 1) * rows + main + EDGE + col_of, -1)
    for t in range(ntiles):
        slot = iota((rows, blocks), 0) + t * rows
        slots_ref[pl.ds(t * rows, rows), :] = onehot(
            (slot == own_slot) | (slot == low_slot) | (slot == high_slot)
        )
    lane_of = rank_c + (me_ref[0] % per_lane) * main
    place = onehot(lane_of == iota((blocks, LANE), 1))
    ids_ref[0] = dot(jnp.where(match_r, (col_of + 1).astype(F32), 0.0).astype(BF16), place)
    ids_ref[1] = dot(jnp.where(match_r, row_of.astype(F32), 0.0).astype(BF16), place)


def forward_kernel(
    ntiles, main, me_ref, gain_ref, coef_ref, atm_ref, kappa_ref, even_ref, odd_ref, forcing_ref,
    pick_ref, slots_ref, ids_ref, weight_ref, next_ref, out_ref, work,
):
    atm_rows, cols = atm_ref.shape
    rows = main + 2 * EDGE
    even = me_ref[0] % 2 == 0
    ev, od = even_ref[:, :cols], odd_ref[:, :cols]
    size = 2 * atm_rows
    work[0:atm_rows] = atm_ref[...]
    work[atm_rows : 2 * atm_rows] = jnp.zeros((atm_rows, cols), F32)
    work[size - 2 : size] = jnp.where(even, od, ev)
    work[atm_rows : atm_rows + 2] = jnp.where(even, ev, od)
    x = work[...]
    kappa = kappa_ref[...]
    for _ in range(2):
        near = (
            pltpu.roll(x, 1, 0) + pltpu.roll(x, size - 1, 0)
            + pltpu.roll(x, 1, 1) + pltpu.roll(x, cols - 1, 1)
        )
        x = x + kappa * (near - 4.0 * x)
    atm = x[:atm_rows]
    next_ref[...] = atm
    nflux = forcing_ref.shape[0]
    scale = coef_ref[0] * gain_ref[0]
    for k in range(1, nflux):
        scale = scale + coef_ref[k] * gain_ref[k]
    field = scale * atm
    for k in range(nflux):
        field = field + coef_ref[k] * forcing_ref[k].astype(F32)
    tiles = jnp.concatenate(
        [field[:, c * LANE : (c + 1) * LANE] for c in range(cols // LANE)], axis=0
    ).astype(BF16)
    pieces = dot(pick_ref[...], tiles)
    blocks = pieces.shape[0]
    row = iota((CHUNK, LANE), 0)
    parts = []
    for n in range(blocks // CHUNK):
        piece = pieces[n * CHUNK : (n + 1) * CHUNK]
        spread = jnp.concatenate(
            [jnp.where(row == q, piece, 0.0) for q in range(CHUNK)], axis=1
        ).astype(BF16)
        weight = weight_ref[pl.ds(n * CHUNK, CHUNK)].reshape(CHUNK * LANE, LANE)
        parts.append(dot(spread, weight))
    contribution = jnp.concatenate(parts, axis=0).astype(BF16)
    at = iota((EDGE, LANE), 0)
    for t in range(ntiles):
        sent = dot(slots_ref[pl.ds(t * rows, rows), :], contribution)
        low = sent[main : main + EDGE]
        low = jnp.where(at == EDGE - 4, ids_ref[0, t : t + 1, :], low)
        low = jnp.where(at == EDGE - 3, ids_ref[1, t : t + 1, :], low)
        out_ref[pl.ds(t * rows, main), :] = sent[:main].astype(BF16)
        out_ref[pl.ds(t * rows + main, EDGE), :] = low.astype(BF16)
        out_ref[pl.ds(t * rows + main + EDGE, EDGE), :] = sent[main + EDGE :].astype(BF16)


def reverse_lanes(x):
    tiles = x.shape[1] // LANE
    back = LANE - 1 - iota((x.shape[0], LANE), 1)
    parts = [
        jnp.take_along_axis(x[:, c * LANE : (c + 1) * LANE], back, axis=1) for c in range(tiles)
    ]
    return jnp.concatenate(parts[::-1], axis=1)


def free_ocean_kernel(ntiles, offset, me_ref, ocean_ref, nu_ref, even_ref, odd_ref, out_ref, work):
    rows, cols = ocean_ref.shape
    me = me_ref[0]
    even, bottom, top = me % 2 == 0, me == 0, me == ntiles - 1
    ev, od = even_ref[:, offset:], odd_ref[:, offset:]
    size = rows + 8
    work[0:rows] = ocean_ref[...]
    work[rows:size] = jnp.zeros((8, cols), F32)
    work[size - 2 : size] = jnp.where(bottom, 0.0, jnp.where(even, od, ev))
    work[rows : rows + 2] = jnp.where(even, ev, od)
    nu = nu_ref[...]
    x = work[...]
    at = iota((size, cols), 0)
    for _ in range(2):
        folded = pltpu.roll(reverse_lanes(x[rows - 8 : rows]), 1, 0)
        tail = jnp.where(top & (iota((8, cols), 0) == 0), folded, x[rows:])
        x = jnp.concatenate([x[:rows], tail], axis=0)
        near = (
            pltpu.roll(x, 1, 0) + pltpu.roll(x, size - 1, 0)
            + pltpu.roll(x, 1, 1) + pltpu.roll(x, cols - 1, 1)
        )
        x = x + nu * (near - 4.0 * x)
        x = jnp.where(bottom & (at >= rows + 4), 0.0, x)
    out_ref[...] = x[:rows]


def ocean_kernel(ntiles, main, me_ref, arrived_ref, free_ref, nu_ref, next_ref, return_ref):
    rows, cols = free_ref.shape
    row_tiles = cols // LANE
    per_lane = LANE // main
    step = main + 2 * EDGE
    total = rows * row_tiles
    top = me_ref[0] == ntiles - 1
    groups = ntiles // per_lane
    drive = jnp.zeros((total, LANE), F32)
    low = jnp.zeros((EDGE, LANE), F32)
    high = jnp.zeros((EDGE, LANE), F32)
    keys = []
    for g in range(groups):
        edge = jnp.zeros((EDGE, LANE), F32)
        values = []
        for s in range(g * per_lane, (g + 1) * per_lane):
            values.append(arrived_ref[pl.ds(s * step, main), :])
            edge = edge + arrived_ref[pl.ds(s * step + main, EDGE), :].astype(F32)
            high = high + arrived_ref[pl.ds(s * step + main + EDGE, EDGE), :].astype(F32)
        low = low + edge
        key = (edge[EDGE - 4 : EDGE - 3] - 1.0) * rows + edge[EDGE - 3 : EDGE - 2]
        key = key.astype(jnp.int32)
        keys.append(key)
        drive = drive + dot(
            onehot(key == iota((total, LANE), 0)), jnp.concatenate(values, axis=0)
        )
    tile = lambda c: drive[c * rows : (c + 1) * rows]
    spun = [pltpu.roll(tile(c), 1, 1) for c in range(row_tiles)]
    back = [pltpu.roll(tile(c), LANE - 1, 1) for c in range(row_tiles)]
    lane, at = iota((rows, LANE), 1), iota((rows, LANE), 0)
    turned = LANE - 1 - iota((8, LANE), 1)
    results = []
    for c in range(row_tiles):
        d = tile(c)
        left = jnp.where(lane == 0, spun[c - 1], spun[c])
        right = jnp.where(lane == LANE - 1, back[(c + 1) % row_tiles], back[c])
        under = jnp.where(at == 0, low[c : c + 1], pltpu.roll(d, 1, 0))
        fold = jnp.take_along_axis(tile(row_tiles - 1 - c)[rows - 8 :], turned, axis=1)[7:8]
        over_row = jnp.where(top, fold, high[c : c + 1])
        over = jnp.where(at == rows - 1, over_row, pltpu.roll(d, rows - 1, 0))
        span = slice(c * LANE, (c + 1) * LANE)
        near = under + over + left + right
        value = free_ref[:, span] + (2.0 * d + nu_ref[:, span] * (near - 4.0 * d))
        next_ref[:, span] = value
        results.append(value.astype(BF16))
    cells = jnp.concatenate(results, axis=0)
    for g in range(groups):
        column = jnp.transpose(jnp.broadcast_to(keys[g], (LANE, LANE)))
        wide = jnp.concatenate([column] * -(-total // LANE), axis=1)[:, :total]
        picked = dot(onehot(wide == iota((LANE, total), 1)), cells)
        return_ref[pl.ds(g * LANE, LANE), :] = picked.astype(BF16)


def backward_kernel(came_ref, sort_ref, back_ref, weight_ref, out_ref):
    values = dot(sort_ref[...], came_ref[...])
    blocks = values.shape[0]
    row = iota((CHUNK, LANE), 0)
    parts = []
    for n in range(blocks // CHUNK):
        value = values[n * CHUNK : (n + 1) * CHUNK].astype(BF16)
        weight = weight_ref[pl.ds(n * CHUNK, CHUNK)].reshape(CHUNK * LANE, LANE)
        full = dot_nt(value, weight)
        part = full[:, :LANE]
        for q in range(1, CHUNK):
            part = jnp.where(row == q, full[:, q * LANE : (q + 1) * LANE], part)
        parts.append(part)
    result = jnp.concatenate(parts, axis=0)
    coarse = result.astype(BF16)
    fine = (result - coarse.astype(F32)).astype(BF16)
    tiles = dot(back_ref[...], coarse) + dot(back_ref[...], fine)
    rows = out_ref.shape[0]
    for c in range(out_ref.shape[1] // LANE):
        out_ref[:, c * LANE : (c + 1) * LANE] = tiles[c * rows : (c + 1) * rows]


def call(kernel, outs, specs, cost, scratch=(), limit=24 << 20):
    return pl.pallas_call(
        kernel,
        out_shape=outs,
        in_specs=specs,
        out_specs=jax.tree.map(lambda _: VMEM, outs),
        scratch_shapes=scratch,
        compiler_params=pltpu.CompilerParams(vmem_limit_bytes=limit),
        cost_estimate=pl.CostEstimate(flops=cost, bytes_accessed=cost // 64, transcendentals=0),
    )


def per_device(
    atm_state,
    atm_kappa,
    forcing,
    flux_gain,
    remap_weight,
    remap_source,
    remap_owner,
    remap_dest,
    ocean_state,
    ocean_nu,
    flux_coef,
):
    ntiles = lax.axis_size("tiles")
    me = lax.axis_index("tiles")
    blocks = remap_source.shape[0]
    capacity = max(2, 2 * blocks // ntiles)
    main = -(-capacity // 16) * 16
    rows = main + 2 * EDGE
    atm_rows, atm_cols = atm_state.shape
    ocean_rows, ocean_cols = ocean_state.shape
    atm_tiles = atm_rows * atm_cols // LANE
    row_tiles = ocean_cols // LANE
    shape = jax.ShapeDtypeStruct
    even = me % 2 == 0
    first = jnp.concatenate([atm_state[:2], ocean_state[:2]], axis=1)
    last = jnp.concatenate([atm_state[-2:], ocean_state[-2:]], axis=1)
    pairs = [(2 * k + 1, (2 * k + 2) % ntiles) for k in range(ntiles // 2)]
    from_odd = lax.ppermute(
        jnp.where(even, first, last), "tiles", pairs + [(j, i) for i, j in pairs]
    )
    from_even = lax.ppermute(
        jnp.where(even, last, first), "tiles", [(i, i ^ 1) for i in range(ntiles)]
    )
    me_arr = me.astype(jnp.int32).reshape(1)
    atm_cols_tiles = atm_cols // LANE
    source = (remap_source % atm_cols_tiles) * atm_rows + remap_source // atm_cols_tiles
    pick, back, slots, sort, ids = call(
        functools.partial(routing_kernel, ntiles, main, ocean_rows, row_tiles),
        (
            shape((blocks, atm_tiles), BF16),
            shape((atm_tiles, blocks), BF16),
            shape((ntiles * rows, blocks), BF16),
            shape((blocks, ntiles * main), BF16),
            shape((2, ntiles, LANE), F32),
        ),
        [SMEM, VMEM, VMEM, VMEM, VMEM, VMEM],
        1 << 27,
    )(
        me_arr,
        source[:, None],
        source[None, :],
        remap_owner,
        remap_owner.reshape(1, blocks),
        remap_dest[None, :],
    )
    atm_next, outgoing = call(
        functools.partial(forward_kernel, ntiles, main),
        (shape(atm_state.shape, F32), shape((ntiles * rows, LANE), BF16)),
        [SMEM, SMEM, SMEM] + [VMEM] * 9,
        1 << 28,
        [pltpu.VMEM((2 * atm_rows, atm_cols), F32)],
    )(
        me_arr,
        flux_gain,
        flux_coef,
        atm_state,
        atm_kappa[None, :],
        from_even,
        from_odd,
        forcing,
        pick,
        slots,
        ids,
        remap_weight,
    )
    arrived = lax.all_to_all(outgoing, "tiles", split_axis=0, concat_axis=0, tiled=True)
    free = call(
        functools.partial(free_ocean_kernel, ntiles, atm_cols),
        shape(ocean_state.shape, F32),
        [SMEM] + [VMEM] * 4,
        1 << 27,
        [pltpu.VMEM((ocean_rows + 8, ocean_cols), F32)],
    )(me_arr, ocean_state, ocean_nu[None, :], from_even, from_odd)
    ocean_next, returned = call(
        functools.partial(ocean_kernel, ntiles, main),
        (shape(ocean_state.shape, F32), shape((ntiles * main, LANE), BF16)),
        [SMEM] + [VMEM] * 3,
        1 << 27,
    )(me_arr, arrived, free, ocean_nu[None, :])
    came_back = lax.all_to_all(returned, "tiles", split_axis=0, concat_axis=0, tiled=True)
    feedback = call(
        backward_kernel,
        shape(atm_state.shape, F32),
        [VMEM] * 4,
        1 << 28,
    )(came_back, sort, back, remap_weight)
    return (atm_next, ocean_next, feedback)


def solution(mesh):
    return jax.shard_map(
        per_device,
        mesh=mesh,
        in_specs=(
            P(("members", "tiles"), None),
            P(),
            P(None, ("members", "tiles"), None),
            P(),
            P("tiles", None, None),
            P("tiles"),
            P("tiles", None),
            P("tiles"),
            P(("members", "tiles"), None),
            P(),
            P(),
        ),
        out_specs=(
            P(("members", "tiles"), None),
            P(("members", "tiles"), None),
            P(("members", "tiles"), None),
        ),
        check_vma=False,
    )
```

```python
import functools

import jax
import jax.numpy as jnp
from jax import lax
from jax.experimental import pallas as pl
from jax.experimental.pallas import tpu as pltpu
from jax.sharding import PartitionSpec as P

LANE = 128
EDGE = 32
CHUNK = 8
PIECES = 8
F32 = jnp.float32
BF16 = jnp.bfloat16
VMEM = pl.BlockSpec(memory_space=pltpu.VMEM)
SMEM = pl.BlockSpec(memory_space=pltpu.SMEM)
HBM = pl.BlockSpec(memory_space=pltpu.HBM)


def iota(shape, dim):
    return lax.broadcasted_iota(jnp.int32, shape, dim)


def dot(a, b):
    return lax.dot_general(a, b, (((1,), (0,)), ((), ())), preferred_element_type=F32)


def dot_nt(a, b):
    return lax.dot_general(a, b, (((1,), (1,)), ((), ())), preferred_element_type=F32)


def onehot(mask):
    return jnp.where(mask, 1.0, 0.0).astype(BF16)


def as_column(row):
    parts = [
        jnp.transpose(jnp.broadcast_to(row[:, k : k + LANE], (LANE, LANE)))
        for k in range(0, row.shape[1], LANE)
    ]
    return jnp.concatenate(parts, axis=0)


def matches_lane(column, width):
    parts = [
        onehot(column == iota(column.shape, 1) + k)[:, : min(LANE, width - k)]
        for k in range(0, width, LANE)
    ]
    return jnp.concatenate(parts, axis=1)


def send_kernel(me_ref, atm_hbm, ocean_hbm, atm_ref, ocean_ref, even_ref, odd_ref, sems):
    copies = [
        pltpu.make_async_copy(atm_hbm, atm_ref, sems.at[0]),
        pltpu.make_async_copy(ocean_hbm, ocean_ref, sems.at[1]),
    ]
    for copy in copies:
        copy.start()
    even = me_ref[0] % 2 == 0
    start = 0
    for copy, ref in zip(copies, (atm_ref, ocean_ref)):
        copy.wait()
        rows, cols = ref.shape
        first, last = ref[0:2], ref[rows - 2 : rows]
        even_ref[:, start : start + cols] = jnp.where(even, last, first)
        odd_ref[:, start : start + cols] = jnp.where(even, first, last)
        start += cols


def stage_kernel(
    ntiles, main, atm_rows, atm_row_tiles, ocean_rows, row_tiles,
    me_ref, src_hbm, own_hbm, dst_hbm, gain_hbm, coef_hbm, kappa_hbm, nu_hbm, forcing_hbm,
    weight_hbm,
    pick_ref, back_ref, slots_ref, sort_ref, ids_ref, field_ref, scale_ref, kappa_ref, nu_ref,
    weight_ref,
    ints, gains, forcing_ref, sems,
):
    small = [
        (src_hbm, ints.at[0]), (own_hbm, ints.at[1]), (dst_hbm, ints.at[2]),
        (gain_hbm, gains.at[0]), (coef_hbm, gains.at[1]), (forcing_hbm, forcing_ref),
        (kappa_hbm, kappa_ref), (nu_hbm, nu_ref),
    ]
    copies = [pltpu.make_async_copy(a, b, sems.at[k]) for k, (a, b) in enumerate(small)]
    share = weight_hbm.shape[0] // PIECES
    for n in range(PIECES):
        span = pl.ds(n * share, share)
        copies.append(
            pltpu.make_async_copy(
                weight_hbm.at[span], weight_ref.at[span], sems.at[len(small) + n]
            )
        )
    for copy in copies:
        copy.start()
    for copy in copies[:3]:
        copy.wait()
    rows = main + 2 * EDGE
    per_lane = LANE // main
    source, owner, dest = ints[0], ints[1], ints[2]
    blocks = owner.shape[1]
    source = (source % atm_row_tiles) * atm_rows + source // atm_row_tiles
    row_of, col_of = dest // row_tiles, dest % row_tiles
    match = owner == iota((ntiles, blocks), 0)
    above = onehot(iota((blocks, blocks), 0) < iota((blocks, blocks), 1))
    rank = jnp.sum(
        jnp.where(match, dot(onehot(match), above), 0.0), axis=0, keepdims=True
    ).astype(jnp.int32)
    pick_ref[...] = matches_lane(as_column(source), pick_ref.shape[1])
    back_ref[...] = onehot(source == iota(back_ref.shape, 0))
    sort_ref[...] = matches_lane(as_column(owner * main + rank), sort_ref.shape[1])
    own_slot = owner * rows + rank
    low = (row_of == ocean_rows - 1) & (owner < ntiles - 1)
    low_slot = jnp.where(low, (owner + 1) * rows + main + col_of, -1)
    high = (row_of == 0) & (owner > 0)
    high_slot = jnp.where(high, (owner - 1) * rows + main + EDGE + col_of, -1)
    for t in range(ntiles):
        slot = iota((rows, blocks), 0) + t * rows
        slots_ref[pl.ds(t * rows, rows), :] = onehot(
            (slot == own_slot) | (slot == low_slot) | (slot == high_slot)
        )
    lane_of = rank + (me_ref[0] % per_lane) * main
    place = onehot(lane_of == iota((LANE, blocks), 0))
    ids_ref[0] = dot_nt(jnp.where(match, (col_of + 1).astype(F32), 0.0).astype(BF16), place)
    ids_ref[1] = dot_nt(jnp.where(match, row_of.astype(F32), 0.0).astype(BF16), place)
    for copy in copies[3 : len(small)]:
        copy.wait()
    coef = gains[1]
    scale_ref[...] = jnp.broadcast_to(
        jnp.sum(gains[0] * coef, axis=1, keepdims=True), scale_ref.shape
    )
    field = jnp.zeros(field_ref.shape, F32)
    for k in range(forcing_ref.shape[0]):
        field = field + coef[:, k : k + 1] * forcing_ref[k].astype(F32)
    field_ref[...] = field
    for copy in copies[len(small) :]:
        copy.wait()


def forward_kernel(
    ntiles, main, me_ref, atm_ref, kappa_ref, even_ref, odd_ref, field_ref, scale_ref,
    pick_ref, slots_ref, ids_ref, weight_ref, next_ref, out_ref, work,
):
    atm_rows, cols = atm_ref.shape
    rows = main + 2 * EDGE
    even = me_ref[0] % 2 == 0
    ev, od = even_ref[:, :cols], odd_ref[:, :cols]
    size = 2 * atm_rows
    work[0:atm_rows] = atm_ref[...]
    work[atm_rows : 2 * atm_rows] = jnp.zeros((atm_rows, cols), F32)
    work[size - 2 : size] = jnp.where(even, od, ev)
    work[atm_rows : atm_rows + 2] = jnp.where(even, ev, od)
    x = work[...]
    kappa = kappa_ref[...]
    for _ in range(2):
        near = (
            pltpu.roll(x, 1, 0) + pltpu.roll(x, size - 1, 0)
            + pltpu.roll(x, 1, 1) + pltpu.roll(x, cols - 1, 1)
        )
        x = x + kappa * (near - 4.0 * x)
    atm = x[:atm_rows]
    next_ref[...] = atm
    field = field_ref[...] + scale_ref[:, 0:1] * atm
    tiles = jnp.concatenate(
        [field[:, c * LANE : (c + 1) * LANE] for c in range(cols // LANE)], axis=0
    ).astype(BF16)
    pieces = dot(pick_ref[...], tiles)
    blocks = pieces.shape[0]
    row = iota((CHUNK, LANE), 0)
    parts = []
    for n in range(blocks // CHUNK):
        piece = pieces[n * CHUNK : (n + 1) * CHUNK]
        spread = jnp.concatenate(
            [jnp.where(row == q, piece, 0.0) for q in range(CHUNK)], axis=1
        ).astype(BF16)
        weight = weight_ref[pl.ds(n * CHUNK, CHUNK)].reshape(CHUNK * LANE, LANE)
        parts.append(dot(spread, weight))
    contribution = jnp.concatenate(parts, axis=0).astype(BF16)
    at = iota((EDGE, LANE), 0)
    for t in range(ntiles):
        sent = dot(slots_ref[pl.ds(t * rows, rows), :], contribution)
        low = sent[main : main + EDGE]
        low = jnp.where(at == EDGE - 4, ids_ref[0, t : t + 1, :], low)
        low = jnp.where(at == EDGE - 3, ids_ref[1, t : t + 1, :], low)
        out_ref[pl.ds(t * rows, main), :] = sent[:main].astype(BF16)
        out_ref[pl.ds(t * rows + main, EDGE), :] = low.astype(BF16)
        out_ref[pl.ds(t * rows + main + EDGE, EDGE), :] = sent[main + EDGE :].astype(BF16)


def reverse_lanes(x):
    tiles = x.shape[1] // LANE
    back = LANE - 1 - iota((x.shape[0], LANE), 1)
    parts = [
        jnp.take_along_axis(x[:, c * LANE : (c + 1) * LANE], back, axis=1) for c in range(tiles)
    ]
    return jnp.concatenate(parts[::-1], axis=1)


def free_ocean_kernel(ntiles, offset, me_ref, ocean_ref, nu_ref, even_ref, odd_ref, out_ref, work):
    rows, cols = ocean_ref.shape
    me = me_ref[0]
    even, bottom, top = me % 2 == 0, me == 0, me == ntiles - 1
    ev, od = even_ref[:, offset:], odd_ref[:, offset:]
    size = rows + 8
    work[0:rows] = ocean_ref[...]
    work[rows:size] = jnp.zeros((8, cols), F32)
    work[size - 2 : size] = jnp.where(bottom, 0.0, jnp.where(even, od, ev))
    work[rows : rows + 2] = jnp.where(even, ev, od)
    nu = jnp.concatenate([nu_ref[c : c + 1] for c in range(cols // LANE)], axis=1)
    x = work[...]
    at = iota((size, cols), 0)
    for _ in range(2):
        folded = pltpu.roll(reverse_lanes(x[rows - 8 : rows]), 1, 0)
        tail = jnp.where(top & (iota((8, cols), 0) == 0), folded, x[rows:])
        x = jnp.concatenate([x[:rows], tail], axis=0)
        near = (
            pltpu.roll(x, 1, 0) + pltpu.roll(x, size - 1, 0)
            + pltpu.roll(x, 1, 1) + pltpu.roll(x, cols - 1, 1)
        )
        x = x + nu * (near - 4.0 * x)
        x = jnp.where(bottom & (at >= rows + 4), 0.0, x)
    out_ref[...] = x[:rows]


def ocean_kernel(ntiles, main, me_ref, arrived_ref, free_ref, nu_ref, next_ref, return_ref):
    rows, cols = free_ref.shape
    row_tiles = cols // LANE
    per_lane = LANE // main
    step = main + 2 * EDGE
    total = rows * row_tiles
    top = me_ref[0] == ntiles - 1
    groups = ntiles // per_lane
    drive = jnp.zeros((total, LANE), F32)
    low = jnp.zeros((EDGE, LANE), F32)
    high = jnp.zeros((EDGE, LANE), F32)
    keys = []
    for g in range(groups):
        edge = jnp.zeros((EDGE, LANE), F32)
        values = []
        for s in range(g * per_lane, (g + 1) * per_lane):
            values.append(arrived_ref[pl.ds(s * step, main), :])
            edge = edge + arrived_ref[pl.ds(s * step + main, EDGE), :].astype(F32)
            high = high + arrived_ref[pl.ds(s * step + main + EDGE, EDGE), :].astype(F32)
        low = low + edge
        key = (edge[EDGE - 4 : EDGE - 3] - 1.0) * rows + edge[EDGE - 3 : EDGE - 2]
        key = key.astype(jnp.int32)
        keys.append(key)
        drive = drive + dot(
            onehot(key == iota((total, LANE), 0)), jnp.concatenate(values, axis=0)
        )
    tile = lambda c: drive[c * rows : (c + 1) * rows]
    spun = [pltpu.roll(tile(c), 1, 1) for c in range(row_tiles)]
    back = [pltpu.roll(tile(c), LANE - 1, 1) for c in range(row_tiles)]
    lane, at = iota((rows, LANE), 1), iota((rows, LANE), 0)
    turned = LANE - 1 - iota((8, LANE), 1)
    results = []
    for c in range(row_tiles):
        d = tile(c)
        left = jnp.where(lane == 0, spun[c - 1], spun[c])
        right = jnp.where(lane == LANE - 1, back[(c + 1) % row_tiles], back[c])
        under = jnp.where(at == 0, low[c : c + 1], pltpu.roll(d, 1, 0))
        fold = jnp.take_along_axis(tile(row_tiles - 1 - c)[rows - 8 :], turned, axis=1)[7:8]
        over_row = jnp.where(top, fold, high[c : c + 1])
        over = jnp.where(at == rows - 1, over_row, pltpu.roll(d, rows - 1, 0))
        span = slice(c * LANE, (c + 1) * LANE)
        near = under + over + left + right
        value = free_ref[:, span] + (2.0 * d + nu_ref[c : c + 1] * (near - 4.0 * d))
        next_ref[:, span] = value
        results.append(value.astype(BF16))
    cells = jnp.concatenate(results, axis=0)
    for g in range(groups):
        column = jnp.transpose(jnp.broadcast_to(keys[g], (LANE, LANE)))
        wide = jnp.concatenate([column] * -(-total // LANE), axis=1)[:, :total]
        picked = dot(onehot(wide == iota((LANE, total), 1)), cells)
        return_ref[pl.ds(g * LANE, LANE), :] = picked.astype(BF16)


def backward_kernel(came_ref, sort_ref, back_ref, weight_ref, out_ref):
    values = dot(sort_ref[...], came_ref[...])
    blocks = values.shape[0]
    row = iota((CHUNK, LANE), 0)
    parts = []
    for n in range(blocks // CHUNK):
        value = values[n * CHUNK : (n + 1) * CHUNK].astype(BF16)
        weight = weight_ref[pl.ds(n * CHUNK, CHUNK)].reshape(CHUNK * LANE, LANE)
        full = dot_nt(value, weight)
        part = full[:, :LANE]
        for q in range(1, CHUNK):
            part = jnp.where(row == q, full[:, q * LANE : (q + 1) * LANE], part)
        parts.append(part)
    result = jnp.concatenate(parts, axis=0)
    coarse = result.astype(BF16)
    fine = (result - coarse.astype(F32)).astype(BF16)
    tiles = dot(back_ref[...], coarse) + dot(back_ref[...], fine)
    rows = out_ref.shape[0]
    for c in range(out_ref.shape[1] // LANE):
        out_ref[:, c * LANE : (c + 1) * LANE] = tiles[c * rows : (c + 1) * rows]


def call(kernel, outs, specs, cost, scratch=(), limit=24 << 20):
    run = pl.pallas_call(
        kernel,
        out_shape=outs,
        in_specs=specs,
        out_specs=jax.tree.map(lambda _: VMEM, outs),
        scratch_shapes=scratch,
        compiler_params=pltpu.CompilerParams(vmem_limit_bytes=limit),
        cost_estimate=pl.CostEstimate(flops=cost, bytes_accessed=cost // 64, transcendentals=0),
    )

    def placed(*args):
        return run(
            *[
                pltpu.with_memory_space_constraint(x, pltpu.HBM) if spec is HBM else x
                for x, spec in zip(args, specs)
            ]
        )

    return placed


def per_device(
    atm_state,
    atm_kappa,
    forcing,
    flux_gain,
    remap_weight,
    remap_source,
    remap_owner,
    remap_dest,
    ocean_state,
    ocean_nu,
    flux_coef,
):
    ntiles = lax.axis_size("tiles")
    me = lax.axis_index("tiles")
    blocks = remap_source.shape[0]
    capacity = max(2, 2 * blocks // ntiles)
    main = -(-capacity // 16) * 16
    rows = main + 2 * EDGE
    atm_rows, atm_cols = atm_state.shape
    ocean_rows, ocean_cols = ocean_state.shape
    atm_tiles = atm_rows * atm_cols // LANE
    row_tiles = ocean_cols // LANE
    shape = jax.ShapeDtypeStruct
    me_arr = me.astype(jnp.int32).reshape(1)
    edges = shape((2, atm_cols + ocean_cols), F32)
    atm, ocean, to_even, to_odd = call(
        send_kernel,
        (shape(atm_state.shape, F32), shape(ocean_state.shape, F32), edges, edges),
        [SMEM, HBM, HBM],
        1 << 20,
        [pltpu.SemaphoreType.DMA((2,))],
    )(me_arr, atm_state, ocean_state)
    pairs = [(2 * k + 1, (2 * k + 2) % ntiles) for k in range(ntiles // 2)]
    from_odd = lax.ppermute(to_odd, "tiles", pairs + [(j, i) for i, j in pairs])
    from_even = lax.ppermute(to_even, "tiles", [(i, i ^ 1) for i in range(ntiles)])
    atm_row_tiles = atm_cols // LANE
    nflux = forcing.shape[0]
    pick, back, slots, sort, ids, field, scale, kappa, nu, weight = call(
        functools.partial(
            stage_kernel, ntiles, main, atm_rows, atm_row_tiles, ocean_rows, row_tiles
        ),
        (
            shape((blocks, atm_tiles), BF16),
            shape((atm_tiles, blocks), BF16),
            shape((ntiles * rows, blocks), BF16),
            shape((blocks, ntiles * main), BF16),
            shape((2, ntiles, LANE), F32),
            shape(atm_state.shape, F32),
            shape((1, LANE), F32),
            shape((1, atm_cols), F32),
            shape((row_tiles, LANE), F32),
            shape(remap_weight.shape, BF16),
        ),
        [SMEM] + [HBM] * 9,
        1 << 31,
        [
            pltpu.VMEM((3, 1, blocks), jnp.int32),
            pltpu.VMEM((2, 1, nflux), F32),
            pltpu.VMEM(forcing.shape, BF16),
            pltpu.SemaphoreType.DMA((8 + PIECES,)),
        ],
    )(
        me_arr,
        remap_source.reshape(1, blocks),
        remap_owner.reshape(1, blocks),
        remap_dest.reshape(1, blocks),
        flux_gain.reshape(1, nflux),
        flux_coef.reshape(1, nflux),
        atm_kappa.reshape(1, atm_cols),
        ocean_nu.reshape(row_tiles, LANE),
        forcing,
        remap_weight,
    )
    atm_next, outgoing = call(
        functools.partial(forward_kernel, ntiles, main),
        (shape(atm_state.shape, F32), shape((ntiles * rows, LANE), BF16)),
        [SMEM] + [VMEM] * 10,
        1 << 28,
        [pltpu.VMEM((2 * atm_rows, atm_cols), F32)],
    )(me_arr, atm, kappa, from_even, from_odd, field, scale, pick, slots, ids, weight)
    arrived = lax.all_to_all(outgoing, "tiles", split_axis=0, concat_axis=0, tiled=True)
    free = call(
        functools.partial(free_ocean_kernel, ntiles, atm_cols),
        shape(ocean_state.shape, F32),
        [SMEM] + [VMEM] * 4,
        1 << 27,
        [pltpu.VMEM((ocean_rows + 8, ocean_cols), F32)],
    )(me_arr, ocean, nu, from_even, from_odd)
    ocean_next, returned = call(
        functools.partial(ocean_kernel, ntiles, main),
        (shape(ocean_state.shape, F32), shape((ntiles * main, LANE), BF16)),
        [SMEM] + [VMEM] * 3,
        1 << 27,
    )(me_arr, arrived, free, nu)
    came_back = lax.all_to_all(returned, "tiles", split_axis=0, concat_axis=0, tiled=True)
    feedback = call(
        backward_kernel,
        shape(atm_state.shape, F32),
        [VMEM] * 4,
        1 << 28,
    )(came_back, sort, back, weight)
    return (atm_next, ocean_next, feedback)


def solution(mesh):
    return jax.shard_map(
        per_device,
        mesh=mesh,
        in_specs=(
            P(("members", "tiles"), None),
            P(),
            P(None, ("members", "tiles"), None),
            P(),
            P("tiles", None, None),
            P("tiles"),
            P("tiles", None),
            P("tiles"),
            P(("members", "tiles"), None),
            P(),
            P(),
        ),
        out_specs=(
            P(("members", "tiles"), None),
            P(("members", "tiles"), None),
            P(("members", "tiles"), None),
        ),
        check_vma=False,
    )
```

```python
import functools

import jax
import jax.numpy as jnp
from jax import lax
from jax.experimental import pallas as pl
from jax.experimental.pallas import tpu as pltpu
from jax.sharding import PartitionSpec as P

LANE = 128
EDGE = 32
CHUNK = 8
PIECE = 32
EARLY = 64
F32 = jnp.float32
BF16 = jnp.bfloat16
VMEM = pl.BlockSpec(memory_space=pltpu.VMEM)
SMEM = pl.BlockSpec(memory_space=pltpu.SMEM)
HBM = pl.BlockSpec(memory_space=pltpu.HBM)


def iota(shape, dim):
    return lax.broadcasted_iota(jnp.int32, shape, dim)


def dot(a, b):
    return lax.dot_general(a, b, (((1,), (0,)), ((), ())), preferred_element_type=F32)


def dot_nt(a, b):
    return lax.dot_general(a, b, (((1,), (1,)), ((), ())), preferred_element_type=F32)


def onehot(mask):
    return jnp.where(mask, 1.0, 0.0).astype(BF16)


def as_column(row):
    parts = [
        jnp.transpose(jnp.broadcast_to(row[:, k : k + LANE], (LANE, LANE)))
        for k in range(0, row.shape[1], LANE)
    ]
    return jnp.concatenate(parts, axis=0)


def matches_lane(column, width):
    parts = [
        onehot(column == iota(column.shape, 1) + k)[:, : min(LANE, width - k)]
        for k in range(0, width, LANE)
    ]
    return jnp.concatenate(parts, axis=1)


def fetches(weight_hbm, first, held, sems):
    copies = []
    for n in range(held.shape[0] // PIECE):
        copies.append(
            pltpu.make_async_copy(
                weight_hbm.at[pl.ds(first + n * PIECE, PIECE)],
                held.at[pl.ds(n * PIECE, PIECE)],
                sems.at[n],
            )
        )
    return copies


def send_kernel(me_ref, atm_hbm, ocean_hbm, atm_ref, ocean_ref, even_ref, odd_ref, sems):
    copies = [
        pltpu.make_async_copy(atm_hbm, atm_ref, sems.at[0]),
        pltpu.make_async_copy(ocean_hbm, ocean_ref, sems.at[1]),
    ]
    for copy in copies:
        copy.start()
    even = me_ref[0] % 2 == 0
    start = 0
    for copy, ref in zip(copies, (atm_ref, ocean_ref)):
        copy.wait()
        rows, cols = ref.shape
        first, last = ref[0:2], ref[rows - 2 : rows]
        even_ref[:, start : start + cols] = jnp.where(even, last, first)
        odd_ref[:, start : start + cols] = jnp.where(even, first, last)
        start += cols


def stage_kernel(
    ntiles, main, atm_rows, atm_row_tiles, ocean_rows, row_tiles,
    me_ref, src_hbm, own_hbm, dst_hbm, gain_hbm, coef_hbm, kappa_hbm, nu_hbm, forcing_hbm,
    weight_hbm,
    pick_ref, back_ref, slots_ref, sort_ref, ids_ref, field_ref, scale_ref, kappa_ref, nu_ref,
    weight_ref,
    ints, gains, forcing_ref, sems, weight_sems,
):
    small = [
        (src_hbm, ints.at[0]), (own_hbm, ints.at[1]), (dst_hbm, ints.at[2]),
        (gain_hbm, gains.at[0]), (coef_hbm, gains.at[1]), (forcing_hbm, forcing_ref),
        (kappa_hbm, kappa_ref), (nu_hbm, nu_ref),
    ]
    copies = [pltpu.make_async_copy(a, b, sems.at[k]) for k, (a, b) in enumerate(small)]
    copies += fetches(weight_hbm, 0, weight_ref, weight_sems)
    for copy in copies:
        copy.start()
    for copy in copies[:3]:
        copy.wait()
    rows = main + 2 * EDGE
    per_lane = LANE // main
    source, owner, dest = ints[0], ints[1], ints[2]
    blocks = owner.shape[1]
    source = (source % atm_row_tiles) * atm_rows + source // atm_row_tiles
    row_of, col_of = dest // row_tiles, dest % row_tiles
    match = owner == iota((ntiles, blocks), 0)
    above = onehot(iota((blocks, blocks), 0) < iota((blocks, blocks), 1))
    rank = jnp.sum(
        jnp.where(match, dot(onehot(match), above), 0.0), axis=0, keepdims=True
    ).astype(jnp.int32)
    pick_ref[...] = matches_lane(as_column(source), pick_ref.shape[1])
    back_ref[...] = onehot(source == iota(back_ref.shape, 0))
    sort_ref[...] = matches_lane(as_column(owner * main + rank), sort_ref.shape[1])
    own_slot = owner * rows + rank
    low = (row_of == ocean_rows - 1) & (owner < ntiles - 1)
    low_slot = jnp.where(low, (owner + 1) * rows + main + col_of, -1)
    high = (row_of == 0) & (owner > 0)
    high_slot = jnp.where(high, (owner - 1) * rows + main + EDGE + col_of, -1)
    for t in range(ntiles):
        slot = iota((rows, blocks), 0) + t * rows
        slots_ref[pl.ds(t * rows, rows), :] = onehot(
            (slot == own_slot) | (slot == low_slot) | (slot == high_slot)
        )
    lane_of = rank + (me_ref[0] % per_lane) * main
    place = onehot(lane_of == iota((LANE, blocks), 0))
    ids_ref[0] = dot_nt(jnp.where(match, (col_of + 1).astype(F32), 0.0).astype(BF16), place)
    ids_ref[1] = dot_nt(jnp.where(match, row_of.astype(F32), 0.0).astype(BF16), place)
    for copy in copies[3 : len(small)]:
        copy.wait()
    coef = gains[1]
    scale_ref[...] = jnp.broadcast_to(
        jnp.sum(gains[0] * coef, axis=1, keepdims=True), scale_ref.shape
    )
    field = jnp.zeros(field_ref.shape, F32)
    for k in range(forcing_ref.shape[0]):
        field = field + coef[:, k : k + 1] * forcing_ref[k].astype(F32)
    field_ref[...] = field
    for copy in copies[len(small) :]:
        copy.wait()


def forward_kernel(
    ntiles, main, me_ref, atm_ref, kappa_ref, even_ref, odd_ref, field_ref, scale_ref,
    pick_ref, slots_ref, ids_ref, weight_ref, next_ref, out_ref, work,
):
    atm_rows, cols = atm_ref.shape
    rows = main + 2 * EDGE
    even = me_ref[0] % 2 == 0
    ev, od = even_ref[:, :cols], odd_ref[:, :cols]
    size = 2 * atm_rows
    work[0:atm_rows] = atm_ref[...]
    work[atm_rows : 2 * atm_rows] = jnp.zeros((atm_rows, cols), F32)
    work[size - 2 : size] = jnp.where(even, od, ev)
    work[atm_rows : atm_rows + 2] = jnp.where(even, ev, od)
    x = work[...]
    kappa = kappa_ref[...]
    for _ in range(2):
        near = (
            pltpu.roll(x, 1, 0) + pltpu.roll(x, size - 1, 0)
            + pltpu.roll(x, 1, 1) + pltpu.roll(x, cols - 1, 1)
        )
        x = x + kappa * (near - 4.0 * x)
    atm = x[:atm_rows]
    next_ref[...] = atm
    field = field_ref[...] + scale_ref[:, 0:1] * atm
    tiles = jnp.concatenate(
        [field[:, c * LANE : (c + 1) * LANE] for c in range(cols // LANE)], axis=0
    ).astype(BF16)
    pieces = dot(pick_ref[...], tiles)
    blocks = pieces.shape[0]
    row = iota((CHUNK, LANE), 0)
    parts = []
    for n in range(blocks // CHUNK):
        piece = pieces[n * CHUNK : (n + 1) * CHUNK]
        spread = jnp.concatenate(
            [jnp.where(row == q, piece, 0.0) for q in range(CHUNK)], axis=1
        ).astype(BF16)
        weight = weight_ref[pl.ds(n * CHUNK, CHUNK)].reshape(CHUNK * LANE, LANE)
        parts.append(dot(spread, weight))
    contribution = jnp.concatenate(parts, axis=0).astype(BF16)
    at = iota((EDGE, LANE), 0)
    for t in range(ntiles):
        sent = dot(slots_ref[pl.ds(t * rows, rows), :], contribution)
        low = sent[main : main + EDGE]
        low = jnp.where(at == EDGE - 4, ids_ref[0, t : t + 1, :], low)
        low = jnp.where(at == EDGE - 3, ids_ref[1, t : t + 1, :], low)
        out_ref[pl.ds(t * rows, main), :] = sent[:main].astype(BF16)
        out_ref[pl.ds(t * rows + main, EDGE), :] = low.astype(BF16)
        out_ref[pl.ds(t * rows + main + EDGE, EDGE), :] = sent[main + EDGE :].astype(BF16)


def reverse_lanes(x):
    tiles = x.shape[1] // LANE
    back = LANE - 1 - iota((x.shape[0], LANE), 1)
    parts = [
        jnp.take_along_axis(x[:, c * LANE : (c + 1) * LANE], back, axis=1) for c in range(tiles)
    ]
    return jnp.concatenate(parts[::-1], axis=1)


def free_ocean_kernel(ntiles, offset, me_ref, ocean_ref, nu_ref, even_ref, odd_ref, out_ref, work):
    rows, cols = ocean_ref.shape
    me = me_ref[0]
    even, bottom, top = me % 2 == 0, me == 0, me == ntiles - 1
    ev, od = even_ref[:, offset:], odd_ref[:, offset:]
    size = rows + 8
    work[0:rows] = ocean_ref[...]
    work[rows:size] = jnp.zeros((8, cols), F32)
    work[size - 2 : size] = jnp.where(bottom, 0.0, jnp.where(even, od, ev))
    work[rows : rows + 2] = jnp.where(even, ev, od)
    nu = jnp.concatenate([nu_ref[c : c + 1] for c in range(cols // LANE)], axis=1)
    x = work[...]
    at = iota((size, cols), 0)
    for _ in range(2):
        folded = pltpu.roll(reverse_lanes(x[rows - 8 : rows]), 1, 0)
        tail = jnp.where(top & (iota((8, cols), 0) == 0), folded, x[rows:])
        x = jnp.concatenate([x[:rows], tail], axis=0)
        near = (
            pltpu.roll(x, 1, 0) + pltpu.roll(x, size - 1, 0)
            + pltpu.roll(x, 1, 1) + pltpu.roll(x, cols - 1, 1)
        )
        x = x + nu * (near - 4.0 * x)
        x = jnp.where(bottom & (at >= rows + 4), 0.0, x)
    out_ref[...] = x[:rows]


def ocean_kernel(ntiles, main, me_ref, arrived_ref, free_ref, nu_ref, next_ref, return_ref):
    rows, cols = free_ref.shape
    row_tiles = cols // LANE
    per_lane = LANE // main
    step = main + 2 * EDGE
    total = rows * row_tiles
    top = me_ref[0] == ntiles - 1
    groups = ntiles // per_lane
    drive = jnp.zeros((total, LANE), F32)
    low = jnp.zeros((EDGE, LANE), F32)
    high = jnp.zeros((EDGE, LANE), F32)
    keys = []
    for g in range(groups):
        edge = jnp.zeros((EDGE, LANE), F32)
        values = []
        for s in range(g * per_lane, (g + 1) * per_lane):
            values.append(arrived_ref[pl.ds(s * step, main), :])
            edge = edge + arrived_ref[pl.ds(s * step + main, EDGE), :].astype(F32)
            high = high + arrived_ref[pl.ds(s * step + main + EDGE, EDGE), :].astype(F32)
        low = low + edge
        key = (edge[EDGE - 4 : EDGE - 3] - 1.0) * rows + edge[EDGE - 3 : EDGE - 2]
        key = key.astype(jnp.int32)
        keys.append(key)
        drive = drive + dot(
            onehot(key == iota((total, LANE), 0)), jnp.concatenate(values, axis=0)
        )
    tile = lambda c: drive[c * rows : (c + 1) * rows]
    spun = [pltpu.roll(tile(c), 1, 1) for c in range(row_tiles)]
    back = [pltpu.roll(tile(c), LANE - 1, 1) for c in range(row_tiles)]
    lane, at = iota((rows, LANE), 1), iota((rows, LANE), 0)
    turned = LANE - 1 - iota((8, LANE), 1)
    results = []
    for c in range(row_tiles):
        d = tile(c)
        left = jnp.where(lane == 0, spun[c - 1], spun[c])
        right = jnp.where(lane == LANE - 1, back[(c + 1) % row_tiles], back[c])
        under = jnp.where(at == 0, low[c : c + 1], pltpu.roll(d, 1, 0))
        fold = jnp.take_along_axis(tile(row_tiles - 1 - c)[rows - 8 :], turned, axis=1)[7:8]
        over_row = jnp.where(top, fold, high[c : c + 1])
        over = jnp.where(at == rows - 1, over_row, pltpu.roll(d, rows - 1, 0))
        span = slice(c * LANE, (c + 1) * LANE)
        near = under + over + left + right
        value = free_ref[:, span] + (2.0 * d + nu_ref[c : c + 1] * (near - 4.0 * d))
        next_ref[:, span] = value
        results.append(value.astype(BF16))
    cells = jnp.concatenate(results, axis=0)
    for g in range(groups):
        column = jnp.transpose(jnp.broadcast_to(keys[g], (LANE, LANE)))
        wide = jnp.concatenate([column] * -(-total // LANE), axis=1)[:, :total]
        picked = dot(onehot(wide == iota((LANE, total), 1)), cells)
        return_ref[pl.ds(g * LANE, LANE), :] = picked.astype(BF16)


def fetch_kernel(after_hbm, weight_hbm, weight_ref, sems):
    copies = fetches(weight_hbm, 0, weight_ref, sems)
    for copy in copies:
        copy.start()
    for copy in copies:
        copy.wait()


def backward_kernel(
    came_ref, sort_ref, back_ref, early_ref, weight_hbm, out_ref, late_ref, sems
):
    early = early_ref.shape[0]
    copies = fetches(weight_hbm, early, late_ref, sems)
    for copy in copies:
        copy.start()
    values = dot(sort_ref[...], came_ref[...])
    blocks = values.shape[0]
    row = iota((CHUNK, LANE), 0)
    parts = []
    for n in range(blocks // CHUNK):
        value = values[n * CHUNK : (n + 1) * CHUNK].astype(BF16)
        at = n * CHUNK - early
        if at >= 0 and at % PIECE == 0:
            copies[at // PIECE].wait()
        held = early_ref[pl.ds(n * CHUNK, CHUNK)] if at < 0 else late_ref[pl.ds(at, CHUNK)]
        weight = held.reshape(CHUNK * LANE, LANE)
        full = dot_nt(value, weight)
        part = full[:, :LANE]
        for q in range(1, CHUNK):
            part = jnp.where(row == q, full[:, q * LANE : (q + 1) * LANE], part)
        parts.append(part)
    result = jnp.concatenate(parts, axis=0)
    coarse = result.astype(BF16)
    fine = (result - coarse.astype(F32)).astype(BF16)
    tiles = dot(back_ref[...], coarse) + dot(back_ref[...], fine)
    rows = out_ref.shape[0]
    for c in range(out_ref.shape[1] // LANE):
        out_ref[:, c * LANE : (c + 1) * LANE] = tiles[c * rows : (c + 1) * rows]


def call(kernel, outs, specs, cost, scratch=(), limit=24 << 20):
    run = pl.pallas_call(
        kernel,
        out_shape=outs,
        in_specs=specs,
        out_specs=jax.tree.map(lambda _: VMEM, outs),
        scratch_shapes=scratch,
        compiler_params=pltpu.CompilerParams(vmem_limit_bytes=limit),
        cost_estimate=pl.CostEstimate(flops=cost, bytes_accessed=cost // 64, transcendentals=0),
    )

    def placed(*args):
        return run(
            *[
                pltpu.with_memory_space_constraint(x, pltpu.HBM) if spec is HBM else x
                for x, spec in zip(args, specs)
            ]
        )

    return placed


def per_device(
    atm_state,
    atm_kappa,
    forcing,
    flux_gain,
    remap_weight,
    remap_source,
    remap_owner,
    remap_dest,
    ocean_state,
    ocean_nu,
    flux_coef,
):
    ntiles = lax.axis_size("tiles")
    me = lax.axis_index("tiles")
    blocks = remap_source.shape[0]
    capacity = max(2, 2 * blocks // ntiles)
    main = -(-capacity // 16) * 16
    rows = main + 2 * EDGE
    atm_rows, atm_cols = atm_state.shape
    ocean_rows, ocean_cols = ocean_state.shape
    atm_tiles = atm_rows * atm_cols // LANE
    row_tiles = ocean_cols // LANE
    shape = jax.ShapeDtypeStruct
    me_arr = me.astype(jnp.int32).reshape(1)
    edges = shape((2, atm_cols + ocean_cols), F32)
    atm, ocean, to_even, to_odd = call(
        send_kernel,
        (shape(atm_state.shape, F32), shape(ocean_state.shape, F32), edges, edges),
        [SMEM, HBM, HBM],
        1 << 20,
        [pltpu.SemaphoreType.DMA((2,))],
    )(me_arr, atm_state, ocean_state)
    pairs = [(2 * k + 1, (2 * k + 2) % ntiles) for k in range(ntiles // 2)]
    from_odd = lax.ppermute(to_odd, "tiles", pairs + [(j, i) for i, j in pairs])
    from_even = lax.ppermute(to_even, "tiles", [(i, i ^ 1) for i in range(ntiles)])
    atm_row_tiles = atm_cols // LANE
    early = min(EARLY, blocks)
    whole = blocks // PIECE
    nflux = forcing.shape[0]
    pick, back, slots, sort, ids, field, scale, kappa, nu, weight = call(
        functools.partial(
            stage_kernel, ntiles, main, atm_rows, atm_row_tiles, ocean_rows, row_tiles
        ),
        (
            shape((blocks, atm_tiles), BF16),
            shape((atm_tiles, blocks), BF16),
            shape((ntiles * rows, blocks), BF16),
            shape((blocks, ntiles * main), BF16),
            shape((2, ntiles, LANE), F32),
            shape(atm_state.shape, F32),
            shape((1, LANE), F32),
            shape((1, atm_cols), F32),
            shape((row_tiles, LANE), F32),
            shape(remap_weight.shape, BF16),
        ),
        [SMEM] + [HBM] * 9,
        1 << 31,
        [
            pltpu.VMEM((3, 1, blocks), jnp.int32),
            pltpu.VMEM((2, 1, nflux), F32),
            pltpu.VMEM(forcing.shape, BF16),
            pltpu.SemaphoreType.DMA((8,)),
            pltpu.SemaphoreType.DMA((whole,)),
        ],
    )(
        me_arr,
        remap_source.reshape(1, blocks),
        remap_owner.reshape(1, blocks),
        remap_dest.reshape(1, blocks),
        flux_gain.reshape(1, nflux),
        flux_coef.reshape(1, nflux),
        atm_kappa.reshape(1, atm_cols),
        ocean_nu.reshape(row_tiles, LANE),
        forcing,
        remap_weight,
    )
    atm_next, outgoing = call(
        functools.partial(forward_kernel, ntiles, main),
        (shape(atm_state.shape, F32), shape((ntiles * rows, LANE), BF16)),
        [SMEM] + [VMEM] * 10,
        1 << 28,
        [pltpu.VMEM((2 * atm_rows, atm_cols), F32)],
    )(me_arr, atm, kappa, from_even, from_odd, field, scale, pick, slots, ids, weight)
    arrived = lax.all_to_all(outgoing, "tiles", split_axis=0, concat_axis=0, tiled=True)
    free = call(
        functools.partial(free_ocean_kernel, ntiles, atm_cols),
        shape(ocean_state.shape, F32),
        [SMEM] + [VMEM] * 4,
        1 << 27,
        [pltpu.VMEM((ocean_rows + 8, ocean_cols), F32)],
    )(me_arr, ocean, nu, from_even, from_odd)
    ocean_next, returned = call(
        functools.partial(ocean_kernel, ntiles, main),
        (shape(ocean_state.shape, F32), shape((ntiles * main, LANE), BF16)),
        [SMEM] + [VMEM] * 3,
        1 << 27,
    )(me_arr, arrived, free, nu)
    came_back = lax.all_to_all(returned, "tiles", split_axis=0, concat_axis=0, tiled=True)
    again = call(
        fetch_kernel,
        shape((early, LANE, LANE), BF16),
        [HBM, HBM],
        1 << 31,
        [pltpu.SemaphoreType.DMA((early // PIECE,))],
    )(ocean_next, remap_weight)
    feedback = call(
        backward_kernel,
        shape(atm_state.shape, F32),
        [VMEM] * 4 + [HBM],
        1 << 28,
        [
            pltpu.VMEM((blocks - early, LANE, LANE), BF16),
            pltpu.SemaphoreType.DMA(((blocks - early) // PIECE,)),
        ],
    )(came_back, sort, back, again, remap_weight)
    return (atm_next, ocean_next, feedback)


def solution(mesh):
    return jax.shard_map(
        per_device,
        mesh=mesh,
        in_specs=(
            P(("members", "tiles"), None),
            P(),
            P(None, ("members", "tiles"), None),
            P(),
            P("tiles", None, None),
            P("tiles"),
            P("tiles", None),
            P("tiles"),
            P(("members", "tiles"), None),
            P(),
            P(),
        ),
        out_specs=(
            P(("members", "tiles"), None),
            P(("members", "tiles"), None),
            P(("members", "tiles"), None),
        ),
        check_vma=False,
    )
```

```python
import functools

import jax
import jax.numpy as jnp
from jax import lax
from jax.experimental import pallas as pl
from jax.experimental.pallas import tpu as pltpu
from jax.sharding import PartitionSpec as P

LANE = 128
EDGE = 32
CHUNK = 8
PIECE = 32
EARLY = 64
F32 = jnp.float32
BF16 = jnp.bfloat16
VMEM = pl.BlockSpec(memory_space=pltpu.VMEM)
SMEM = pl.BlockSpec(memory_space=pltpu.SMEM)
HBM = pl.BlockSpec(memory_space=pltpu.HBM)


def iota(shape, dim):
    return lax.broadcasted_iota(jnp.int32, shape, dim)


def dot(a, b):
    return lax.dot_general(a, b, (((1,), (0,)), ((), ())), preferred_element_type=F32)


def dot_nt(a, b):
    return lax.dot_general(a, b, (((1,), (1,)), ((), ())), preferred_element_type=F32)


def onehot(mask):
    return jnp.where(mask, 1.0, 0.0).astype(BF16)


def as_column(row):
    parts = [
        jnp.transpose(jnp.broadcast_to(row[:, k : k + LANE], (LANE, LANE)))
        for k in range(0, row.shape[1], LANE)
    ]
    return jnp.concatenate(parts, axis=0)


def matches_lane(column, width):
    parts = [
        onehot(column == iota(column.shape, 1) + k)[:, : min(LANE, width - k)]
        for k in range(0, width, LANE)
    ]
    return jnp.concatenate(parts, axis=1)


def fetches(weight_hbm, first, held, sems):
    copies = []
    for n in range(held.shape[0] // PIECE):
        copies.append(
            pltpu.make_async_copy(
                weight_hbm.at[pl.ds(first + n * PIECE, PIECE)],
                held.at[pl.ds(n * PIECE, PIECE)],
                sems.at[n],
            )
        )
    return copies


def edge_rows(upper, atm_ref, ocean_ref, out_ref):
    start = 0
    for ref in (atm_ref, ocean_ref):
        rows, cols = ref.shape
        first, last = ref[0:2], ref[rows - 2 : rows]
        out_ref[:, start : start + cols] = jnp.where(upper, last, first)
        start += cols


def send_kernel(me_ref, atm_hbm, ocean_hbm, atm_ref, ocean_ref, odd_ref, sems):
    copies = [
        pltpu.make_async_copy(atm_hbm, atm_ref, sems.at[0]),
        pltpu.make_async_copy(ocean_hbm, ocean_ref, sems.at[1]),
    ]
    for copy in copies:
        copy.start()
    for copy in copies:
        copy.wait()
    edge_rows(me_ref[0] % 2 == 1, atm_ref, ocean_ref, odd_ref)


def stage_kernel(
    ntiles, main, atm_rows, atm_row_tiles, ocean_rows, row_tiles,
    me_ref, atm_ref, ocean_ref, src_hbm, own_hbm, dst_hbm, gain_hbm, coef_hbm, kappa_hbm, nu_hbm, forcing_hbm,
    pick_ref, back_ref, slots_ref, sort_ref, ids_ref, field_ref, scale_ref, kappa_ref, nu_ref,
    even_ref,
    ints, gains, forcing_ref, sems,
):
    small = [
        (src_hbm, ints.at[0]), (own_hbm, ints.at[1]), (dst_hbm, ints.at[2]),
        (gain_hbm, gains.at[0]), (coef_hbm, gains.at[1]), (forcing_hbm, forcing_ref),
        (kappa_hbm, kappa_ref), (nu_hbm, nu_ref),
    ]
    copies = [pltpu.make_async_copy(a, b, sems.at[k]) for k, (a, b) in enumerate(small)]
    for copy in copies:
        copy.start()
    edge_rows(me_ref[0] % 2 == 0, atm_ref, ocean_ref, even_ref)
    for copy in copies[:3]:
        copy.wait()
    rows = main + 2 * EDGE
    per_lane = LANE // main
    source, owner, dest = ints[0], ints[1], ints[2]
    blocks = owner.shape[1]
    source = (source % atm_row_tiles) * atm_rows + source // atm_row_tiles
    row_of, col_of = dest // row_tiles, dest % row_tiles
    match = owner == iota((ntiles, blocks), 0)
    above = onehot(iota((blocks, blocks), 0) < iota((blocks, blocks), 1))
    rank = jnp.sum(
        jnp.where(match, dot(onehot(match), above), 0.0), axis=0, keepdims=True
    ).astype(jnp.int32)
    pick_ref[...] = matches_lane(as_column(source), pick_ref.shape[1])
    back_ref[...] = onehot(source == iota(back_ref.shape, 0))
    sort_ref[...] = matches_lane(as_column(owner * main + rank), sort_ref.shape[1])
    own_slot = owner * rows + rank
    low = (row_of == ocean_rows - 1) & (owner < ntiles - 1)
    low_slot = jnp.where(low, (owner + 1) * rows + main + col_of, -1)
    high = (row_of == 0) & (owner > 0)
    high_slot = jnp.where(high, (owner - 1) * rows + main + EDGE + col_of, -1)
    for t in range(ntiles):
        slot = iota((rows, blocks), 0) + t * rows
        slots_ref[pl.ds(t * rows, rows), :] = onehot(
            (slot == own_slot) | (slot == low_slot) | (slot == high_slot)
        )
    lane_of = rank + (me_ref[0] % per_lane) * main
    place = onehot(lane_of == iota((LANE, blocks), 0))
    ids_ref[0] = dot_nt(jnp.where(match, (col_of + 1).astype(F32), 0.0).astype(BF16), place)
    ids_ref[1] = dot_nt(jnp.where(match, row_of.astype(F32), 0.0).astype(BF16), place)
    for copy in copies[3 : len(small)]:
        copy.wait()
    coef = gains[1]
    scale_ref[...] = jnp.broadcast_to(
        jnp.sum(gains[0] * coef, axis=1, keepdims=True), scale_ref.shape
    )
    field = jnp.zeros(field_ref.shape, F32)
    for k in range(forcing_ref.shape[0]):
        field = field + coef[:, k : k + 1] * forcing_ref[k].astype(F32)
    field_ref[...] = field


def forward_kernel(
    ntiles, main, me_ref, atm_ref, kappa_ref, even_ref, odd_ref, field_ref, scale_ref,
    pick_ref, slots_ref, ids_ref, weight_ref, next_ref, out_ref, work,
):
    atm_rows, cols = atm_ref.shape
    rows = main + 2 * EDGE
    even = me_ref[0] % 2 == 0
    ev, od = even_ref[:, :cols], odd_ref[:, :cols]
    size = 2 * atm_rows
    work[0:atm_rows] = atm_ref[...]
    work[atm_rows : 2 * atm_rows] = jnp.zeros((atm_rows, cols), F32)
    work[size - 2 : size] = jnp.where(even, od, ev)
    work[atm_rows : atm_rows + 2] = jnp.where(even, ev, od)
    x = work[...]
    kappa = kappa_ref[...]
    for _ in range(2):
        near = (
            pltpu.roll(x, 1, 0) + pltpu.roll(x, size - 1, 0)
            + pltpu.roll(x, 1, 1) + pltpu.roll(x, cols - 1, 1)
        )
        x = x + kappa * (near - 4.0 * x)
    atm = x[:atm_rows]
    next_ref[...] = atm
    field = field_ref[...] + scale_ref[:, 0:1] * atm
    tiles = jnp.concatenate(
        [field[:, c * LANE : (c + 1) * LANE] for c in range(cols // LANE)], axis=0
    ).astype(BF16)
    pieces = dot(pick_ref[...], tiles)
    blocks = pieces.shape[0]
    row = iota((CHUNK, LANE), 0)
    parts = []
    for n in range(blocks // CHUNK):
        piece = pieces[n * CHUNK : (n + 1) * CHUNK]
        spread = jnp.concatenate(
            [jnp.where(row == q, piece, 0.0) for q in range(CHUNK)], axis=1
        ).astype(BF16)
        weight = weight_ref[pl.ds(n * CHUNK, CHUNK)].reshape(CHUNK * LANE, LANE)
        parts.append(dot(spread, weight))
    contribution = jnp.concatenate(parts, axis=0).astype(BF16)
    at = iota((EDGE, LANE), 0)
    for t in range(ntiles):
        sent = dot(slots_ref[pl.ds(t * rows, rows), :], contribution)
        low = sent[main : main + EDGE]
        low = jnp.where(at == EDGE - 4, ids_ref[0, t : t + 1, :], low)
        low = jnp.where(at == EDGE - 3, ids_ref[1, t : t + 1, :], low)
        out_ref[pl.ds(t * rows, main), :] = sent[:main].astype(BF16)
        out_ref[pl.ds(t * rows + main, EDGE), :] = low.astype(BF16)
        out_ref[pl.ds(t * rows + main + EDGE, EDGE), :] = sent[main + EDGE :].astype(BF16)


def reverse_lanes(x):
    tiles = x.shape[1] // LANE
    back = LANE - 1 - iota((x.shape[0], LANE), 1)
    parts = [
        jnp.take_along_axis(x[:, c * LANE : (c + 1) * LANE], back, axis=1) for c in range(tiles)
    ]
    return jnp.concatenate(parts[::-1], axis=1)


def free_ocean_kernel(ntiles, offset, me_ref, ocean_ref, nu_ref, even_ref, odd_ref, out_ref, work):
    rows, cols = ocean_ref.shape
    me = me_ref[0]
    even, bottom, top = me % 2 == 0, me == 0, me == ntiles - 1
    ev, od = even_ref[:, offset:], odd_ref[:, offset:]
    size = rows + 8
    work[0:rows] = ocean_ref[...]
    work[rows:size] = jnp.zeros((8, cols), F32)
    work[size - 2 : size] = jnp.where(bottom, 0.0, jnp.where(even, od, ev))
    work[rows : rows + 2] = jnp.where(even, ev, od)
    nu = jnp.concatenate([nu_ref[c : c + 1] for c in range(cols // LANE)], axis=1)
    x = work[...]
    at = iota((size, cols), 0)
    for _ in range(2):
        folded = pltpu.roll(reverse_lanes(x[rows - 8 : rows]), 1, 0)
        tail = jnp.where(top & (iota((8, cols), 0) == 0), folded, x[rows:])
        x = jnp.concatenate([x[:rows], tail], axis=0)
        near = (
            pltpu.roll(x, 1, 0) + pltpu.roll(x, size - 1, 0)
            + pltpu.roll(x, 1, 1) + pltpu.roll(x, cols - 1, 1)
        )
        x = x + nu * (near - 4.0 * x)
        x = jnp.where(bottom & (at >= rows + 4), 0.0, x)
    out_ref[...] = x[:rows]


def ocean_kernel(ntiles, main, me_ref, arrived_ref, free_ref, nu_ref, next_ref, return_ref):
    rows, cols = free_ref.shape
    row_tiles = cols // LANE
    per_lane = LANE // main
    step = main + 2 * EDGE
    total = rows * row_tiles
    top = me_ref[0] == ntiles - 1
    groups = ntiles // per_lane
    drive = jnp.zeros((total, LANE), F32)
    low = jnp.zeros((EDGE, LANE), F32)
    high = jnp.zeros((EDGE, LANE), F32)
    keys = []
    for g in range(groups):
        edge = jnp.zeros((EDGE, LANE), F32)
        values = []
        for s in range(g * per_lane, (g + 1) * per_lane):
            values.append(arrived_ref[pl.ds(s * step, main), :])
            edge = edge + arrived_ref[pl.ds(s * step + main, EDGE), :].astype(F32)
            high = high + arrived_ref[pl.ds(s * step + main + EDGE, EDGE), :].astype(F32)
        low = low + edge
        key = (edge[EDGE - 4 : EDGE - 3] - 1.0) * rows + edge[EDGE - 3 : EDGE - 2]
        key = key.astype(jnp.int32)
        keys.append(key)
        drive = drive + dot(
            onehot(key == iota((total, LANE), 0)), jnp.concatenate(values, axis=0)
        )
    tile = lambda c: drive[c * rows : (c + 1) * rows]
    spun = [pltpu.roll(tile(c), 1, 1) for c in range(row_tiles)]
    back = [pltpu.roll(tile(c), LANE - 1, 1) for c in range(row_tiles)]
    lane, at = iota((rows, LANE), 1), iota((rows, LANE), 0)
    turned = LANE - 1 - iota((8, LANE), 1)
    results = []
    for c in range(row_tiles):
        d = tile(c)
        left = jnp.where(lane == 0, spun[c - 1], spun[c])
        right = jnp.where(lane == LANE - 1, back[(c + 1) % row_tiles], back[c])
        under = jnp.where(at == 0, low[c : c + 1], pltpu.roll(d, 1, 0))
        fold = jnp.take_along_axis(tile(row_tiles - 1 - c)[rows - 8 :], turned, axis=1)[7:8]
        over_row = jnp.where(top, fold, high[c : c + 1])
        over = jnp.where(at == rows - 1, over_row, pltpu.roll(d, rows - 1, 0))
        span = slice(c * LANE, (c + 1) * LANE)
        near = under + over + left + right
        value = free_ref[:, span] + (2.0 * d + nu_ref[c : c + 1] * (near - 4.0 * d))
        next_ref[:, span] = value
        results.append(value.astype(BF16))
    cells = jnp.concatenate(results, axis=0)
    for g in range(groups):
        column = jnp.transpose(jnp.broadcast_to(keys[g], (LANE, LANE)))
        wide = jnp.concatenate([column] * -(-total // LANE), axis=1)[:, :total]
        picked = dot(onehot(wide == iota((LANE, total), 1)), cells)
        return_ref[pl.ds(g * LANE, LANE), :] = picked.astype(BF16)


def fetch_kernel(after_hbm, weight_hbm, weight_ref, sems):
    copies = fetches(weight_hbm, 0, weight_ref, sems)
    for copy in copies:
        copy.start()
    for copy in copies:
        copy.wait()


def backward_kernel(
    came_ref, sort_ref, back_ref, early_ref, weight_hbm, out_ref, late_ref, sems
):
    early = early_ref.shape[0]
    copies = fetches(weight_hbm, early, late_ref, sems)
    for copy in copies:
        copy.start()
    values = dot(sort_ref[...], came_ref[...])
    blocks = values.shape[0]
    row = iota((CHUNK, LANE), 0)
    parts = []
    for n in range(blocks // CHUNK):
        value = values[n * CHUNK : (n + 1) * CHUNK].astype(BF16)
        at = n * CHUNK - early
        if at >= 0 and at % PIECE == 0:
            copies[at // PIECE].wait()
        held = early_ref[pl.ds(n * CHUNK, CHUNK)] if at < 0 else late_ref[pl.ds(at, CHUNK)]
        weight = held.reshape(CHUNK * LANE, LANE)
        full = dot_nt(value, weight)
        part = full[:, :LANE]
        for q in range(1, CHUNK):
            part = jnp.where(row == q, full[:, q * LANE : (q + 1) * LANE], part)
        parts.append(part)
    result = jnp.concatenate(parts, axis=0)
    coarse = result.astype(BF16)
    fine = (result - coarse.astype(F32)).astype(BF16)
    tiles = dot(back_ref[...], coarse) + dot(back_ref[...], fine)
    rows = out_ref.shape[0]
    for c in range(out_ref.shape[1] // LANE):
        out_ref[:, c * LANE : (c + 1) * LANE] = tiles[c * rows : (c + 1) * rows]


def call(kernel, outs, specs, cost, scratch=(), limit=24 << 20):
    run = pl.pallas_call(
        kernel,
        out_shape=outs,
        in_specs=specs,
        out_specs=jax.tree.map(lambda _: VMEM, outs),
        scratch_shapes=scratch,
        compiler_params=pltpu.CompilerParams(vmem_limit_bytes=limit),
        cost_estimate=pl.CostEstimate(flops=cost, bytes_accessed=cost // 64, transcendentals=0),
    )

    def placed(*args):
        return run(
            *[
                pltpu.with_memory_space_constraint(x, pltpu.HBM) if spec is HBM else x
                for x, spec in zip(args, specs)
            ]
        )

    return placed


def per_device(
    atm_state,
    atm_kappa,
    forcing,
    flux_gain,
    remap_weight,
    remap_source,
    remap_owner,
    remap_dest,
    ocean_state,
    ocean_nu,
    flux_coef,
):
    ntiles = lax.axis_size("tiles")
    me = lax.axis_index("tiles")
    blocks = remap_source.shape[0]
    capacity = max(2, 2 * blocks // ntiles)
    main = -(-capacity // 16) * 16
    rows = main + 2 * EDGE
    atm_rows, atm_cols = atm_state.shape
    ocean_rows, ocean_cols = ocean_state.shape
    atm_tiles = atm_rows * atm_cols // LANE
    row_tiles = ocean_cols // LANE
    shape = jax.ShapeDtypeStruct
    me_arr = me.astype(jnp.int32).reshape(1)
    edges = shape((2, atm_cols + ocean_cols), F32)
    atm, ocean, to_odd = call(
        send_kernel,
        (shape(atm_state.shape, F32), shape(ocean_state.shape, F32), edges),
        [SMEM, HBM, HBM],
        1 << 34,
        [pltpu.SemaphoreType.DMA((2,))],
    )(me_arr, atm_state, ocean_state)
    pairs = [(2 * k + 1, (2 * k + 2) % ntiles) for k in range(ntiles // 2)]
    from_odd = lax.ppermute(to_odd, "tiles", pairs + [(j, i) for i, j in pairs])
    atm_row_tiles = atm_cols // LANE
    early = min(EARLY, blocks)
    whole = blocks // PIECE
    nflux = forcing.shape[0]
    pick, back, slots, sort, ids, field, scale, kappa, nu, to_even = call(
        functools.partial(
            stage_kernel, ntiles, main, atm_rows, atm_row_tiles, ocean_rows, row_tiles
        ),
        (
            shape((blocks, atm_tiles), BF16),
            shape((atm_tiles, blocks), BF16),
            shape((ntiles * rows, blocks), BF16),
            shape((blocks, ntiles * main), BF16),
            shape((2, ntiles, LANE), F32),
            shape(atm_state.shape, F32),
            shape((1, LANE), F32),
            shape((1, atm_cols), F32),
            shape((row_tiles, LANE), F32),
            edges,
        ),
        [SMEM, VMEM, VMEM] + [HBM] * 8,
        1 << 20,
        [
            pltpu.VMEM((3, 1, blocks), jnp.int32),
            pltpu.VMEM((2, 1, nflux), F32),
            pltpu.VMEM(forcing.shape, BF16),
            pltpu.SemaphoreType.DMA((8,)),
        ],
    )(
        me_arr,
        atm,
        ocean,
        remap_source.reshape(1, blocks),
        remap_owner.reshape(1, blocks),
        remap_dest.reshape(1, blocks),
        flux_gain.reshape(1, nflux),
        flux_coef.reshape(1, nflux),
        atm_kappa.reshape(1, atm_cols),
        ocean_nu.reshape(row_tiles, LANE),
        forcing,
    )
    from_even = lax.ppermute(to_even, "tiles", [(i, i ^ 1) for i in range(ntiles)])
    atm_next, outgoing = call(
        functools.partial(forward_kernel, ntiles, main),
        (shape(atm_state.shape, F32), shape((ntiles * rows, LANE), BF16)),
        [SMEM] + [VMEM] * 10,
        1 << 28,
        [pltpu.VMEM((2 * atm_rows, atm_cols), F32)],
    )(me_arr, atm, kappa, from_even, from_odd, field, scale, pick, slots, ids, remap_weight)
    arrived = lax.all_to_all(outgoing, "tiles", split_axis=0, concat_axis=0, tiled=True)
    free = call(
        functools.partial(free_ocean_kernel, ntiles, atm_cols),
        shape(ocean_state.shape, F32),
        [SMEM] + [VMEM] * 4,
        1 << 27,
        [pltpu.VMEM((ocean_rows + 8, ocean_cols), F32)],
    )(me_arr, ocean, nu, from_even, from_odd)
    ocean_next, returned = call(
        functools.partial(ocean_kernel, ntiles, main),
        (shape(ocean_state.shape, F32), shape((ntiles * main, LANE), BF16)),
        [SMEM] + [VMEM] * 3,
        1 << 27,
    )(me_arr, arrived, free, nu)
    came_back = lax.all_to_all(returned, "tiles", split_axis=0, concat_axis=0, tiled=True)
    again = call(
        fetch_kernel,
        shape((early, LANE, LANE), BF16),
        [HBM, HBM],
        1 << 31,
        [pltpu.SemaphoreType.DMA((early // PIECE,))],
    )(ocean_next, remap_weight)
    feedback = call(
        backward_kernel,
        shape(atm_state.shape, F32),
        [VMEM] * 4 + [HBM],
        1 << 28,
        [
            pltpu.VMEM((blocks - early, LANE, LANE), BF16),
            pltpu.SemaphoreType.DMA(((blocks - early) // PIECE,)),
        ],
    )(came_back, sort, back, again, remap_weight)
    return (atm_next, ocean_next, feedback)


def solution(mesh):
    return jax.shard_map(
        per_device,
        mesh=mesh,
        in_specs=(
            P(("members", "tiles"), None),
            P(),
            P(None, ("members", "tiles"), None),
            P(),
            P("tiles", None, None),
            P("tiles"),
            P("tiles", None),
            P("tiles"),
            P(("members", "tiles"), None),
            P(),
            P(),
        ),
        out_specs=(
            P(("members", "tiles"), None),
            P(("members", "tiles"), None),
            P(("members", "tiles"), None),
        ),
        check_vma=False,
    )
```

```python
import functools

import jax
import jax.numpy as jnp
from jax import lax
from jax.experimental import pallas as pl
from jax.experimental.pallas import tpu as pltpu
from jax.sharding import PartitionSpec as P

LANE = 128
EDGE = 32
CHUNK = 8
PIECE = 32
EARLY = 64
F32 = jnp.float32
BF16 = jnp.bfloat16
VMEM = pl.BlockSpec(memory_space=pltpu.VMEM)
SMEM = pl.BlockSpec(memory_space=pltpu.SMEM)
HBM = pl.BlockSpec(memory_space=pltpu.HBM)


def iota(shape, dim):
    return lax.broadcasted_iota(jnp.int32, shape, dim)


def dot(a, b):
    return lax.dot_general(a, b, (((1,), (0,)), ((), ())), preferred_element_type=F32)


def dot_nt(a, b):
    return lax.dot_general(a, b, (((1,), (1,)), ((), ())), preferred_element_type=F32)


def onehot(mask):
    return jnp.where(mask, 1.0, 0.0).astype(BF16)


def as_column(row):
    parts = [
        jnp.transpose(jnp.broadcast_to(row[:, k : k + LANE], (LANE, LANE)))
        for k in range(0, row.shape[1], LANE)
    ]
    return jnp.concatenate(parts, axis=0)


def matches_lane(column, width):
    parts = [
        onehot(column == iota(column.shape, 1) + k)[:, : min(LANE, width - k)]
        for k in range(0, width, LANE)
    ]
    return jnp.concatenate(parts, axis=1)


def fetches(weight_hbm, first, held, sems):
    copies = []
    for n in range(held.shape[0] // PIECE):
        copies.append(
            pltpu.make_async_copy(
                weight_hbm.at[pl.ds(first + n * PIECE, PIECE)],
                held.at[pl.ds(n * PIECE, PIECE)],
                sems.at[n],
            )
        )
    return copies


def edge_rows(upper, atm_ref, ocean_ref, out_ref):
    start = 0
    for ref in (atm_ref, ocean_ref):
        rows, cols = ref.shape
        first, last = ref[0:2], ref[rows - 2 : rows]
        out_ref[:, start : start + cols] = jnp.where(upper, last, first)
        start += cols


def send_kernel(me_ref, atm_hbm, ocean_hbm, atm_ref, ocean_ref, odd_ref, sems):
    copies = [
        pltpu.make_async_copy(atm_hbm, atm_ref, sems.at[0]),
        pltpu.make_async_copy(ocean_hbm, ocean_ref, sems.at[1]),
    ]
    for copy in copies:
        copy.start()
    for copy in copies:
        copy.wait()
    edge_rows(me_ref[0] % 2 == 1, atm_ref, ocean_ref, odd_ref)


def stage_kernel(
    ntiles, main, atm_rows, atm_row_tiles, ocean_rows, row_tiles,
    me_ref, atm_ref, ocean_ref, src_hbm, own_hbm, dst_hbm, gain_hbm, coef_hbm, kappa_hbm, nu_hbm, forcing_hbm,
    pick_ref, keys_ref, slots_ref, ids_ref, field_ref, scale_ref, kappa_ref, nu_ref,
    even_ref,
    ints, gains, forcing_ref, sems,
):
    small = [
        (src_hbm, ints.at[0]), (own_hbm, ints.at[1]), (dst_hbm, ints.at[2]),
        (gain_hbm, gains.at[0]), (coef_hbm, gains.at[1]), (forcing_hbm, forcing_ref),
        (kappa_hbm, kappa_ref), (nu_hbm, nu_ref),
    ]
    copies = [pltpu.make_async_copy(a, b, sems.at[k]) for k, (a, b) in enumerate(small)]
    for copy in copies:
        copy.start()
    edge_rows(me_ref[0] % 2 == 0, atm_ref, ocean_ref, even_ref)
    for copy in copies[:3]:
        copy.wait()
    rows = main + EDGE
    per_lane = LANE // main
    source, owner, dest = ints[0], ints[1], ints[2]
    blocks = owner.shape[1]
    source = (source % atm_row_tiles) * atm_rows + source // atm_row_tiles
    row_of, col_of = dest // row_tiles, dest % row_tiles
    match = owner == iota((ntiles, blocks), 0)
    above = onehot(iota((blocks, blocks), 0) < iota((blocks, blocks), 1))
    rank = jnp.sum(
        jnp.where(match, dot(onehot(match), above), 0.0), axis=0, keepdims=True
    ).astype(jnp.int32)
    pick_ref[...] = matches_lane(as_column(source), pick_ref.shape[1])
    keys_ref[0] = source
    keys_ref[1] = owner * main + rank
    odd = owner % 2 == 1
    own_slot = owner * rows + rank
    beside = jnp.where(
        odd,
        (row_of - (ocean_rows - 1)) + jnp.where(owner < ntiles - 1, 0, 1),
        row_of + jnp.where(owner > 0, 0, 1),
    )
    side_slot = jnp.where(odd, owner + 1, owner - 1) * rows + main + col_of
    side_slot = jnp.where(beside == 0, side_slot, -1)
    for t in range(ntiles):
        slot = iota((rows, blocks), 0) + t * rows
        slots_ref[pl.ds(t * rows, rows), :] = onehot((slot == own_slot) | (slot == side_slot))
    lane_of = rank + (me_ref[0] % per_lane) * main
    place = onehot(lane_of == iota((LANE, blocks), 0))
    ids_ref[0] = dot_nt(jnp.where(match, (col_of + 1).astype(F32), 0.0).astype(BF16), place)
    ids_ref[1] = dot_nt(jnp.where(match, row_of.astype(F32), 0.0).astype(BF16), place)
    for copy in copies[3 : len(small)]:
        copy.wait()
    coef = gains[1]
    scale_ref[...] = jnp.broadcast_to(
        jnp.sum(gains[0] * coef, axis=1, keepdims=True), scale_ref.shape
    )
    field = jnp.zeros(field_ref.shape, F32)
    for k in range(forcing_ref.shape[0]):
        field = field + coef[:, k : k + 1] * forcing_ref[k].astype(F32)
    field_ref[...] = field


def forward_kernel(
    ntiles, main, me_ref, atm_ref, kappa_ref, even_ref, odd_ref, field_ref, scale_ref,
    pick_ref, slots_ref, ids_ref, weight_ref, next_ref, out_ref, work,
):
    atm_rows, cols = atm_ref.shape
    rows = main + EDGE
    even = me_ref[0] % 2 == 0
    ev, od = even_ref[:, :cols], odd_ref[:, :cols]
    size = 2 * atm_rows
    work[0:atm_rows] = atm_ref[...]
    work[atm_rows : 2 * atm_rows] = jnp.zeros((atm_rows, cols), F32)
    work[size - 2 : size] = jnp.where(even, od, ev)
    work[atm_rows : atm_rows + 2] = jnp.where(even, ev, od)
    x = work[...]
    kappa = kappa_ref[...]
    for _ in range(2):
        near = (
            pltpu.roll(x, 1, 0) + pltpu.roll(x, size - 1, 0)
            + pltpu.roll(x, 1, 1) + pltpu.roll(x, cols - 1, 1)
        )
        x = x + kappa * (near - 4.0 * x)
    atm = x[:atm_rows]
    next_ref[...] = atm
    field = field_ref[...] + scale_ref[:, 0:1] * atm
    tiles = jnp.concatenate(
        [field[:, c * LANE : (c + 1) * LANE] for c in range(cols // LANE)], axis=0
    ).astype(BF16)
    pieces = dot(pick_ref[...], tiles)
    blocks = pieces.shape[0]
    row = iota((CHUNK, LANE), 0)
    parts = []
    for n in range(blocks // CHUNK):
        piece = pieces[n * CHUNK : (n + 1) * CHUNK]
        spread = jnp.concatenate(
            [jnp.where(row == q, piece, 0.0) for q in range(CHUNK)], axis=1
        ).astype(BF16)
        weight = weight_ref[pl.ds(n * CHUNK, CHUNK)].reshape(CHUNK * LANE, LANE)
        parts.append(dot(spread, weight))
    contribution = jnp.concatenate(parts, axis=0).astype(BF16)
    at = iota((EDGE, LANE), 0)
    for t in range(ntiles):
        sent = dot(slots_ref[pl.ds(t * rows, rows), :], contribution)
        low = sent[main:]
        low = jnp.where(at == EDGE - 4, ids_ref[0, t : t + 1, :], low)
        low = jnp.where(at == EDGE - 3, ids_ref[1, t : t + 1, :], low)
        out_ref[pl.ds(t * rows, main), :] = sent[:main].astype(BF16)
        out_ref[pl.ds(t * rows + main, EDGE), :] = low.astype(BF16)


def reverse_lanes(x):
    tiles = x.shape[1] // LANE
    back = LANE - 1 - iota((x.shape[0], LANE), 1)
    parts = [
        jnp.take_along_axis(x[:, c * LANE : (c + 1) * LANE], back, axis=1) for c in range(tiles)
    ]
    return jnp.concatenate(parts[::-1], axis=1)


def free_ocean_kernel(
    ntiles, me_ref, ocean_ref, nu_ref, even_ref, odd_ref, atm_ref, out_ref, next_ref, work
):
    next_ref[...] = atm_ref[...]
    offset = atm_ref.shape[1]
    rows, cols = ocean_ref.shape
    me = me_ref[0]
    even, bottom, top = me % 2 == 0, me == 0, me == ntiles - 1
    ev, od = even_ref[:, offset:], odd_ref[:, offset:]
    size = rows + 8
    work[0:rows] = ocean_ref[...]
    work[rows:size] = jnp.zeros((8, cols), F32)
    work[size - 2 : size] = jnp.where(bottom, 0.0, jnp.where(even, od, ev))
    work[rows : rows + 2] = jnp.where(even, ev, od)
    nu = jnp.concatenate([nu_ref[c : c + 1] for c in range(cols // LANE)], axis=1)
    x = work[...]
    at = iota((size, cols), 0)
    for _ in range(2):
        folded = pltpu.roll(reverse_lanes(x[rows - 8 : rows]), 1, 0)
        tail = jnp.where(top & (iota((8, cols), 0) == 0), folded, x[rows:])
        x = jnp.concatenate([x[:rows], tail], axis=0)
        near = (
            pltpu.roll(x, 1, 0) + pltpu.roll(x, size - 1, 0)
            + pltpu.roll(x, 1, 1) + pltpu.roll(x, cols - 1, 1)
        )
        x = x + nu * (near - 4.0 * x)
        x = jnp.where(bottom & (at >= rows + 4), 0.0, x)
    out_ref[...] = x[:rows]


def drive_kernel(ntiles, main, rows, me_ref, arrived_ref, drive_ref, side_ref, keys_ref, pair_ref):
    per_lane = LANE // main
    step = main + EDGE
    total = drive_ref.shape[0]
    row_tiles = total // rows
    drive = jnp.zeros((total, LANE), F32)
    side = jnp.zeros((EDGE, LANE), F32)
    for g in range(ntiles // per_lane):
        edge = jnp.zeros((EDGE, LANE), F32)
        values = []
        for s in range(g * per_lane, (g + 1) * per_lane):
            values.append(arrived_ref[pl.ds(s * step, main), :])
            edge = edge + arrived_ref[pl.ds(s * step + main, EDGE), :].astype(F32)
        side = side + edge
        key = (edge[EDGE - 4 : EDGE - 3] - 1.0) * rows + edge[EDGE - 3 : EDGE - 2]
        key = key.astype(jnp.int32)
        keys_ref[g : g + 1] = key
        drive = drive + dot(
            onehot(key == iota((total, LANE), 0)), jnp.concatenate(values, axis=0)
        )
    side_ref[...] = side
    drive_ref[...] = drive
    even = me_ref[0] % 2 == 0
    pair_ref[...] = jnp.where(
        even,
        drive_ref[pl.ds(rows - 1, row_tiles, stride=rows), :],
        drive_ref[pl.ds(0, row_tiles, stride=rows), :],
    )


def ocean_kernel(
    ntiles, me_ref, drive_ref, side_ref, keys_ref, free_ref, nu_ref, value_ref, pick_ref
):
    rows, cols = free_ref.shape
    row_tiles = cols // LANE
    total = rows * row_tiles
    even, top = me_ref[0] % 2 == 0, me_ref[0] == ntiles - 1
    drive, side = drive_ref[...], side_ref[...]
    tile = lambda c: drive[c * rows : (c + 1) * rows]
    spun = [pltpu.roll(tile(c), 1, 1) for c in range(row_tiles)]
    back = [pltpu.roll(tile(c), LANE - 1, 1) for c in range(row_tiles)]
    lane, at = iota((rows, LANE), 1), iota((rows, LANE), 0)
    turned = LANE - 1 - iota((8, LANE), 1)
    for c in range(row_tiles):
        d = tile(c)
        left = jnp.where(lane == 0, spun[c - 1], spun[c])
        right = jnp.where(lane == LANE - 1, back[(c + 1) % row_tiles], back[c])
        under_row = jnp.where(even, side[c : c + 1], 0.0)
        under = jnp.where(at == 0, under_row, pltpu.roll(d, 1, 0))
        fold = jnp.take_along_axis(tile(row_tiles - 1 - c)[rows - 8 :], turned, axis=1)[7:8]
        over_row = jnp.where(top, fold, jnp.where(even, 0.0, side[c : c + 1]))
        over = jnp.where(at == rows - 1, over_row, pltpu.roll(d, rows - 1, 0))
        near = under + over + left + right
        value_ref[c * rows : (c + 1) * rows] = free_ref[:, c * LANE : (c + 1) * LANE] + (
            2.0 * d + nu_ref[c : c + 1] * (near - 4.0 * d)
        )
    for g in range(keys_ref.shape[0]):
        column = jnp.transpose(jnp.broadcast_to(keys_ref[g : g + 1], (LANE, LANE)))
        wide = jnp.concatenate([column] * -(-total // LANE), axis=1)[:, :total]
        pick_ref[pl.ds(g * LANE, LANE), :] = onehot(wide == iota((LANE, total), 1))


def return_kernel(rows, me_ref, value_ref, pick_ref, nu_ref, pair_ref, cells_ref, return_ref):
    row_tiles = nu_ref.shape[0]
    even = me_ref[0] % 2 == 0
    cells_ref[...] = value_ref[...]
    extra = nu_ref[...] * pair_ref[...]
    high, low = pl.ds(rows - 1, row_tiles, stride=rows), pl.ds(0, row_tiles, stride=rows)
    cells_ref[high, :] = cells_ref[high, :] + jnp.where(even, extra, 0.0)
    cells_ref[low, :] = cells_ref[low, :] + jnp.where(even, 0.0, extra)
    return_ref[...] = dot(pick_ref[...], cells_ref[...].astype(BF16)).astype(BF16)


def fetch_kernel(cells_ref, weight_hbm, next_ref, weight_ref, sems):
    copies = fetches(weight_hbm, 0, weight_ref, sems)
    for copy in copies:
        copy.start()
    rows = next_ref.shape[0]
    for c in range(next_ref.shape[1] // LANE):
        next_ref[:, c * LANE : (c + 1) * LANE] = cells_ref[c * rows : (c + 1) * rows]
    for copy in copies:
        copy.wait()


def backward_kernel(
    came_ref, keys_ref, early_ref, weight_hbm, out_ref, late_ref, sems
):
    early = early_ref.shape[0]
    copies = fetches(weight_hbm, early, late_ref, sems)
    for copy in copies:
        copy.start()
    values = dot(matches_lane(as_column(keys_ref[1]), came_ref.shape[0]), came_ref[...])
    blocks = values.shape[0]
    row = iota((CHUNK, LANE), 0)
    parts = []
    for n in range(blocks // CHUNK):
        value = values[n * CHUNK : (n + 1) * CHUNK].astype(BF16)
        at = n * CHUNK - early
        if at >= 0 and at % PIECE == 0:
            copies[at // PIECE].wait()
        held = early_ref[pl.ds(n * CHUNK, CHUNK)] if at < 0 else late_ref[pl.ds(at, CHUNK)]
        weight = held.reshape(CHUNK * LANE, LANE)
        full = dot_nt(value, weight)
        part = full[:, :LANE]
        for q in range(1, CHUNK):
            part = jnp.where(row == q, full[:, q * LANE : (q + 1) * LANE], part)
        parts.append(part)
    result = jnp.concatenate(parts, axis=0)
    coarse = result.astype(BF16)
    fine = (result - coarse.astype(F32)).astype(BF16)
    rows = out_ref.shape[0]
    total = rows * out_ref.shape[1] // LANE
    back = onehot(keys_ref[0] == iota((total, blocks), 0))
    tiles = dot(back, coarse) + dot(back, fine)
    for c in range(out_ref.shape[1] // LANE):
        out_ref[:, c * LANE : (c + 1) * LANE] = tiles[c * rows : (c + 1) * rows]


def call(kernel, outs, specs, cost, scratch=(), limit=24 << 20):
    run = pl.pallas_call(
        kernel,
        out_shape=outs,
        in_specs=specs,
        out_specs=jax.tree.map(lambda _: VMEM, outs),
        scratch_shapes=scratch,
        compiler_params=pltpu.CompilerParams(vmem_limit_bytes=limit),
        cost_estimate=pl.CostEstimate(flops=cost, bytes_accessed=cost // 64, transcendentals=0),
    )

    def placed(*args):
        return run(
            *[
                pltpu.with_memory_space_constraint(x, pltpu.HBM) if spec is HBM else x
                for x, spec in zip(args, specs)
            ]
        )

    return placed


def per_device(
    atm_state,
    atm_kappa,
    forcing,
    flux_gain,
    remap_weight,
    remap_source,
    remap_owner,
    remap_dest,
    ocean_state,
    ocean_nu,
    flux_coef,
):
    ntiles = lax.axis_size("tiles")
    me = lax.axis_index("tiles")
    blocks = remap_source.shape[0]
    capacity = max(2, 2 * blocks // ntiles)
    main = -(-capacity // 16) * 16
    rows = main + EDGE
    atm_rows, atm_cols = atm_state.shape
    ocean_rows, ocean_cols = ocean_state.shape
    atm_tiles = atm_rows * atm_cols // LANE
    row_tiles = ocean_cols // LANE
    shape = jax.ShapeDtypeStruct
    me_arr = me.astype(jnp.int32).reshape(1)
    edges = shape((2, atm_cols + ocean_cols), F32)
    atm, ocean, to_odd = call(
        send_kernel,
        (shape(atm_state.shape, F32), shape(ocean_state.shape, F32), edges),
        [SMEM, HBM, HBM],
        1 << 34,
        [pltpu.SemaphoreType.DMA((2,))],
    )(me_arr, atm_state, ocean_state)
    pairs = [(2 * k + 1, (2 * k + 2) % ntiles) for k in range(ntiles // 2)]
    from_odd = lax.ppermute(to_odd, "tiles", pairs + [(j, i) for i, j in pairs])
    atm_row_tiles = atm_cols // LANE
    early = min(EARLY, blocks)
    whole = blocks // PIECE
    nflux = forcing.shape[0]
    pick, keys, slots, ids, field, scale, kappa, nu, to_even = call(
        functools.partial(
            stage_kernel, ntiles, main, atm_rows, atm_row_tiles, ocean_rows, row_tiles
        ),
        (
            shape((blocks, atm_tiles), BF16),
            shape((2, 1, blocks), jnp.int32),
            shape((ntiles * rows, blocks), BF16),
            shape((2, ntiles, LANE), F32),
            shape(atm_state.shape, F32),
            shape((1, LANE), F32),
            shape((1, atm_cols), F32),
            shape((row_tiles, LANE), F32),
            edges,
        ),
        [SMEM, VMEM, VMEM] + [HBM] * 8,
        1 << 20,
        [
            pltpu.VMEM((3, 1, blocks), jnp.int32),
            pltpu.VMEM((2, 1, nflux), F32),
            pltpu.VMEM(forcing.shape, BF16),
            pltpu.SemaphoreType.DMA((8,)),
        ],
    )(
        me_arr,
        atm,
        ocean,
        remap_source.reshape(1, blocks),
        remap_owner.reshape(1, blocks),
        remap_dest.reshape(1, blocks),
        flux_gain.reshape(1, nflux),
        flux_coef.reshape(1, nflux),
        atm_kappa.reshape(1, atm_cols),
        ocean_nu.reshape(row_tiles, LANE),
        forcing,
    )
    from_even = lax.ppermute(to_even, "tiles", [(i, i ^ 1) for i in range(ntiles)])
    atm_next, outgoing = call(
        functools.partial(forward_kernel, ntiles, main),
        (shape(atm_state.shape, F32), shape((ntiles * rows, LANE), BF16)),
        [SMEM] + [VMEM] * 10,
        1 << 28,
        [pltpu.VMEM((2 * atm_rows, atm_cols), F32)],
    )(me_arr, atm, kappa, from_even, from_odd, field, scale, pick, slots, ids, remap_weight)
    arrived = lax.all_to_all(outgoing, "tiles", split_axis=0, concat_axis=0, tiled=True)
    free, atm_out = call(
        functools.partial(free_ocean_kernel, ntiles),
        (shape(ocean_state.shape, F32), shape(atm_state.shape, F32)),
        [SMEM] + [VMEM] * 5,
        1 << 27,
        [pltpu.VMEM((ocean_rows + 8, ocean_cols), F32)],
    )(me_arr, ocean, nu, from_even, from_odd, atm_next)
    total = ocean_rows * row_tiles
    drive, side, slot_keys, to_pair = call(
        functools.partial(drive_kernel, ntiles, main, ocean_rows),
        (
            shape((total, LANE), F32),
            shape((EDGE, LANE), F32),
            shape((ntiles * main // LANE, LANE), jnp.int32),
            shape((row_tiles, LANE), F32),
        ),
        [SMEM, VMEM],
        1 << 27,
    )(me_arr, arrived)
    from_pair = lax.ppermute(to_pair, "tiles", [(i, i ^ 1) for i in range(ntiles)])
    value, take = call(
        functools.partial(ocean_kernel, ntiles),
        (shape((total, LANE), F32), shape((ntiles * main, total), BF16)),
        [SMEM] + [VMEM] * 5,
        1 << 31,
    )(me_arr, drive, side, slot_keys, free, nu)
    cells, returned = call(
        functools.partial(return_kernel, ocean_rows),
        (shape((total, LANE), F32), shape((ntiles * main, LANE), BF16)),
        [SMEM] + [VMEM] * 4,
        1 << 27,
    )(me_arr, value, take, nu, from_pair)
    came_back = lax.all_to_all(returned, "tiles", split_axis=0, concat_axis=0, tiled=True)
    ocean_next, again = call(
        fetch_kernel,
        (shape(ocean_state.shape, F32), shape((early, LANE, LANE), BF16)),
        [VMEM, HBM],
        1 << 31,
        [pltpu.SemaphoreType.DMA((early // PIECE,))],
    )(cells, remap_weight)
    feedback = call(
        backward_kernel,
        shape(atm_state.shape, F32),
        [VMEM] * 3 + [HBM],
        1 << 28,
        [
            pltpu.VMEM((blocks - early, LANE, LANE), BF16),
            pltpu.SemaphoreType.DMA(((blocks - early) // PIECE,)),
        ],
    )(came_back, keys, again, remap_weight)
    return (atm_out, ocean_next, feedback)


def solution(mesh):
    return jax.shard_map(
        per_device,
        mesh=mesh,
        in_specs=(
            P(("members", "tiles"), None),
            P(),
            P(None, ("members", "tiles"), None),
            P(),
            P("tiles", None, None),
            P("tiles"),
            P("tiles", None),
            P("tiles"),
            P(("members", "tiles"), None),
            P(),
            P(),
        ),
        out_specs=(
            P(("members", "tiles"), None),
            P(("members", "tiles"), None),
            P(("members", "tiles"), None),
        ),
        check_vma=False,
    )
```

```python
import functools

import jax
import jax.numpy as jnp
from jax import lax
from jax.experimental import pallas as pl
from jax.experimental.pallas import tpu as pltpu
from jax.sharding import PartitionSpec as P

LANE = 128
EDGE = 32
CHUNK = 8
PIECE = 32
EARLY = 96
F32 = jnp.float32
BF16 = jnp.bfloat16
VMEM = pl.BlockSpec(memory_space=pltpu.VMEM)
SMEM = pl.BlockSpec(memory_space=pltpu.SMEM)
HBM = pl.BlockSpec(memory_space=pltpu.HBM)


def iota(shape, dim):
    return lax.broadcasted_iota(jnp.int32, shape, dim)


def dot(a, b):
    return lax.dot_general(a, b, (((1,), (0,)), ((), ())), preferred_element_type=F32)


def dot_nt(a, b):
    return lax.dot_general(a, b, (((1,), (1,)), ((), ())), preferred_element_type=F32)


def onehot(mask):
    return jnp.where(mask, 1.0, 0.0).astype(BF16)


def as_column(row):
    parts = [
        jnp.transpose(jnp.broadcast_to(row[:, k : k + LANE], (LANE, LANE)))
        for k in range(0, row.shape[1], LANE)
    ]
    return jnp.concatenate(parts, axis=0)


def matches_lane(column, width):
    parts = [
        onehot(column == iota(column.shape, 1) + k)[:, : min(LANE, width - k)]
        for k in range(0, width, LANE)
    ]
    return jnp.concatenate(parts, axis=1)


def fetches(weight_hbm, first, held, sems):
    copies = []
    for n in range(held.shape[0] // PIECE):
        copies.append(
            pltpu.make_async_copy(
                weight_hbm.at[pl.ds(first + n * PIECE, PIECE)],
                held.at[pl.ds(n * PIECE, PIECE)],
                sems.at[n],
            )
        )
    return copies


def edge_rows(upper, atm_ref, ocean_ref, out_ref):
    start = 0
    for ref in (atm_ref, ocean_ref):
        rows, cols = ref.shape
        first, last = ref[0:2], ref[rows - 2 : rows]
        out_ref[:, start : start + cols] = jnp.where(upper, last, first)
        start += cols


def send_kernel(me_ref, atm_hbm, ocean_hbm, atm_ref, ocean_ref, odd_ref, sems):
    copies = [
        pltpu.make_async_copy(atm_hbm, atm_ref, sems.at[0]),
        pltpu.make_async_copy(ocean_hbm, ocean_ref, sems.at[1]),
    ]
    for copy in copies:
        copy.start()
    for copy in copies:
        copy.wait()
    edge_rows(me_ref[0] % 2 == 1, atm_ref, ocean_ref, odd_ref)


def stage_kernel(
    ntiles, main, atm_rows, atm_row_tiles, ocean_rows, row_tiles,
    me_ref, atm_ref, ocean_ref, src_hbm, own_hbm, dst_hbm, gain_hbm, coef_hbm, kappa_hbm, nu_hbm, forcing_hbm,
    pick_ref, keys_ref, slots_ref, ids_ref, field_ref, scale_ref, kappa_ref, nu_ref,
    even_ref,
    ints, gains, forcing_ref, sems,
):
    small = [
        (src_hbm, ints.at[0]), (own_hbm, ints.at[1]), (dst_hbm, ints.at[2]),
        (gain_hbm, gains.at[0]), (coef_hbm, gains.at[1]), (forcing_hbm, forcing_ref),
        (kappa_hbm, kappa_ref), (nu_hbm, nu_ref),
    ]
    copies = [pltpu.make_async_copy(a, b, sems.at[k]) for k, (a, b) in enumerate(small)]
    for copy in copies:
        copy.start()
    edge_rows(me_ref[0] % 2 == 0, atm_ref, ocean_ref, even_ref)
    for copy in copies[:3]:
        copy.wait()
    rows = main + EDGE
    per_lane = LANE // main
    source, owner, dest = ints[0], ints[1], ints[2]
    blocks = owner.shape[1]
    source = (source % atm_row_tiles) * atm_rows + source // atm_row_tiles
    row_of, col_of = dest // row_tiles, dest % row_tiles
    match = owner == iota((ntiles, blocks), 0)
    above = onehot(iota((blocks, blocks), 0) < iota((blocks, blocks), 1))
    rank = jnp.sum(
        jnp.where(match, dot(onehot(match), above), 0.0), axis=0, keepdims=True
    ).astype(jnp.int32)
    pick_ref[...] = matches_lane(as_column(source), pick_ref.shape[1])
    keys_ref[0] = source
    keys_ref[1] = owner * main + rank
    odd = owner % 2 == 1
    own_slot = owner * rows + rank
    beside = jnp.where(
        odd,
        (row_of - (ocean_rows - 1)) + jnp.where(owner < ntiles - 1, 0, 1),
        row_of + jnp.where(owner > 0, 0, 1),
    )
    side_slot = jnp.where(odd, owner + 1, owner - 1) * rows + main + col_of
    side_slot = jnp.where(beside == 0, side_slot, -1)
    for t in range(ntiles):
        slot = iota((rows, blocks), 0) + t * rows
        slots_ref[pl.ds(t * rows, rows), :] = onehot((slot == own_slot) | (slot == side_slot))
    lane_of = rank + (me_ref[0] % per_lane) * main
    place = onehot(lane_of == iota((LANE, blocks), 0))
    ids_ref[0] = dot_nt(jnp.where(match, (col_of + 1).astype(F32), 0.0).astype(BF16), place)
    ids_ref[1] = dot_nt(jnp.where(match, row_of.astype(F32), 0.0).astype(BF16), place)
    for copy in copies[3 : len(small)]:
        copy.wait()
    coef = gains[1]
    scale_ref[...] = jnp.broadcast_to(
        jnp.sum(gains[0] * coef, axis=1, keepdims=True), scale_ref.shape
    )
    field = jnp.zeros(field_ref.shape, F32)
    for k in range(forcing_ref.shape[0]):
        field = field + coef[:, k : k + 1] * forcing_ref[k].astype(F32)
    field_ref[...] = field


def forward_kernel(
    ntiles, main, me_ref, atm_ref, kappa_ref, even_ref, odd_ref, field_ref, scale_ref,
    pick_ref, slots_ref, ids_ref, weight_ref, next_ref, out_ref, work,
):
    atm_rows, cols = atm_ref.shape
    rows = main + EDGE
    even = me_ref[0] % 2 == 0
    ev, od = even_ref[:, :cols], odd_ref[:, :cols]
    size = 2 * atm_rows
    work[0:atm_rows] = atm_ref[...]
    work[atm_rows : 2 * atm_rows] = jnp.zeros((atm_rows, cols), F32)
    work[size - 2 : size] = jnp.where(even, od, ev)
    work[atm_rows : atm_rows + 2] = jnp.where(even, ev, od)
    x = work[...]
    kappa = kappa_ref[...]
    for _ in range(2):
        near = (
            pltpu.roll(x, 1, 0) + pltpu.roll(x, size - 1, 0)
            + pltpu.roll(x, 1, 1) + pltpu.roll(x, cols - 1, 1)
        )
        x = x + kappa * (near - 4.0 * x)
    atm = x[:atm_rows]
    next_ref[...] = atm
    field = field_ref[...] + scale_ref[:, 0:1] * atm
    tiles = jnp.concatenate(
        [field[:, c * LANE : (c + 1) * LANE] for c in range(cols // LANE)], axis=0
    ).astype(BF16)
    pieces = dot(pick_ref[...], tiles)
    blocks = pieces.shape[0]
    row = iota((CHUNK, LANE), 0)
    parts = []
    for n in range(blocks // CHUNK):
        piece = pieces[n * CHUNK : (n + 1) * CHUNK]
        spread = jnp.concatenate(
            [jnp.where(row == q, piece, 0.0) for q in range(CHUNK)], axis=1
        ).astype(BF16)
        weight = weight_ref[pl.ds(n * CHUNK, CHUNK)].reshape(CHUNK * LANE, LANE)
        parts.append(dot(spread, weight))
    contribution = jnp.concatenate(parts, axis=0).astype(BF16)
    at = iota((EDGE, LANE), 0)
    for t in range(ntiles):
        sent = dot(slots_ref[pl.ds(t * rows, rows), :], contribution)
        low = sent[main:]
        low = jnp.where(at == EDGE - 4, ids_ref[0, t : t + 1, :], low)
        low = jnp.where(at == EDGE - 3, ids_ref[1, t : t + 1, :], low)
        out_ref[pl.ds(t * rows, main), :] = sent[:main].astype(BF16)
        out_ref[pl.ds(t * rows + main, EDGE), :] = low.astype(BF16)


def reverse_lanes(x):
    tiles = x.shape[1] // LANE
    back = LANE - 1 - iota((x.shape[0], LANE), 1)
    parts = [
        jnp.take_along_axis(x[:, c * LANE : (c + 1) * LANE], back, axis=1) for c in range(tiles)
    ]
    return jnp.concatenate(parts[::-1], axis=1)


def free_ocean(ntiles, me, ocean_ref, nu_ref, even_ref, odd_ref, work):
    rows, cols = ocean_ref.shape
    offset = even_ref.shape[1] - cols
    even, bottom, top = me % 2 == 0, me == 0, me == ntiles - 1
    ev, od = even_ref[:, offset:], odd_ref[:, offset:]
    size = rows + 8
    work[0:rows] = ocean_ref[...]
    work[rows:size] = jnp.zeros((8, cols), F32)
    work[size - 2 : size] = jnp.where(bottom, 0.0, jnp.where(even, od, ev))
    work[rows : rows + 2] = jnp.where(even, ev, od)
    nu = jnp.concatenate([nu_ref[c : c + 1] for c in range(cols // LANE)], axis=1)
    x = work[...]
    at = iota((size, cols), 0)
    for _ in range(2):
        folded = pltpu.roll(reverse_lanes(x[rows - 8 : rows]), 1, 0)
        tail = jnp.where(top & (iota((8, cols), 0) == 0), folded, x[rows:])
        x = jnp.concatenate([x[:rows], tail], axis=0)
        near = (
            pltpu.roll(x, 1, 0) + pltpu.roll(x, size - 1, 0)
            + pltpu.roll(x, 1, 1) + pltpu.roll(x, cols - 1, 1)
        )
        x = x + nu * (near - 4.0 * x)
        x = jnp.where(bottom & (at >= rows + 4), 0.0, x)
    return x[:rows]


def drive_kernel(ntiles, main, rows, me_ref, arrived_ref, drive_ref, side_ref, keys_ref, pair_ref):
    per_lane = LANE // main
    step = main + EDGE
    total = drive_ref.shape[0]
    row_tiles = total // rows
    drive = jnp.zeros((total, LANE), F32)
    side = jnp.zeros((EDGE, LANE), F32)
    for g in range(ntiles // per_lane):
        edge = jnp.zeros((EDGE, LANE), F32)
        values = []
        for s in range(g * per_lane, (g + 1) * per_lane):
            values.append(arrived_ref[pl.ds(s * step, main), :])
            edge = edge + arrived_ref[pl.ds(s * step + main, EDGE), :].astype(F32)
        side = side + edge
        key = (edge[EDGE - 4 : EDGE - 3] - 1.0) * rows + edge[EDGE - 3 : EDGE - 2]
        key = key.astype(jnp.int32)
        keys_ref[g : g + 1] = key
        drive = drive + dot(
            onehot(key == iota((total, LANE), 0)), jnp.concatenate(values, axis=0)
        )
    side_ref[...] = side
    drive_ref[...] = drive
    even = me_ref[0] % 2 == 0
    pair_ref[...] = jnp.where(
        even,
        drive_ref[pl.ds(rows - 1, row_tiles, stride=rows), :],
        drive_ref[pl.ds(0, row_tiles, stride=rows), :],
    )


def ocean_kernel(
    ntiles, me_ref, drive_ref, side_ref, keys_ref, ocean_ref, nu_ref, even_ref, odd_ref,
    value_ref, pick_ref, work,
):
    rows, cols = ocean_ref.shape
    free = free_ocean(ntiles, me_ref[0], ocean_ref, nu_ref, even_ref, odd_ref, work)
    row_tiles = cols // LANE
    total = rows * row_tiles
    even, top = me_ref[0] % 2 == 0, me_ref[0] == ntiles - 1
    drive, side = drive_ref[...], side_ref[...]
    tile = lambda c: drive[c * rows : (c + 1) * rows]
    spun = [pltpu.roll(tile(c), 1, 1) for c in range(row_tiles)]
    back = [pltpu.roll(tile(c), LANE - 1, 1) for c in range(row_tiles)]
    lane, at = iota((rows, LANE), 1), iota((rows, LANE), 0)
    turned = LANE - 1 - iota((8, LANE), 1)
    for c in range(row_tiles):
        d = tile(c)
        left = jnp.where(lane == 0, spun[c - 1], spun[c])
        right = jnp.where(lane == LANE - 1, back[(c + 1) % row_tiles], back[c])
        under_row = jnp.where(even, side[c : c + 1], 0.0)
        under = jnp.where(at == 0, under_row, pltpu.roll(d, 1, 0))
        fold = jnp.take_along_axis(tile(row_tiles - 1 - c)[rows - 8 :], turned, axis=1)[7:8]
        over_row = jnp.where(top, fold, jnp.where(even, 0.0, side[c : c + 1]))
        over = jnp.where(at == rows - 1, over_row, pltpu.roll(d, rows - 1, 0))
        near = under + over + left + right
        value_ref[c * rows : (c + 1) * rows] = free[:, c * LANE : (c + 1) * LANE] + (
            2.0 * d + nu_ref[c : c + 1] * (near - 4.0 * d)
        )
    for g in range(keys_ref.shape[0]):
        column = jnp.transpose(jnp.broadcast_to(keys_ref[g : g + 1], (LANE, LANE)))
        wide = jnp.concatenate([column] * -(-total // LANE), axis=1)[:, :total]
        pick_ref[pl.ds(g * LANE, LANE), :] = onehot(wide == iota((LANE, total), 1))


def return_kernel(rows, me_ref, value_ref, pick_ref, nu_ref, pair_ref, cells_ref, return_ref):
    row_tiles = nu_ref.shape[0]
    even = me_ref[0] % 2 == 0
    cells_ref[...] = value_ref[...]
    extra = nu_ref[...] * pair_ref[...]
    high, low = pl.ds(rows - 1, row_tiles, stride=rows), pl.ds(0, row_tiles, stride=rows)
    cells_ref[high, :] = cells_ref[high, :] + jnp.where(even, extra, 0.0)
    cells_ref[low, :] = cells_ref[low, :] + jnp.where(even, 0.0, extra)
    return_ref[...] = dot(pick_ref[...], cells_ref[...].astype(BF16)).astype(BF16)


def fetch_kernel(cells_ref, atm_ref, weight_hbm, next_ref, atm_out, weight_ref, sems):
    atm_out[...] = atm_ref[...]
    copies = fetches(weight_hbm, 0, weight_ref, sems)
    for copy in copies:
        copy.start()
    rows = next_ref.shape[0]
    for c in range(next_ref.shape[1] // LANE):
        next_ref[:, c * LANE : (c + 1) * LANE] = cells_ref[c * rows : (c + 1) * rows]
    for copy in copies:
        copy.wait()


def backward_kernel(
    came_ref, keys_ref, early_ref, weight_hbm, out_ref, late_ref, sems
):
    early = early_ref.shape[0]
    copies = fetches(weight_hbm, early, late_ref, sems)
    for copy in copies:
        copy.start()
    values = dot(matches_lane(as_column(keys_ref[1]), came_ref.shape[0]), came_ref[...])
    blocks = values.shape[0]
    row = iota((CHUNK, LANE), 0)
    parts = []
    for n in range(blocks // CHUNK):
        value = values[n * CHUNK : (n + 1) * CHUNK].astype(BF16)
        at = n * CHUNK - early
        if at >= 0 and at % PIECE == 0:
            copies[at // PIECE].wait()
        held = early_ref[pl.ds(n * CHUNK, CHUNK)] if at < 0 else late_ref[pl.ds(at, CHUNK)]
        weight = held.reshape(CHUNK * LANE, LANE)
        full = dot_nt(value, weight)
        part = full[:, :LANE]
        for q in range(1, CHUNK):
            part = jnp.where(row == q, full[:, q * LANE : (q + 1) * LANE], part)
        parts.append(part)
    result = jnp.concatenate(parts, axis=0)
    coarse = result.astype(BF16)
    fine = (result - coarse.astype(F32)).astype(BF16)
    rows = out_ref.shape[0]
    total = rows * out_ref.shape[1] // LANE
    back = onehot(keys_ref[0] == iota((total, blocks), 0))
    tiles = dot(back, coarse) + dot(back, fine)
    for c in range(out_ref.shape[1] // LANE):
        out_ref[:, c * LANE : (c + 1) * LANE] = tiles[c * rows : (c + 1) * rows]


def call(kernel, outs, specs, cost, scratch=(), limit=24 << 20):
    run = pl.pallas_call(
        kernel,
        out_shape=outs,
        in_specs=specs,
        out_specs=jax.tree.map(lambda _: VMEM, outs),
        scratch_shapes=scratch,
        compiler_params=pltpu.CompilerParams(vmem_limit_bytes=limit),
        cost_estimate=pl.CostEstimate(flops=cost, bytes_accessed=cost // 64, transcendentals=0),
    )

    def placed(*args):
        return run(
            *[
                pltpu.with_memory_space_constraint(x, pltpu.HBM) if spec is HBM else x
                for x, spec in zip(args, specs)
            ]
        )

    return placed


def per_device(
    atm_state,
    atm_kappa,
    forcing,
    flux_gain,
    remap_weight,
    remap_source,
    remap_owner,
    remap_dest,
    ocean_state,
    ocean_nu,
    flux_coef,
):
    ntiles = lax.axis_size("tiles")
    me = lax.axis_index("tiles")
    blocks = remap_source.shape[0]
    capacity = max(2, 2 * blocks // ntiles)
    main = -(-capacity // 16) * 16
    rows = main + EDGE
    atm_rows, atm_cols = atm_state.shape
    ocean_rows, ocean_cols = ocean_state.shape
    atm_tiles = atm_rows * atm_cols // LANE
    row_tiles = ocean_cols // LANE
    shape = jax.ShapeDtypeStruct
    me_arr = me.astype(jnp.int32).reshape(1)
    edges = shape((2, atm_cols + ocean_cols), F32)
    atm, ocean, to_odd = call(
        send_kernel,
        (shape(atm_state.shape, F32), shape(ocean_state.shape, F32), edges),
        [SMEM, HBM, HBM],
        1 << 34,
        [pltpu.SemaphoreType.DMA((2,))],
    )(me_arr, atm_state, ocean_state)
    pairs = [(2 * k + 1, (2 * k + 2) % ntiles) for k in range(ntiles // 2)]
    from_odd = lax.ppermute(to_odd, "tiles", pairs + [(j, i) for i, j in pairs])
    atm_row_tiles = atm_cols // LANE
    early = min(EARLY, blocks)
    whole = blocks // PIECE
    nflux = forcing.shape[0]
    pick, keys, slots, ids, field, scale, kappa, nu, to_even = call(
        functools.partial(
            stage_kernel, ntiles, main, atm_rows, atm_row_tiles, ocean_rows, row_tiles
        ),
        (
            shape((blocks, atm_tiles), BF16),
            shape((2, 1, blocks), jnp.int32),
            shape((ntiles * rows, blocks), BF16),
            shape((2, ntiles, LANE), F32),
            shape(atm_state.shape, F32),
            shape((1, LANE), F32),
            shape((1, atm_cols), F32),
            shape((row_tiles, LANE), F32),
            edges,
        ),
        [SMEM, VMEM, VMEM] + [HBM] * 8,
        1 << 20,
        [
            pltpu.VMEM((3, 1, blocks), jnp.int32),
            pltpu.VMEM((2, 1, nflux), F32),
            pltpu.VMEM(forcing.shape, BF16),
            pltpu.SemaphoreType.DMA((8,)),
        ],
    )(
        me_arr,
        atm,
        ocean,
        remap_source.reshape(1, blocks),
        remap_owner.reshape(1, blocks),
        remap_dest.reshape(1, blocks),
        flux_gain.reshape(1, nflux),
        flux_coef.reshape(1, nflux),
        atm_kappa.reshape(1, atm_cols),
        ocean_nu.reshape(row_tiles, LANE),
        forcing,
    )
    from_even = lax.ppermute(to_even, "tiles", [(i, i ^ 1) for i in range(ntiles)])
    atm_next, outgoing = call(
        functools.partial(forward_kernel, ntiles, main),
        (shape(atm_state.shape, F32), shape((ntiles * rows, LANE), BF16)),
        [SMEM] + [VMEM] * 10,
        1 << 28,
        [pltpu.VMEM((2 * atm_rows, atm_cols), F32)],
    )(me_arr, atm, kappa, from_even, from_odd, field, scale, pick, slots, ids, remap_weight)
    arrived = lax.all_to_all(outgoing, "tiles", split_axis=0, concat_axis=0, tiled=True)
    total = ocean_rows * row_tiles
    drive, side, slot_keys, to_pair = call(
        functools.partial(drive_kernel, ntiles, main, ocean_rows),
        (
            shape((total, LANE), F32),
            shape((EDGE, LANE), F32),
            shape((ntiles * main // LANE, LANE), jnp.int32),
            shape((row_tiles, LANE), F32),
        ),
        [SMEM, VMEM],
        1 << 27,
    )(me_arr, arrived)
    from_pair = lax.ppermute(to_pair, "tiles", [(i, i ^ 1) for i in range(ntiles)])
    value, take = call(
        functools.partial(ocean_kernel, ntiles),
        (shape((total, LANE), F32), shape((ntiles * main, total), BF16)),
        [SMEM] + [VMEM] * 7,
        1 << 31,
        [pltpu.VMEM((ocean_rows + 8, ocean_cols), F32)],
    )(me_arr, drive, side, slot_keys, ocean, nu, from_even, from_odd)
    cells, returned = call(
        functools.partial(return_kernel, ocean_rows),
        (shape((total, LANE), F32), shape((ntiles * main, LANE), BF16)),
        [SMEM] + [VMEM] * 4,
        1 << 27,
    )(me_arr, value, take, nu, from_pair)
    came_back = lax.all_to_all(returned, "tiles", split_axis=0, concat_axis=0, tiled=True)
    ocean_next, atm_out, again = call(
        fetch_kernel,
        (
            shape(ocean_state.shape, F32),
            shape(atm_state.shape, F32),
            shape((early, LANE, LANE), BF16),
        ),
        [VMEM, VMEM, HBM],
        1 << 31,
        [pltpu.SemaphoreType.DMA((early // PIECE,))],
    )(cells, atm_next, remap_weight)
    feedback = call(
        backward_kernel,
        shape(atm_state.shape, F32),
        [VMEM] * 3 + [HBM],
        1 << 28,
        [
            pltpu.VMEM((blocks - early, LANE, LANE), BF16),
            pltpu.SemaphoreType.DMA(((blocks - early) // PIECE,)),
        ],
    )(came_back, keys, again, remap_weight)
    return (atm_out, ocean_next, feedback)


def solution(mesh):
    return jax.shard_map(
        per_device,
        mesh=mesh,
        in_specs=(
            P(("members", "tiles"), None),
            P(),
            P(None, ("members", "tiles"), None),
            P(),
            P("tiles", None, None),
            P("tiles"),
            P("tiles", None),
            P("tiles"),
            P(("members", "tiles"), None),
            P(),
            P(),
        ),
        out_specs=(
            P(("members", "tiles"), None),
            P(("members", "tiles"), None),
            P(("members", "tiles"), None),
        ),
        check_vma=False,
    )
```

```python
import functools

import jax
import jax.numpy as jnp
from jax import lax
from jax.experimental import pallas as pl
from jax.experimental.pallas import tpu as pltpu
from jax.sharding import PartitionSpec as P

LANE = 128
EDGE = 32
CHUNK = 8
PIECE = 32
EARLY = 64
F32 = jnp.float32
BF16 = jnp.bfloat16
VMEM = pl.BlockSpec(memory_space=pltpu.VMEM)
SMEM = pl.BlockSpec(memory_space=pltpu.SMEM)
HBM = pl.BlockSpec(memory_space=pltpu.HBM)


def iota(shape, dim):
    return lax.broadcasted_iota(jnp.int32, shape, dim)


def dot(a, b):
    return lax.dot_general(a, b, (((1,), (0,)), ((), ())), preferred_element_type=F32)


def dot_nt(a, b):
    return lax.dot_general(a, b, (((1,), (1,)), ((), ())), preferred_element_type=F32)


def onehot(mask):
    return jnp.where(mask, 1.0, 0.0).astype(BF16)


def as_column(row):
    parts = [
        jnp.transpose(jnp.broadcast_to(row[:, k : k + LANE], (LANE, LANE)))
        for k in range(0, row.shape[1], LANE)
    ]
    return jnp.concatenate(parts, axis=0)


def matches_lane(column, width):
    parts = [
        onehot(column == iota(column.shape, 1) + k)[:, : min(LANE, width - k)]
        for k in range(0, width, LANE)
    ]
    return jnp.concatenate(parts, axis=1)


def fetches(weight_hbm, first, held, sems):
    copies = []
    for n in range(held.shape[0] // PIECE):
        copies.append(
            pltpu.make_async_copy(
                weight_hbm.at[pl.ds(first + n * PIECE, PIECE)],
                held.at[pl.ds(n * PIECE, PIECE)],
                sems.at[n],
            )
        )
    return copies


def edge_rows(upper, atm_ref, ocean_ref, out_ref):
    start = 0
    for ref in (atm_ref, ocean_ref):
        rows, cols = ref.shape
        first, last = ref[0:2], ref[rows - 2 : rows]
        out_ref[:, start : start + cols] = jnp.where(upper, last, first)
        start += cols


def send_kernel(me_ref, atm_hbm, ocean_hbm, atm_ref, ocean_ref, odd_ref, sems):
    copies = [
        pltpu.make_async_copy(atm_hbm, atm_ref, sems.at[0]),
        pltpu.make_async_copy(ocean_hbm, ocean_ref, sems.at[1]),
    ]
    for copy in copies:
        copy.start()
    for copy in copies:
        copy.wait()
    edge_rows(me_ref[0] % 2 == 1, atm_ref, ocean_ref, odd_ref)


def stage_kernel(
    ntiles, main, atm_rows, atm_row_tiles, ocean_rows, row_tiles,
    me_ref, atm_ref, ocean_ref, src_hbm, own_hbm, dst_hbm, gain_hbm, coef_hbm, kappa_hbm, nu_hbm, forcing_hbm,
    weight_hbm, pick_ref, keys_ref, slots_ref, ids_ref, field_ref, scale_ref, kappa_ref, nu_ref,
    even_ref, early_ref,
    ints, gains, forcing_ref, sems, early_sems,
):
    small = [
        (src_hbm, ints.at[0]), (own_hbm, ints.at[1]), (dst_hbm, ints.at[2]),
        (gain_hbm, gains.at[0]), (coef_hbm, gains.at[1]), (forcing_hbm, forcing_ref),
        (kappa_hbm, kappa_ref), (nu_hbm, nu_ref),
    ]
    copies = [pltpu.make_async_copy(a, b, sems.at[k]) for k, (a, b) in enumerate(small)]
    weights = fetches(weight_hbm, 0, early_ref, early_sems)
    for copy in copies + weights:
        copy.start()
    edge_rows(me_ref[0] % 2 == 0, atm_ref, ocean_ref, even_ref)
    for copy in copies[:3]:
        copy.wait()
    rows = main + EDGE
    per_lane = LANE // main
    source, owner, dest = ints[0], ints[1], ints[2]
    blocks = owner.shape[1]
    source = (source % atm_row_tiles) * atm_rows + source // atm_row_tiles
    row_of, col_of = dest // row_tiles, dest % row_tiles
    match = owner == iota((ntiles, blocks), 0)
    above = onehot(iota((blocks, blocks), 0) < iota((blocks, blocks), 1))
    rank = jnp.sum(
        jnp.where(match, dot(onehot(match), above), 0.0), axis=0, keepdims=True
    ).astype(jnp.int32)
    pick_ref[...] = matches_lane(as_column(source), pick_ref.shape[1])
    keys_ref[0] = source
    keys_ref[1] = owner * main + rank
    odd = owner % 2 == 1
    own_slot = owner * rows + rank
    beside = jnp.where(
        odd,
        (row_of - (ocean_rows - 1)) + jnp.where(owner < ntiles - 1, 0, 1),
        row_of + jnp.where(owner > 0, 0, 1),
    )
    side_slot = jnp.where(odd, owner + 1, owner - 1) * rows + main + col_of
    side_slot = jnp.where(beside == 0, side_slot, -1)
    for t in range(ntiles):
        slot = iota((rows, blocks), 0) + t * rows
        slots_ref[pl.ds(t * rows, rows), :] = onehot((slot == own_slot) | (slot == side_slot))
    lane_of = rank + (me_ref[0] % per_lane) * main
    place = onehot(lane_of == iota((LANE, blocks), 0))
    ids_ref[0] = dot_nt(jnp.where(match, (col_of + 1).astype(F32), 0.0).astype(BF16), place)
    ids_ref[1] = dot_nt(jnp.where(match, row_of.astype(F32), 0.0).astype(BF16), place)
    for copy in copies[3 : len(small)]:
        copy.wait()
    coef = gains[1]
    scale_ref[...] = jnp.broadcast_to(
        jnp.sum(gains[0] * coef, axis=1, keepdims=True), scale_ref.shape
    )
    field = jnp.zeros(field_ref.shape, F32)
    for k in range(forcing_ref.shape[0]):
        field = field + coef[:, k : k + 1] * forcing_ref[k].astype(F32)
    field_ref[...] = field
    for copy in weights:
        copy.wait()


def forward_kernel(
    ntiles, main, me_ref, atm_ref, kappa_ref, even_ref, odd_ref, field_ref, scale_ref,
    pick_ref, slots_ref, ids_ref, early_ref, weight_ref, next_ref, out_ref, work,
):
    atm_rows, cols = atm_ref.shape
    rows = main + EDGE
    even = me_ref[0] % 2 == 0
    ev, od = even_ref[:, :cols], odd_ref[:, :cols]
    size = 2 * atm_rows
    work[0:atm_rows] = atm_ref[...]
    work[atm_rows : 2 * atm_rows] = jnp.zeros((atm_rows, cols), F32)
    work[size - 2 : size] = jnp.where(even, od, ev)
    work[atm_rows : atm_rows + 2] = jnp.where(even, ev, od)
    x = work[...]
    kappa = kappa_ref[...]
    for _ in range(2):
        near = (
            pltpu.roll(x, 1, 0) + pltpu.roll(x, size - 1, 0)
            + pltpu.roll(x, 1, 1) + pltpu.roll(x, cols - 1, 1)
        )
        x = x + kappa * (near - 4.0 * x)
    atm = x[:atm_rows]
    next_ref[...] = atm
    field = field_ref[...] + scale_ref[:, 0:1] * atm
    tiles = jnp.concatenate(
        [field[:, c * LANE : (c + 1) * LANE] for c in range(cols // LANE)], axis=0
    ).astype(BF16)
    pieces = dot(pick_ref[...], tiles)
    blocks = pieces.shape[0]
    row = iota((CHUNK, LANE), 0)
    parts = []
    for n in range(blocks // CHUNK):
        piece = pieces[n * CHUNK : (n + 1) * CHUNK]
        spread = jnp.concatenate(
            [jnp.where(row == q, piece, 0.0) for q in range(CHUNK)], axis=1
        ).astype(BF16)
        held = early_ref if n * CHUNK < early_ref.shape[0] else weight_ref
        weight = held[pl.ds(n * CHUNK, CHUNK)].reshape(CHUNK * LANE, LANE)
        parts.append(dot(spread, weight))
    contribution = jnp.concatenate(parts, axis=0).astype(BF16)
    at = iota((EDGE, LANE), 0)
    for t in range(ntiles):
        sent = dot(slots_ref[pl.ds(t * rows, rows), :], contribution)
        low = sent[main:]
        low = jnp.where(at == EDGE - 4, ids_ref[0, t : t + 1, :], low)
        low = jnp.where(at == EDGE - 3, ids_ref[1, t : t + 1, :], low)
        out_ref[pl.ds(t * rows, main), :] = sent[:main].astype(BF16)
        out_ref[pl.ds(t * rows + main, EDGE), :] = low.astype(BF16)


def reverse_lanes(x):
    tiles = x.shape[1] // LANE
    back = LANE - 1 - iota((x.shape[0], LANE), 1)
    parts = [
        jnp.take_along_axis(x[:, c * LANE : (c + 1) * LANE], back, axis=1) for c in range(tiles)
    ]
    return jnp.concatenate(parts[::-1], axis=1)


def free_ocean(ntiles, me, ocean_ref, nu_ref, even_ref, odd_ref, work):
    rows, cols = ocean_ref.shape
    offset = even_ref.shape[1] - cols
    even, bottom, top = me % 2 == 0, me == 0, me == ntiles - 1
    ev, od = even_ref[:, offset:], odd_ref[:, offset:]
    size = rows + 8
    work[0:rows] = ocean_ref[...]
    work[rows:size] = jnp.zeros((8, cols), F32)
    work[size - 2 : size] = jnp.where(bottom, 0.0, jnp.where(even, od, ev))
    work[rows : rows + 2] = jnp.where(even, ev, od)
    nu = jnp.concatenate([nu_ref[c : c + 1] for c in range(cols // LANE)], axis=1)
    x = work[...]
    at = iota((size, cols), 0)
    for _ in range(2):
        folded = pltpu.roll(reverse_lanes(x[rows - 8 : rows]), 1, 0)
        tail = jnp.where(top & (iota((8, cols), 0) == 0), folded, x[rows:])
        x = jnp.concatenate([x[:rows], tail], axis=0)
        near = (
            pltpu.roll(x, 1, 0) + pltpu.roll(x, size - 1, 0)
            + pltpu.roll(x, 1, 1) + pltpu.roll(x, cols - 1, 1)
        )
        x = x + nu * (near - 4.0 * x)
        x = jnp.where(bottom & (at >= rows + 4), 0.0, x)
    return x[:rows]


def drive_kernel(ntiles, main, rows, me_ref, arrived_ref, drive_ref, side_ref, keys_ref, pair_ref):
    per_lane = LANE // main
    step = main + EDGE
    total = drive_ref.shape[0]
    row_tiles = total // rows
    drive = jnp.zeros((total, LANE), F32)
    side = jnp.zeros((EDGE, LANE), F32)
    for g in range(ntiles // per_lane):
        edge = jnp.zeros((EDGE, LANE), F32)
        values = []
        for s in range(g * per_lane, (g + 1) * per_lane):
            values.append(arrived_ref[pl.ds(s * step, main), :])
            edge = edge + arrived_ref[pl.ds(s * step + main, EDGE), :].astype(F32)
        side = side + edge
        key = (edge[EDGE - 4 : EDGE - 3] - 1.0) * rows + edge[EDGE - 3 : EDGE - 2]
        key = key.astype(jnp.int32)
        keys_ref[g : g + 1] = key
        drive = drive + dot(
            onehot(key == iota((total, LANE), 0)), jnp.concatenate(values, axis=0)
        )
    side_ref[...] = side
    drive_ref[...] = drive
    even = me_ref[0] % 2 == 0
    pair_ref[...] = jnp.where(
        even,
        drive_ref[pl.ds(rows - 1, row_tiles, stride=rows), :],
        drive_ref[pl.ds(0, row_tiles, stride=rows), :],
    )


def ocean_kernel(
    ntiles, me_ref, drive_ref, side_ref, keys_ref, ocean_ref, nu_ref, even_ref, odd_ref,
    value_ref, pick_ref, work,
):
    rows, cols = ocean_ref.shape
    free = free_ocean(ntiles, me_ref[0], ocean_ref, nu_ref, even_ref, odd_ref, work)
    row_tiles = cols // LANE
    total = rows * row_tiles
    even, top = me_ref[0] % 2 == 0, me_ref[0] == ntiles - 1
    drive, side = drive_ref[...], side_ref[...]
    tile = lambda c: drive[c * rows : (c + 1) * rows]
    spun = [pltpu.roll(tile(c), 1, 1) for c in range(row_tiles)]
    back = [pltpu.roll(tile(c), LANE - 1, 1) for c in range(row_tiles)]
    lane, at = iota((rows, LANE), 1), iota((rows, LANE), 0)
    turned = LANE - 1 - iota((8, LANE), 1)
    for c in range(row_tiles):
        d = tile(c)
        left = jnp.where(lane == 0, spun[c - 1], spun[c])
        right = jnp.where(lane == LANE - 1, back[(c + 1) % row_tiles], back[c])
        under_row = jnp.where(even, side[c : c + 1], 0.0)
        under = jnp.where(at == 0, under_row, pltpu.roll(d, 1, 0))
        fold = jnp.take_along_axis(tile(row_tiles - 1 - c)[rows - 8 :], turned, axis=1)[7:8]
        over_row = jnp.where(top, fold, jnp.where(even, 0.0, side[c : c + 1]))
        over = jnp.where(at == rows - 1, over_row, pltpu.roll(d, rows - 1, 0))
        near = under + over + left + right
        value_ref[c * rows : (c + 1) * rows] = free[:, c * LANE : (c + 1) * LANE] + (
            2.0 * d + nu_ref[c : c + 1] * (near - 4.0 * d)
        )
    for g in range(keys_ref.shape[0]):
        column = jnp.transpose(jnp.broadcast_to(keys_ref[g : g + 1], (LANE, LANE)))
        wide = jnp.concatenate([column] * -(-total // LANE), axis=1)[:, :total]
        pick_ref[pl.ds(g * LANE, LANE), :] = onehot(wide == iota((LANE, total), 1))


def return_kernel(rows, me_ref, value_ref, pick_ref, nu_ref, pair_ref, cells_ref, return_ref):
    row_tiles = nu_ref.shape[0]
    even = me_ref[0] % 2 == 0
    cells_ref[...] = value_ref[...]
    extra = nu_ref[...] * pair_ref[...]
    high, low = pl.ds(rows - 1, row_tiles, stride=rows), pl.ds(0, row_tiles, stride=rows)
    cells_ref[high, :] = cells_ref[high, :] + jnp.where(even, extra, 0.0)
    cells_ref[low, :] = cells_ref[low, :] + jnp.where(even, 0.0, extra)
    return_ref[...] = dot(pick_ref[...], cells_ref[...].astype(BF16)).astype(BF16)


def backward_kernel(
    came_ref, keys_ref, early_ref, cells_ref, atm_ref, weight_hbm,
    out_ref, next_hbm, atm_hbm, late_ref, next_ref, sems, out_sems,
):
    early = early_ref.shape[0]
    copies = fetches(weight_hbm, early, late_ref, sems)
    for copy in copies:
        copy.start()
    rows = next_ref.shape[0]
    for c in range(next_ref.shape[1] // LANE):
        next_ref[:, c * LANE : (c + 1) * LANE] = cells_ref[c * rows : (c + 1) * rows]
    written = [
        pltpu.make_async_copy(atm_ref, atm_hbm, out_sems.at[0]),
        pltpu.make_async_copy(next_ref, next_hbm, out_sems.at[1]),
    ]
    for copy in written:
        copy.start()
    values = dot(matches_lane(as_column(keys_ref[1]), came_ref.shape[0]), came_ref[...])
    blocks = values.shape[0]
    row = iota((CHUNK, LANE), 0)
    parts = []
    for n in range(blocks // CHUNK):
        value = values[n * CHUNK : (n + 1) * CHUNK].astype(BF16)
        at = n * CHUNK - early
        if at >= 0 and at % PIECE == 0:
            copies[at // PIECE].wait()
        held = early_ref[pl.ds(n * CHUNK, CHUNK)] if at < 0 else late_ref[pl.ds(at, CHUNK)]
        weight = held.reshape(CHUNK * LANE, LANE)
        full = dot_nt(value, weight)
        part = full[:, :LANE]
        for q in range(1, CHUNK):
            part = jnp.where(row == q, full[:, q * LANE : (q + 1) * LANE], part)
        parts.append(part)
    result = jnp.concatenate(parts, axis=0)
    coarse = result.astype(BF16)
    fine = (result - coarse.astype(F32)).astype(BF16)
    rows = out_ref.shape[0]
    total = rows * out_ref.shape[1] // LANE
    back = onehot(keys_ref[0] == iota((total, blocks), 0))
    tiles = dot(back, coarse) + dot(back, fine)
    for c in range(out_ref.shape[1] // LANE):
        out_ref[:, c * LANE : (c + 1) * LANE] = tiles[c * rows : (c + 1) * rows]
    for copy in written:
        copy.wait()


def call(kernel, outs, specs, cost, scratch=(), limit=24 << 20, out_specs=None):
    run = pl.pallas_call(
        kernel,
        out_shape=outs,
        in_specs=specs,
        out_specs=out_specs or jax.tree.map(lambda _: VMEM, outs),
        scratch_shapes=scratch,
        compiler_params=pltpu.CompilerParams(vmem_limit_bytes=limit),
        cost_estimate=pl.CostEstimate(flops=cost, bytes_accessed=cost // 64, transcendentals=0),
    )

    def placed(*args):
        return run(
            *[
                pltpu.with_memory_space_constraint(x, pltpu.HBM) if spec is HBM else x
                for x, spec in zip(args, specs)
            ]
        )

    return placed


def per_device(
    atm_state,
    atm_kappa,
    forcing,
    flux_gain,
    remap_weight,
    remap_source,
    remap_owner,
    remap_dest,
    ocean_state,
    ocean_nu,
    flux_coef,
):
    ntiles = lax.axis_size("tiles")
    me = lax.axis_index("tiles")
    blocks = remap_source.shape[0]
    capacity = max(2, 2 * blocks // ntiles)
    main = -(-capacity // 16) * 16
    rows = main + EDGE
    atm_rows, atm_cols = atm_state.shape
    ocean_rows, ocean_cols = ocean_state.shape
    atm_tiles = atm_rows * atm_cols // LANE
    row_tiles = ocean_cols // LANE
    shape = jax.ShapeDtypeStruct
    me_arr = me.astype(jnp.int32).reshape(1)
    edges = shape((2, atm_cols + ocean_cols), F32)
    atm, ocean, to_odd = call(
        send_kernel,
        (shape(atm_state.shape, F32), shape(ocean_state.shape, F32), edges),
        [SMEM, HBM, HBM],
        1 << 34,
        [pltpu.SemaphoreType.DMA((2,))],
    )(me_arr, atm_state, ocean_state)
    pairs = [(2 * k + 1, (2 * k + 2) % ntiles) for k in range(ntiles // 2)]
    from_odd = lax.ppermute(to_odd, "tiles", pairs + [(j, i) for i, j in pairs])
    atm_row_tiles = atm_cols // LANE
    early = min(EARLY, blocks)
    whole = blocks // PIECE
    nflux = forcing.shape[0]
    pick, keys, slots, ids, field, scale, kappa, nu, to_even, again = call(
        functools.partial(
            stage_kernel, ntiles, main, atm_rows, atm_row_tiles, ocean_rows, row_tiles
        ),
        (
            shape((blocks, atm_tiles), BF16),
            shape((2, 1, blocks), jnp.int32),
            shape((ntiles * rows, blocks), BF16),
            shape((2, ntiles, LANE), F32),
            shape(atm_state.shape, F32),
            shape((1, LANE), F32),
            shape((1, atm_cols), F32),
            shape((row_tiles, LANE), F32),
            edges,
            shape((early, LANE, LANE), BF16),
        ),
        [SMEM, VMEM, VMEM] + [HBM] * 9,
        1 << 20,
        [
            pltpu.VMEM((3, 1, blocks), jnp.int32),
            pltpu.VMEM((2, 1, nflux), F32),
            pltpu.VMEM(forcing.shape, BF16),
            pltpu.SemaphoreType.DMA((8,)),
            pltpu.SemaphoreType.DMA((early // PIECE,)),
        ],
    )(
        me_arr,
        atm,
        ocean,
        remap_source.reshape(1, blocks),
        remap_owner.reshape(1, blocks),
        remap_dest.reshape(1, blocks),
        flux_gain.reshape(1, nflux),
        flux_coef.reshape(1, nflux),
        atm_kappa.reshape(1, atm_cols),
        ocean_nu.reshape(row_tiles, LANE),
        forcing,
        remap_weight,
    )
    from_even = lax.ppermute(to_even, "tiles", [(i, i ^ 1) for i in range(ntiles)])
    atm_next, outgoing = call(
        functools.partial(forward_kernel, ntiles, main),
        (shape(atm_state.shape, F32), shape((ntiles * rows, LANE), BF16)),
        [SMEM] + [VMEM] * 11,
        1 << 28,
        [pltpu.VMEM((2 * atm_rows, atm_cols), F32)],
    )(me_arr, atm, kappa, from_even, from_odd, field, scale, pick, slots, ids, again,
      remap_weight)
    arrived = lax.all_to_all(outgoing, "tiles", split_axis=0, concat_axis=0, tiled=True)
    total = ocean_rows * row_tiles
    drive, side, slot_keys, to_pair = call(
        functools.partial(drive_kernel, ntiles, main, ocean_rows),
        (
            shape((total, LANE), F32),
            shape((EDGE, LANE), F32),
            shape((ntiles * main // LANE, LANE), jnp.int32),
            shape((row_tiles, LANE), F32),
        ),
        [SMEM, VMEM],
        1 << 27,
    )(me_arr, arrived)
    from_pair = lax.ppermute(to_pair, "tiles", [(i, i ^ 1) for i in range(ntiles)])
    value, take = call(
        functools.partial(ocean_kernel, ntiles),
        (shape((total, LANE), F32), shape((ntiles * main, total), BF16)),
        [SMEM] + [VMEM] * 7,
        1 << 31,
        [pltpu.VMEM((ocean_rows + 8, ocean_cols), F32)],
    )(me_arr, drive, side, slot_keys, ocean, nu, from_even, from_odd)
    cells, returned = call(
        functools.partial(return_kernel, ocean_rows),
        (shape((total, LANE), F32), shape((ntiles * main, LANE), BF16)),
        [SMEM] + [VMEM] * 4,
        1 << 27,
    )(me_arr, value, take, nu, from_pair)
    came_back = lax.all_to_all(returned, "tiles", split_axis=0, concat_axis=0, tiled=True)
    feedback, ocean_next, atm_out = call(
        backward_kernel,
        (
            shape(atm_state.shape, F32),
            shape(ocean_state.shape, F32),
            shape(atm_state.shape, F32),
        ),
        [VMEM] * 5 + [HBM],
        1 << 28,
        [
            pltpu.VMEM((blocks - early, LANE, LANE), BF16),
            pltpu.VMEM(ocean_state.shape, F32),
            pltpu.SemaphoreType.DMA(((blocks - early) // PIECE,)),
            pltpu.SemaphoreType.DMA((2,)),
        ],
        out_specs=(VMEM, HBM, HBM),
    )(came_back, keys, again, cells, atm_next, remap_weight)
    return (atm_out, ocean_next, feedback)


def solution(mesh):
    return jax.shard_map(
        per_device,
        mesh=mesh,
        in_specs=(
            P(("members", "tiles"), None),
            P(),
            P(None, ("members", "tiles"), None),
            P(),
            P("tiles", None, None),
            P("tiles"),
            P("tiles", None),
            P("tiles"),
            P(("members", "tiles"), None),
            P(),
            P(),
        ),
        out_specs=(
            P(("members", "tiles"), None),
            P(("members", "tiles"), None),
            P(("members", "tiles"), None),
        ),
        check_vma=False,
    )
```

```python
import functools

import jax
import jax.numpy as jnp
from jax import lax
from jax.experimental import pallas as pl
from jax.experimental.pallas import tpu as pltpu
from jax.sharding import PartitionSpec as P

LANE = 128
EDGE = 32
CHUNK = 8
PIECE = 32
EARLY = 96
F32 = jnp.float32
BF16 = jnp.bfloat16
VMEM = pl.BlockSpec(memory_space=pltpu.VMEM)
SMEM = pl.BlockSpec(memory_space=pltpu.SMEM)
HBM = pl.BlockSpec(memory_space=pltpu.HBM)


def iota(shape, dim):
    return lax.broadcasted_iota(jnp.int32, shape, dim)


def dot(a, b):
    return lax.dot_general(a, b, (((1,), (0,)), ((), ())), preferred_element_type=F32)


def dot_nt(a, b):
    return lax.dot_general(a, b, (((1,), (1,)), ((), ())), preferred_element_type=F32)


def onehot(mask):
    return jnp.where(mask, 1.0, 0.0).astype(BF16)


def as_column(row):
    parts = [
        jnp.transpose(jnp.broadcast_to(row[:, k : k + LANE], (LANE, LANE)))
        for k in range(0, row.shape[1], LANE)
    ]
    return jnp.concatenate(parts, axis=0)


def matches_lane(column, width):
    parts = [
        onehot(column == iota(column.shape, 1) + k)[:, : min(LANE, width - k)]
        for k in range(0, width, LANE)
    ]
    return jnp.concatenate(parts, axis=1)


def fetches(weight_hbm, first, held, sems):
    copies = []
    for n in range(held.shape[0] // PIECE):
        copies.append(
            pltpu.make_async_copy(
                weight_hbm.at[pl.ds(first + n * PIECE, PIECE)],
                held.at[pl.ds(n * PIECE, PIECE)],
                sems.at[n],
            )
        )
    return copies


def edge_rows(upper, atm_ref, ocean_ref, out_ref):
    start = 0
    for ref in (atm_ref, ocean_ref):
        rows, cols = ref.shape
        first, last = ref[0:2], ref[rows - 2 : rows]
        out_ref[:, start : start + cols] = jnp.where(upper, last, first)
        start += cols


def send_kernel(me_ref, atm_hbm, ocean_hbm, atm_ref, ocean_ref, odd_ref, sems):
    copies = [
        pltpu.make_async_copy(atm_hbm, atm_ref, sems.at[0]),
        pltpu.make_async_copy(ocean_hbm, ocean_ref, sems.at[1]),
    ]
    for copy in copies:
        copy.start()
    for copy in copies:
        copy.wait()
    edge_rows(me_ref[0] % 2 == 1, atm_ref, ocean_ref, odd_ref)


def stage_kernel(
    ntiles, main, atm_rows, atm_row_tiles, ocean_rows, row_tiles,
    me_ref, atm_ref, ocean_ref, src_hbm, own_hbm, dst_hbm, gain_hbm, coef_hbm, kappa_hbm, nu_hbm, forcing_hbm,
    weight_hbm, pick_ref, keys_ref, slots_ref, ids_ref, field_ref, scale_ref, kappa_ref, nu_ref,
    even_ref, early_ref,
    ints, gains, forcing_ref, sems, early_sems,
):
    small = [
        (src_hbm, ints.at[0]), (own_hbm, ints.at[1]), (dst_hbm, ints.at[2]),
        (gain_hbm, gains.at[0]), (coef_hbm, gains.at[1]), (forcing_hbm, forcing_ref),
        (kappa_hbm, kappa_ref), (nu_hbm, nu_ref),
    ]
    copies = [pltpu.make_async_copy(a, b, sems.at[k]) for k, (a, b) in enumerate(small)]
    weights = fetches(weight_hbm, 0, early_ref, early_sems)
    for copy in copies + weights:
        copy.start()
    edge_rows(me_ref[0] % 2 == 0, atm_ref, ocean_ref, even_ref)
    for copy in copies[:3]:
        copy.wait()
    rows = main + EDGE
    per_lane = LANE // main
    source, owner, dest = ints[0], ints[1], ints[2]
    blocks = owner.shape[1]
    source = (source % atm_row_tiles) * atm_rows + source // atm_row_tiles
    row_of, col_of = dest // row_tiles, dest % row_tiles
    match = owner == iota((ntiles, blocks), 0)
    above = onehot(iota((blocks, blocks), 0) < iota((blocks, blocks), 1))
    rank = jnp.sum(
        jnp.where(match, dot(onehot(match), above), 0.0), axis=0, keepdims=True
    ).astype(jnp.int32)
    pick_ref[...] = matches_lane(as_column(source), pick_ref.shape[1])
    keys_ref[0] = source
    keys_ref[1] = owner * main + rank
    odd = owner % 2 == 1
    own_slot = owner * rows + rank
    beside = jnp.where(
        odd,
        (row_of - (ocean_rows - 1)) + jnp.where(owner < ntiles - 1, 0, 1),
        row_of + jnp.where(owner > 0, 0, 1),
    )
    side_slot = jnp.where(odd, owner + 1, owner - 1) * rows + main + col_of
    side_slot = jnp.where(beside == 0, side_slot, -1)
    for t in range(ntiles):
        slot = iota((rows, blocks), 0) + t * rows
        slots_ref[pl.ds(t * rows, rows), :] = onehot((slot == own_slot) | (slot == side_slot))
    lane_of = rank + (me_ref[0] % per_lane) * main
    place = onehot(lane_of == iota((LANE, blocks), 0))
    ids_ref[0] = dot_nt(jnp.where(match, (col_of + 1).astype(F32), 0.0).astype(BF16), place)
    ids_ref[1] = dot_nt(jnp.where(match, row_of.astype(F32), 0.0).astype(BF16), place)
    for copy in copies[3 : len(small)]:
        copy.wait()
    coef = gains[1]
    scale_ref[...] = jnp.broadcast_to(
        jnp.sum(gains[0] * coef, axis=1, keepdims=True), scale_ref.shape
    )
    field = jnp.zeros(field_ref.shape, F32)
    for k in range(forcing_ref.shape[0]):
        field = field + coef[:, k : k + 1] * forcing_ref[k].astype(F32)
    field_ref[...] = field
    for copy in weights:
        copy.wait()


def forward_kernel(
    ntiles, main, me_ref, atm_ref, kappa_ref, even_ref, odd_ref, field_ref, scale_ref,
    pick_ref, slots_ref, ids_ref, early_ref, weight_ref, next_ref, out_ref, work,
):
    atm_rows, cols = atm_ref.shape
    rows = main + EDGE
    even = me_ref[0] % 2 == 0
    ev, od = even_ref[:, :cols], odd_ref[:, :cols]
    size = 2 * atm_rows
    work[0:atm_rows] = atm_ref[...]
    work[atm_rows : 2 * atm_rows] = jnp.zeros((atm_rows, cols), F32)
    work[size - 2 : size] = jnp.where(even, od, ev)
    work[atm_rows : atm_rows + 2] = jnp.where(even, ev, od)
    x = work[...]
    kappa = kappa_ref[...]
    for _ in range(2):
        near = (
            pltpu.roll(x, 1, 0) + pltpu.roll(x, size - 1, 0)
            + pltpu.roll(x, 1, 1) + pltpu.roll(x, cols - 1, 1)
        )
        x = x + kappa * (near - 4.0 * x)
    atm = x[:atm_rows]
    next_ref[...] = atm
    field = field_ref[...] + scale_ref[:, 0:1] * atm
    tiles = jnp.concatenate(
        [field[:, c * LANE : (c + 1) * LANE] for c in range(cols // LANE)], axis=0
    ).astype(BF16)
    pieces = dot(pick_ref[...], tiles)
    blocks = pieces.shape[0]
    row = iota((CHUNK, LANE), 0)
    parts = []
    for n in range(blocks // CHUNK):
        piece = pieces[n * CHUNK : (n + 1) * CHUNK]
        spread = jnp.concatenate(
            [jnp.where(row == q, piece, 0.0) for q in range(CHUNK)], axis=1
        ).astype(BF16)
        held = early_ref if n * CHUNK < early_ref.shape[0] else weight_ref
        weight = held[pl.ds(n * CHUNK, CHUNK)].reshape(CHUNK * LANE, LANE)
        parts.append(dot(spread, weight))
    contribution = jnp.concatenate(parts, axis=0).astype(BF16)
    at = iota((EDGE, LANE), 0)
    for t in range(ntiles):
        sent = dot(slots_ref[pl.ds(t * rows, rows), :], contribution)
        low = sent[main:]
        low = jnp.where(at == EDGE - 4, ids_ref[0, t : t + 1, :], low)
        low = jnp.where(at == EDGE - 3, ids_ref[1, t : t + 1, :], low)
        out_ref[pl.ds(t * rows, main), :] = sent[:main].astype(BF16)
        out_ref[pl.ds(t * rows + main, EDGE), :] = low.astype(BF16)


def reverse_lanes(x):
    tiles = x.shape[1] // LANE
    back = LANE - 1 - iota((x.shape[0], LANE), 1)
    parts = [
        jnp.take_along_axis(x[:, c * LANE : (c + 1) * LANE], back, axis=1) for c in range(tiles)
    ]
    return jnp.concatenate(parts[::-1], axis=1)


def free_ocean(ntiles, me, ocean_ref, nu_ref, even_ref, odd_ref, work):
    rows, cols = ocean_ref.shape
    offset = even_ref.shape[1] - cols
    even, bottom, top = me % 2 == 0, me == 0, me == ntiles - 1
    ev, od = even_ref[:, offset:], odd_ref[:, offset:]
    size = rows + 8
    work[0:rows] = ocean_ref[...]
    work[rows:size] = jnp.zeros((8, cols), F32)
    work[size - 2 : size] = jnp.where(bottom, 0.0, jnp.where(even, od, ev))
    work[rows : rows + 2] = jnp.where(even, ev, od)
    nu = jnp.concatenate([nu_ref[c : c + 1] for c in range(cols // LANE)], axis=1)
    x = work[...]
    at = iota((size, cols), 0)
    for _ in range(2):
        folded = pltpu.roll(reverse_lanes(x[rows - 8 : rows]), 1, 0)
        tail = jnp.where(top & (iota((8, cols), 0) == 0), folded, x[rows:])
        x = jnp.concatenate([x[:rows], tail], axis=0)
        near = (
            pltpu.roll(x, 1, 0) + pltpu.roll(x, size - 1, 0)
            + pltpu.roll(x, 1, 1) + pltpu.roll(x, cols - 1, 1)
        )
        x = x + nu * (near - 4.0 * x)
        x = jnp.where(bottom & (at >= rows + 4), 0.0, x)
    return x[:rows]


def drive_kernel(ntiles, main, rows, me_ref, arrived_ref, drive_ref, side_ref, keys_ref, pair_ref):
    per_lane = LANE // main
    step = main + EDGE
    total = drive_ref.shape[0]
    row_tiles = total // rows
    drive = jnp.zeros((total, LANE), F32)
    side = jnp.zeros((EDGE, LANE), F32)
    for g in range(ntiles // per_lane):
        edge = jnp.zeros((EDGE, LANE), F32)
        values = []
        for s in range(g * per_lane, (g + 1) * per_lane):
            values.append(arrived_ref[pl.ds(s * step, main), :])
            edge = edge + arrived_ref[pl.ds(s * step + main, EDGE), :].astype(F32)
        side = side + edge
        key = (edge[EDGE - 4 : EDGE - 3] - 1.0) * rows + edge[EDGE - 3 : EDGE - 2]
        key = key.astype(jnp.int32)
        keys_ref[g : g + 1] = key
        drive = drive + dot(
            onehot(key == iota((total, LANE), 0)), jnp.concatenate(values, axis=0)
        )
    side_ref[...] = side
    drive_ref[...] = drive
    even = me_ref[0] % 2 == 0
    pair_ref[...] = jnp.where(
        even,
        drive_ref[pl.ds(rows - 1, row_tiles, stride=rows), :],
        drive_ref[pl.ds(0, row_tiles, stride=rows), :],
    )


def ocean_kernel(
    ntiles, me_ref, drive_ref, side_ref, keys_ref, ocean_ref, nu_ref, even_ref, odd_ref,
    value_ref, pick_ref, work,
):
    rows, cols = ocean_ref.shape
    free = free_ocean(ntiles, me_ref[0], ocean_ref, nu_ref, even_ref, odd_ref, work)
    row_tiles = cols // LANE
    total = rows * row_tiles
    even, top = me_ref[0] % 2 == 0, me_ref[0] == ntiles - 1
    drive, side = drive_ref[...], side_ref[...]
    tile = lambda c: drive[c * rows : (c + 1) * rows]
    spun = [pltpu.roll(tile(c), 1, 1) for c in range(row_tiles)]
    back = [pltpu.roll(tile(c), LANE - 1, 1) for c in range(row_tiles)]
    lane, at = iota((rows, LANE), 1), iota((rows, LANE), 0)
    turned = LANE - 1 - iota((8, LANE), 1)
    for c in range(row_tiles):
        d = tile(c)
        left = jnp.where(lane == 0, spun[c - 1], spun[c])
        right = jnp.where(lane == LANE - 1, back[(c + 1) % row_tiles], back[c])
        under_row = jnp.where(even, side[c : c + 1], 0.0)
        under = jnp.where(at == 0, under_row, pltpu.roll(d, 1, 0))
        fold = jnp.take_along_axis(tile(row_tiles - 1 - c)[rows - 8 :], turned, axis=1)[7:8]
        over_row = jnp.where(top, fold, jnp.where(even, 0.0, side[c : c + 1]))
        over = jnp.where(at == rows - 1, over_row, pltpu.roll(d, rows - 1, 0))
        near = under + over + left + right
        value_ref[c * rows : (c + 1) * rows] = free[:, c * LANE : (c + 1) * LANE] + (
            2.0 * d + nu_ref[c : c + 1] * (near - 4.0 * d)
        )
    for g in range(keys_ref.shape[0]):
        column = jnp.transpose(jnp.broadcast_to(keys_ref[g : g + 1], (LANE, LANE)))
        wide = jnp.concatenate([column] * -(-total // LANE), axis=1)[:, :total]
        pick_ref[pl.ds(g * LANE, LANE), :] = onehot(wide == iota((LANE, total), 1))


def return_kernel(rows, me_ref, value_ref, pick_ref, nu_ref, pair_ref, cells_ref, return_ref):
    row_tiles = nu_ref.shape[0]
    even = me_ref[0] % 2 == 0
    cells_ref[...] = value_ref[...]
    extra = nu_ref[...] * pair_ref[...]
    high, low = pl.ds(rows - 1, row_tiles, stride=rows), pl.ds(0, row_tiles, stride=rows)
    cells_ref[high, :] = cells_ref[high, :] + jnp.where(even, extra, 0.0)
    cells_ref[low, :] = cells_ref[low, :] + jnp.where(even, 0.0, extra)
    return_ref[...] = dot(pick_ref[...], cells_ref[...].astype(BF16)).astype(BF16)


def backward_kernel(
    came_ref, keys_ref, early_ref, cells_ref, atm_ref, weight_hbm,
    out_ref, next_hbm, atm_hbm, late_ref, next_ref, sems, out_sems,
):
    early = early_ref.shape[0]
    copies = fetches(weight_hbm, early, late_ref, sems)
    for copy in copies:
        copy.start()
    rows = next_ref.shape[0]
    for c in range(next_ref.shape[1] // LANE):
        next_ref[:, c * LANE : (c + 1) * LANE] = cells_ref[c * rows : (c + 1) * rows]
    written = [
        pltpu.make_async_copy(atm_ref, atm_hbm, out_sems.at[0]),
        pltpu.make_async_copy(next_ref, next_hbm, out_sems.at[1]),
    ]
    for copy in written:
        copy.start()
    values = dot(matches_lane(as_column(keys_ref[1]), came_ref.shape[0]), came_ref[...])
    blocks = values.shape[0]
    row = iota((CHUNK, LANE), 0)
    parts = []
    for n in range(blocks // CHUNK):
        value = values[n * CHUNK : (n + 1) * CHUNK].astype(BF16)
        at = n * CHUNK - early
        if at >= 0 and at % PIECE == 0:
            copies[at // PIECE].wait()
        held = early_ref[pl.ds(n * CHUNK, CHUNK)] if at < 0 else late_ref[pl.ds(at, CHUNK)]
        weight = held.reshape(CHUNK * LANE, LANE)
        full = dot_nt(value, weight)
        part = full[:, :LANE]
        for q in range(1, CHUNK):
            part = jnp.where(row == q, full[:, q * LANE : (q + 1) * LANE], part)
        parts.append(part)
    result = jnp.concatenate(parts, axis=0)
    coarse = result.astype(BF16)
    fine = (result - coarse.astype(F32)).astype(BF16)
    rows = out_ref.shape[0]
    total = rows * out_ref.shape[1] // LANE
    back = onehot(keys_ref[0] == iota((total, blocks), 0))
    tiles = dot(back, coarse) + dot(back, fine)
    for c in range(out_ref.shape[1] // LANE):
        out_ref[:, c * LANE : (c + 1) * LANE] = tiles[c * rows : (c + 1) * rows]
    for copy in written:
        copy.wait()


def call(kernel, outs, specs, cost, scratch=(), limit=24 << 20, out_specs=None):
    run = pl.pallas_call(
        kernel,
        out_shape=outs,
        in_specs=specs,
        out_specs=out_specs or jax.tree.map(lambda _: VMEM, outs),
        scratch_shapes=scratch,
        compiler_params=pltpu.CompilerParams(vmem_limit_bytes=limit),
        cost_estimate=pl.CostEstimate(flops=cost, bytes_accessed=cost // 64, transcendentals=0),
    )

    def placed(*args):
        return run(
            *[
                pltpu.with_memory_space_constraint(x, pltpu.HBM) if spec is HBM else x
                for x, spec in zip(args, specs)
            ]
        )

    return placed


def per_device(
    atm_state,
    atm_kappa,
    forcing,
    flux_gain,
    remap_weight,
    remap_source,
    remap_owner,
    remap_dest,
    ocean_state,
    ocean_nu,
    flux_coef,
):
    ntiles = lax.axis_size("tiles")
    me = lax.axis_index("tiles")
    blocks = remap_source.shape[0]
    capacity = max(2, 2 * blocks // ntiles)
    main = -(-capacity // 16) * 16
    rows = main + EDGE
    atm_rows, atm_cols = atm_state.shape
    ocean_rows, ocean_cols = ocean_state.shape
    atm_tiles = atm_rows * atm_cols // LANE
    row_tiles = ocean_cols // LANE
    shape = jax.ShapeDtypeStruct
    me_arr = me.astype(jnp.int32).reshape(1)
    edges = shape((2, atm_cols + ocean_cols), F32)
    atm, ocean, to_odd = call(
        send_kernel,
        (shape(atm_state.shape, F32), shape(ocean_state.shape, F32), edges),
        [SMEM, HBM, HBM],
        1 << 34,
        [pltpu.SemaphoreType.DMA((2,))],
    )(me_arr, atm_state, ocean_state)
    pairs = [(2 * k + 1, (2 * k + 2) % ntiles) for k in range(ntiles // 2)]
    from_odd = lax.ppermute(to_odd, "tiles", pairs + [(j, i) for i, j in pairs])
    atm_row_tiles = atm_cols // LANE
    early = min(EARLY, blocks)
    whole = blocks // PIECE
    nflux = forcing.shape[0]
    pick, keys, slots, ids, field, scale, kappa, nu, to_even, again = call(
        functools.partial(
            stage_kernel, ntiles, main, atm_rows, atm_row_tiles, ocean_rows, row_tiles
        ),
        (
            shape((blocks, atm_tiles), BF16),
            shape((2, 1, blocks), jnp.int32),
            shape((ntiles * rows, blocks), BF16),
            shape((2, ntiles, LANE), F32),
            shape(atm_state.shape, F32),
            shape((1, LANE), F32),
            shape((1, atm_cols), F32),
            shape((row_tiles, LANE), F32),
            edges,
            shape((early, LANE, LANE), BF16),
        ),
        [SMEM, VMEM, VMEM] + [HBM] * 9,
        1 << 20,
        [
            pltpu.VMEM((3, 1, blocks), jnp.int32),
            pltpu.VMEM((2, 1, nflux), F32),
            pltpu.VMEM(forcing.shape, BF16),
            pltpu.SemaphoreType.DMA((8,)),
            pltpu.SemaphoreType.DMA((early // PIECE,)),
        ],
    )(
        me_arr,
        atm,
        ocean,
        remap_source.reshape(1, blocks),
        remap_owner.reshape(1, blocks),
        remap_dest.reshape(1, blocks),
        flux_gain.reshape(1, nflux),
        flux_coef.reshape(1, nflux),
        atm_kappa.reshape(1, atm_cols),
        ocean_nu.reshape(row_tiles, LANE),
        forcing,
        remap_weight,
    )
    from_even = lax.ppermute(to_even, "tiles", [(i, i ^ 1) for i in range(ntiles)])
    atm_next, outgoing = call(
        functools.partial(forward_kernel, ntiles, main),
        (shape(atm_state.shape, F32), shape((ntiles * rows, LANE), BF16)),
        [SMEM] + [VMEM] * 11,
        1 << 28,
        [pltpu.VMEM((2 * atm_rows, atm_cols), F32)],
    )(me_arr, atm, kappa, from_even, from_odd, field, scale, pick, slots, ids, again,
      remap_weight)
    arrived = lax.all_to_all(outgoing, "tiles", split_axis=0, concat_axis=0, tiled=True)
    total = ocean_rows * row_tiles
    drive, side, slot_keys, to_pair = call(
        functools.partial(drive_kernel, ntiles, main, ocean_rows),
        (
            shape((total, LANE), F32),
            shape((EDGE, LANE), F32),
            shape((ntiles * main // LANE, LANE), jnp.int32),
            shape((row_tiles, LANE), F32),
        ),
        [SMEM, VMEM],
        1 << 27,
    )(me_arr, arrived)
    from_pair = lax.ppermute(to_pair, "tiles", [(i, i ^ 1) for i in range(ntiles)])
    value, take = call(
        functools.partial(ocean_kernel, ntiles),
        (shape((total, LANE), F32), shape((ntiles * main, total), BF16)),
        [SMEM] + [VMEM] * 7,
        1 << 31,
        [pltpu.VMEM((ocean_rows + 8, ocean_cols), F32)],
    )(me_arr, drive, side, slot_keys, ocean, nu, from_even, from_odd)
    cells, returned = call(
        functools.partial(return_kernel, ocean_rows),
        (shape((total, LANE), F32), shape((ntiles * main, LANE), BF16)),
        [SMEM] + [VMEM] * 4,
        1 << 27,
    )(me_arr, value, take, nu, from_pair)
    came_back = lax.all_to_all(returned, "tiles", split_axis=0, concat_axis=0, tiled=True)
    feedback, ocean_next, atm_out = call(
        backward_kernel,
        (
            shape(atm_state.shape, F32),
            shape(ocean_state.shape, F32),
            shape(atm_state.shape, F32),
        ),
        [VMEM] * 5 + [HBM],
        1 << 28,
        [
            pltpu.VMEM((blocks - early, LANE, LANE), BF16),
            pltpu.VMEM(ocean_state.shape, F32),
            pltpu.SemaphoreType.DMA(((blocks - early) // PIECE,)),
            pltpu.SemaphoreType.DMA((2,)),
        ],
        out_specs=(VMEM, HBM, HBM),
    )(came_back, keys, again, cells, atm_next, remap_weight)
    return (atm_out, ocean_next, feedback)


def solution(mesh):
    return jax.shard_map(
        per_device,
        mesh=mesh,
        in_specs=(
            P(("members", "tiles"), None),
            P(),
            P(None, ("members", "tiles"), None),
            P(),
            P("tiles", None, None),
            P("tiles"),
            P("tiles", None),
            P("tiles"),
            P(("members", "tiles"), None),
            P(),
            P(),
        ),
        out_specs=(
            P(("members", "tiles"), None),
            P(("members", "tiles"), None),
            P(("members", "tiles"), None),
        ),
        check_vma=False,
    )
```

```python
import functools

import jax
import jax.numpy as jnp
from jax import lax
from jax.experimental import pallas as pl
from jax.experimental.pallas import tpu as pltpu
from jax.sharding import PartitionSpec as P

LANE = 128
EDGE = 32
CHUNK = 8
F32 = jnp.float32
BF16 = jnp.bfloat16
VMEM = pl.BlockSpec(memory_space=pltpu.VMEM)
SMEM = pl.BlockSpec(memory_space=pltpu.SMEM)
HBM = pl.BlockSpec(memory_space=pltpu.HBM)


def iota(shape, dim):
    return lax.broadcasted_iota(jnp.int32, shape, dim)


def dot(a, b):
    return lax.dot_general(a, b, (((1,), (0,)), ((), ())), preferred_element_type=F32)


def dot_nt(a, b):
    return lax.dot_general(a, b, (((1,), (1,)), ((), ())), preferred_element_type=F32)


def onehot(mask):
    return jnp.where(mask, 1.0, 0.0).astype(BF16)


def as_column(row):
    parts = [
        jnp.transpose(jnp.broadcast_to(row[:, k : k + LANE], (LANE, LANE)))
        for k in range(0, row.shape[1], LANE)
    ]
    return jnp.concatenate(parts, axis=0)


def matches_lane(column, width):
    parts = [
        onehot(column == iota(column.shape, 1) + k)[:, : min(LANE, width - k)]
        for k in range(0, width, LANE)
    ]
    return jnp.concatenate(parts, axis=1)


def edge_rows(upper, atm_ref, ocean_ref, out_ref):
    start = 0
    for ref in (atm_ref, ocean_ref):
        rows, cols = ref.shape
        first, last = ref[0:2], ref[rows - 2 : rows]
        out_ref[:, start : start + cols] = jnp.where(upper, last, first)
        start += cols


def send_kernel(me_ref, atm_hbm, ocean_hbm, atm_ref, ocean_ref, odd_ref, sems):
    copies = [
        pltpu.make_async_copy(atm_hbm, atm_ref, sems.at[0]),
        pltpu.make_async_copy(ocean_hbm, ocean_ref, sems.at[1]),
    ]
    for copy in copies:
        copy.start()
    for copy in copies:
        copy.wait()
    edge_rows(me_ref[0] % 2 == 1, atm_ref, ocean_ref, odd_ref)


def stage_kernel(
    ntiles, main, atm_rows, atm_row_tiles, ocean_rows, row_tiles,
    me_ref, atm_ref, ocean_ref, src_hbm, own_hbm, dst_hbm, gain_hbm, coef_hbm, kappa_hbm, nu_hbm, forcing_hbm,
    pick_ref, keys_ref, slots_ref, ids_ref, field_ref, scale_ref, kappa_ref, nu_ref,
    even_ref,
    ints, gains, forcing_ref, sems,
):
    small = [
        (src_hbm, ints.at[0]), (own_hbm, ints.at[1]), (dst_hbm, ints.at[2]),
        (gain_hbm, gains.at[0]), (coef_hbm, gains.at[1]), (forcing_hbm, forcing_ref),
        (kappa_hbm, kappa_ref), (nu_hbm, nu_ref),
    ]
    copies = [pltpu.make_async_copy(a, b, sems.at[k]) for k, (a, b) in enumerate(small)]
    for copy in copies:
        copy.start()
    edge_rows(me_ref[0] % 2 == 0, atm_ref, ocean_ref, even_ref)
    for copy in copies[:3]:
        copy.wait()
    rows = main + EDGE
    per_lane = LANE // main
    source, owner, dest = ints[0], ints[1], ints[2]
    blocks = owner.shape[1]
    source = (source % atm_row_tiles) * atm_rows + source // atm_row_tiles
    row_of, col_of = dest // row_tiles, dest % row_tiles
    match = owner == iota((ntiles, blocks), 0)
    above = onehot(iota((blocks, blocks), 0) < iota((blocks, blocks), 1))
    rank = jnp.sum(
        jnp.where(match, dot(onehot(match), above), 0.0), axis=0, keepdims=True
    ).astype(jnp.int32)
    pick_ref[...] = matches_lane(as_column(source), pick_ref.shape[1])
    keys_ref[0] = source
    keys_ref[1] = owner * main + rank
    odd = owner % 2 == 1
    own_slot = owner * rows + rank
    beside = jnp.where(
        odd,
        (row_of - (ocean_rows - 1)) + jnp.where(owner < ntiles - 1, 0, 1),
        row_of + jnp.where(owner > 0, 0, 1),
    )
    side_slot = jnp.where(odd, owner + 1, owner - 1) * rows + main + col_of
    side_slot = jnp.where(beside == 0, side_slot, -1)
    for t in range(ntiles):
        slot = iota((rows, blocks), 0) + t * rows
        slots_ref[pl.ds(t * rows, rows), :] = onehot((slot == own_slot) | (slot == side_slot))
    lane_of = rank + (me_ref[0] % per_lane) * main
    place = onehot(lane_of == iota((LANE, blocks), 0))
    ids_ref[0] = dot_nt(jnp.where(match, (col_of + 1).astype(F32), 0.0).astype(BF16), place)
    ids_ref[1] = dot_nt(jnp.where(match, row_of.astype(F32), 0.0).astype(BF16), place)
    for copy in copies[3 : len(small)]:
        copy.wait()
    coef = gains[1]
    scale_ref[...] = jnp.broadcast_to(
        jnp.sum(gains[0] * coef, axis=1, keepdims=True), scale_ref.shape
    )
    field = jnp.zeros(field_ref.shape, F32)
    for k in range(forcing_ref.shape[0]):
        field = field + coef[:, k : k + 1] * forcing_ref[k].astype(F32)
    field_ref[...] = field


def forward_kernel(
    ntiles, main, me_ref, atm_ref, kappa_ref, even_ref, odd_ref, field_ref, scale_ref,
    pick_ref, slots_ref, ids_ref, weight_ref, next_ref, out_ref, work,
):
    atm_rows, cols = atm_ref.shape
    rows = main + EDGE
    even = me_ref[0] % 2 == 0
    ev, od = even_ref[:, :cols], odd_ref[:, :cols]
    size = 2 * atm_rows
    work[0:atm_rows] = atm_ref[...]
    work[atm_rows : 2 * atm_rows] = jnp.zeros((atm_rows, cols), F32)
    work[size - 2 : size] = jnp.where(even, od, ev)
    work[atm_rows : atm_rows + 2] = jnp.where(even, ev, od)
    x = work[...]
    kappa = kappa_ref[...]
    for _ in range(2):
        near = (
            pltpu.roll(x, 1, 0) + pltpu.roll(x, size - 1, 0)
            + pltpu.roll(x, 1, 1) + pltpu.roll(x, cols - 1, 1)
        )
        x = x + kappa * (near - 4.0 * x)
    atm = x[:atm_rows]
    next_ref[...] = atm
    field = field_ref[...] + scale_ref[:, 0:1] * atm
    tiles = jnp.concatenate(
        [field[:, c * LANE : (c + 1) * LANE] for c in range(cols // LANE)], axis=0
    ).astype(BF16)
    pieces = dot(pick_ref[...], tiles)
    blocks = pieces.shape[0]
    row = iota((CHUNK, LANE), 0)
    parts = []
    for n in range(blocks // CHUNK):
        piece = pieces[n * CHUNK : (n + 1) * CHUNK]
        spread = jnp.concatenate(
            [jnp.where(row == q, piece, 0.0) for q in range(CHUNK)], axis=1
        ).astype(BF16)
        weight = weight_ref[pl.ds(n * CHUNK, CHUNK)].reshape(CHUNK * LANE, LANE)
        parts.append(dot(spread, weight))
    contribution = jnp.concatenate(parts, axis=0).astype(BF16)
    at = iota((EDGE, LANE), 0)
    for t in range(ntiles):
        sent = dot(slots_ref[pl.ds(t * rows, rows), :], contribution)
        low = sent[main:]
        low = jnp.where(at == EDGE - 4, ids_ref[0, t : t + 1, :], low)
        low = jnp.where(at == EDGE - 3, ids_ref[1, t : t + 1, :], low)
        out_ref[pl.ds(t * rows, main), :] = sent[:main].astype(BF16)
        out_ref[pl.ds(t * rows + main, EDGE), :] = low.astype(BF16)


def reverse_lanes(x):
    tiles = x.shape[1] // LANE
    back = LANE - 1 - iota((x.shape[0], LANE), 1)
    parts = [
        jnp.take_along_axis(x[:, c * LANE : (c + 1) * LANE], back, axis=1) for c in range(tiles)
    ]
    return jnp.concatenate(parts[::-1], axis=1)


def free_ocean(ntiles, me, ocean_ref, nu_ref, even_ref, odd_ref, work):
    rows, cols = ocean_ref.shape
    offset = even_ref.shape[1] - cols
    even, bottom, top = me % 2 == 0, me == 0, me == ntiles - 1
    ev, od = even_ref[:, offset:], odd_ref[:, offset:]
    size = rows + 8
    work[0:rows] = ocean_ref[...]
    work[rows:size] = jnp.zeros((8, cols), F32)
    work[size - 2 : size] = jnp.where(bottom, 0.0, jnp.where(even, od, ev))
    work[rows : rows + 2] = jnp.where(even, ev, od)
    nu = jnp.concatenate([nu_ref[c : c + 1] for c in range(cols // LANE)], axis=1)
    x = work[...]
    at = iota((size, cols), 0)
    for _ in range(2):
        folded = pltpu.roll(reverse_lanes(x[rows - 8 : rows]), 1, 0)
        tail = jnp.where(top & (iota((8, cols), 0) == 0), folded, x[rows:])
        x = jnp.concatenate([x[:rows], tail], axis=0)
        near = (
            pltpu.roll(x, 1, 0) + pltpu.roll(x, size - 1, 0)
            + pltpu.roll(x, 1, 1) + pltpu.roll(x, cols - 1, 1)
        )
        x = x + nu * (near - 4.0 * x)
        x = jnp.where(bottom & (at >= rows + 4), 0.0, x)
    return x[:rows]


def drive_kernel(ntiles, main, rows, me_ref, arrived_ref, drive_ref, side_ref, keys_ref, pair_ref):
    per_lane = LANE // main
    step = main + EDGE
    total = drive_ref.shape[0]
    row_tiles = total // rows
    drive = jnp.zeros((total, LANE), F32)
    side = jnp.zeros((EDGE, LANE), F32)
    for g in range(ntiles // per_lane):
        edge = jnp.zeros((EDGE, LANE), F32)
        values = []
        for s in range(g * per_lane, (g + 1) * per_lane):
            values.append(arrived_ref[pl.ds(s * step, main), :])
            edge = edge + arrived_ref[pl.ds(s * step + main, EDGE), :].astype(F32)
        side = side + edge
        key = (edge[EDGE - 4 : EDGE - 3] - 1.0) * rows + edge[EDGE - 3 : EDGE - 2]
        key = key.astype(jnp.int32)
        keys_ref[g : g + 1] = key
        drive = drive + dot(
            onehot(key == iota((total, LANE), 0)), jnp.concatenate(values, axis=0)
        )
    side_ref[...] = side
    drive_ref[...] = drive
    even = me_ref[0] % 2 == 0
    pair_ref[...] = jnp.where(
        even,
        drive_ref[pl.ds(rows - 1, row_tiles, stride=rows), :],
        drive_ref[pl.ds(0, row_tiles, stride=rows), :],
    )


def ocean_kernel(
    ntiles, me_ref, drive_ref, side_ref, keys_ref, ocean_ref, nu_ref, even_ref, odd_ref,
    value_ref, pick_ref, work,
):
    rows, cols = ocean_ref.shape
    free = free_ocean(ntiles, me_ref[0], ocean_ref, nu_ref, even_ref, odd_ref, work)
    row_tiles = cols // LANE
    total = rows * row_tiles
    even, top = me_ref[0] % 2 == 0, me_ref[0] == ntiles - 1
    drive, side = drive_ref[...], side_ref[...]
    tile = lambda c: drive[c * rows : (c + 1) * rows]
    spun = [pltpu.roll(tile(c), 1, 1) for c in range(row_tiles)]
    back = [pltpu.roll(tile(c), LANE - 1, 1) for c in range(row_tiles)]
    lane, at = iota((rows, LANE), 1), iota((rows, LANE), 0)
    turned = LANE - 1 - iota((8, LANE), 1)
    for c in range(row_tiles):
        d = tile(c)
        left = jnp.where(lane == 0, spun[c - 1], spun[c])
        right = jnp.where(lane == LANE - 1, back[(c + 1) % row_tiles], back[c])
        under_row = jnp.where(even, side[c : c + 1], 0.0)
        under = jnp.where(at == 0, under_row, pltpu.roll(d, 1, 0))
        fold = jnp.take_along_axis(tile(row_tiles - 1 - c)[rows - 8 :], turned, axis=1)[7:8]
        over_row = jnp.where(top, fold, jnp.where(even, 0.0, side[c : c + 1]))
        over = jnp.where(at == rows - 1, over_row, pltpu.roll(d, rows - 1, 0))
        near = under + over + left + right
        value_ref[c * rows : (c + 1) * rows] = free[:, c * LANE : (c + 1) * LANE] + (
            2.0 * d + nu_ref[c : c + 1] * (near - 4.0 * d)
        )
    for g in range(keys_ref.shape[0]):
        column = jnp.transpose(jnp.broadcast_to(keys_ref[g : g + 1], (LANE, LANE)))
        wide = jnp.concatenate([column] * -(-total // LANE), axis=1)[:, :total]
        pick_ref[pl.ds(g * LANE, LANE), :] = onehot(wide == iota((LANE, total), 1))


def return_kernel(rows, me_ref, value_ref, pick_ref, nu_ref, pair_ref, cells_ref, return_ref):
    row_tiles = nu_ref.shape[0]
    even = me_ref[0] % 2 == 0
    cells_ref[...] = value_ref[...]
    extra = nu_ref[...] * pair_ref[...]
    high, low = pl.ds(rows - 1, row_tiles, stride=rows), pl.ds(0, row_tiles, stride=rows)
    cells_ref[high, :] = cells_ref[high, :] + jnp.where(even, extra, 0.0)
    cells_ref[low, :] = cells_ref[low, :] + jnp.where(even, 0.0, extra)
    return_ref[...] = dot(pick_ref[...], cells_ref[...].astype(BF16)).astype(BF16)


def backward_kernel(
    came_ref, keys_ref, cells_ref, atm_ref, weight_ref,
    out_ref, next_hbm, atm_hbm, next_ref, out_sems,
):
    rows = next_ref.shape[0]
    for c in range(next_ref.shape[1] // LANE):
        next_ref[:, c * LANE : (c + 1) * LANE] = cells_ref[c * rows : (c + 1) * rows]
    written = [
        pltpu.make_async_copy(atm_ref, atm_hbm, out_sems.at[0]),
        pltpu.make_async_copy(next_ref, next_hbm, out_sems.at[1]),
    ]
    for copy in written:
        copy.start()
    values = dot(matches_lane(as_column(keys_ref[1]), came_ref.shape[0]), came_ref[...])
    blocks = values.shape[0]
    row = iota((CHUNK, LANE), 0)
    parts = []
    for n in range(blocks // CHUNK):
        value = values[n * CHUNK : (n + 1) * CHUNK].astype(BF16)
        weight = weight_ref[pl.ds(n * CHUNK, CHUNK)].reshape(CHUNK * LANE, LANE)
        full = dot_nt(value, weight)
        part = full[:, :LANE]
        for q in range(1, CHUNK):
            part = jnp.where(row == q, full[:, q * LANE : (q + 1) * LANE], part)
        parts.append(part)
    result = jnp.concatenate(parts, axis=0)
    coarse = result.astype(BF16)
    fine = (result - coarse.astype(F32)).astype(BF16)
    rows = out_ref.shape[0]
    total = rows * out_ref.shape[1] // LANE
    back = onehot(keys_ref[0] == iota((total, blocks), 0))
    tiles = dot(back, coarse) + dot(back, fine)
    for c in range(out_ref.shape[1] // LANE):
        out_ref[:, c * LANE : (c + 1) * LANE] = tiles[c * rows : (c + 1) * rows]
    for copy in written:
        copy.wait()


def call(kernel, outs, specs, cost, scratch=(), limit=24 << 20, out_specs=None):
    run = pl.pallas_call(
        kernel,
        out_shape=outs,
        in_specs=specs,
        out_specs=out_specs or jax.tree.map(lambda _: VMEM, outs),
        scratch_shapes=scratch,
        compiler_params=pltpu.CompilerParams(vmem_limit_bytes=limit),
        cost_estimate=pl.CostEstimate(flops=cost, bytes_accessed=cost // 64, transcendentals=0),
    )

    def placed(*args):
        return run(
            *[
                pltpu.with_memory_space_constraint(x, pltpu.HBM) if spec is HBM else x
                for x, spec in zip(args, specs)
            ]
        )

    return placed


def per_device(
    atm_state,
    atm_kappa,
    forcing,
    flux_gain,
    remap_weight,
    remap_source,
    remap_owner,
    remap_dest,
    ocean_state,
    ocean_nu,
    flux_coef,
):
    ntiles = lax.axis_size("tiles")
    me = lax.axis_index("tiles")
    blocks = remap_source.shape[0]
    capacity = max(2, 2 * blocks // ntiles)
    main = -(-capacity // 16) * 16
    rows = main + EDGE
    atm_rows, atm_cols = atm_state.shape
    ocean_rows, ocean_cols = ocean_state.shape
    atm_tiles = atm_rows * atm_cols // LANE
    row_tiles = ocean_cols // LANE
    shape = jax.ShapeDtypeStruct
    me_arr = me.astype(jnp.int32).reshape(1)
    edges = shape((2, atm_cols + ocean_cols), F32)
    atm, ocean, to_odd = call(
        send_kernel,
        (shape(atm_state.shape, F32), shape(ocean_state.shape, F32), edges),
        [SMEM, HBM, HBM],
        1 << 34,
        [pltpu.SemaphoreType.DMA((2,))],
    )(me_arr, atm_state, ocean_state)
    pairs = [(2 * k + 1, (2 * k + 2) % ntiles) for k in range(ntiles // 2)]
    from_odd = lax.ppermute(to_odd, "tiles", pairs + [(j, i) for i, j in pairs])
    atm_row_tiles = atm_cols // LANE
    nflux = forcing.shape[0]
    pick, keys, slots, ids, field, scale, kappa, nu, to_even = call(
        functools.partial(
            stage_kernel, ntiles, main, atm_rows, atm_row_tiles, ocean_rows, row_tiles
        ),
        (
            shape((blocks, atm_tiles), BF16),
            shape((2, 1, blocks), jnp.int32),
            shape((ntiles * rows, blocks), BF16),
            shape((2, ntiles, LANE), F32),
            shape(atm_state.shape, F32),
            shape((1, LANE), F32),
            shape((1, atm_cols), F32),
            shape((row_tiles, LANE), F32),
            edges,
        ),
        [SMEM, VMEM, VMEM] + [HBM] * 8,
        1 << 20,
        [
            pltpu.VMEM((3, 1, blocks), jnp.int32),
            pltpu.VMEM((2, 1, nflux), F32),
            pltpu.VMEM(forcing.shape, BF16),
            pltpu.SemaphoreType.DMA((8,)),
        ],
    )(
        me_arr,
        atm,
        ocean,
        remap_source.reshape(1, blocks),
        remap_owner.reshape(1, blocks),
        remap_dest.reshape(1, blocks),
        flux_gain.reshape(1, nflux),
        flux_coef.reshape(1, nflux),
        atm_kappa.reshape(1, atm_cols),
        ocean_nu.reshape(row_tiles, LANE),
        forcing,
    )
    from_even = lax.ppermute(to_even, "tiles", [(i, i ^ 1) for i in range(ntiles)])
    atm_next, outgoing = call(
        functools.partial(forward_kernel, ntiles, main),
        (shape(atm_state.shape, F32), shape((ntiles * rows, LANE), BF16)),
        [SMEM] + [VMEM] * 10,
        1 << 28,
        [pltpu.VMEM((2 * atm_rows, atm_cols), F32)],
    )(me_arr, atm, kappa, from_even, from_odd, field, scale, pick, slots, ids, remap_weight)
    arrived = lax.all_to_all(outgoing, "tiles", split_axis=0, concat_axis=0, tiled=True)
    total = ocean_rows * row_tiles
    drive, side, slot_keys, to_pair = call(
        functools.partial(drive_kernel, ntiles, main, ocean_rows),
        (
            shape((total, LANE), F32),
            shape((EDGE, LANE), F32),
            shape((ntiles * main // LANE, LANE), jnp.int32),
            shape((row_tiles, LANE), F32),
        ),
        [SMEM, VMEM],
        1 << 27,
    )(me_arr, arrived)
    from_pair = lax.ppermute(to_pair, "tiles", [(i, i ^ 1) for i in range(ntiles)])
    value, take = call(
        functools.partial(ocean_kernel, ntiles),
        (shape((total, LANE), F32), shape((ntiles * main, total), BF16)),
        [SMEM] + [VMEM] * 7,
        1 << 31,
        [pltpu.VMEM((ocean_rows + 8, ocean_cols), F32)],
    )(me_arr, drive, side, slot_keys, ocean, nu, from_even, from_odd)
    cells, returned = call(
        functools.partial(return_kernel, ocean_rows),
        (shape((total, LANE), F32), shape((ntiles * main, LANE), BF16)),
        [SMEM] + [VMEM] * 4,
        1 << 27,
    )(me_arr, value, take, nu, from_pair)
    came_back = lax.all_to_all(returned, "tiles", split_axis=0, concat_axis=0, tiled=True)
    feedback, ocean_next, atm_out = call(
        backward_kernel,
        (
            shape(atm_state.shape, F32),
            shape(ocean_state.shape, F32),
            shape(atm_state.shape, F32),
        ),
        [VMEM] * 5,
        1 << 28,
        [pltpu.VMEM(ocean_state.shape, F32), pltpu.SemaphoreType.DMA((2,))],
        out_specs=(VMEM, HBM, HBM),
    )(came_back, keys, cells, atm_next, remap_weight)
    return (atm_out, ocean_next, feedback)


def solution(mesh):
    return jax.shard_map(
        per_device,
        mesh=mesh,
        in_specs=(
            P(("members", "tiles"), None),
            P(),
            P(None, ("members", "tiles"), None),
            P(),
            P("tiles", None, None),
            P("tiles"),
            P("tiles", None),
            P("tiles"),
            P(("members", "tiles"), None),
            P(),
            P(),
        ),
        out_specs=(
            P(("members", "tiles"), None),
            P(("members", "tiles"), None),
            P(("members", "tiles"), None),
        ),
        check_vma=False,
    )
```

```python
import functools

import jax
import jax.numpy as jnp
from jax import lax
from jax.experimental import pallas as pl
from jax.experimental.pallas import tpu as pltpu
from jax.sharding import PartitionSpec as P

LANE = 128
EDGE = 32
CHUNK = 8
TURNED = 4
F32 = jnp.float32
BF16 = jnp.bfloat16
VMEM = pl.BlockSpec(memory_space=pltpu.VMEM)
SMEM = pl.BlockSpec(memory_space=pltpu.SMEM)
HBM = pl.BlockSpec(memory_space=pltpu.HBM)


def iota(shape, dim):
    return lax.broadcasted_iota(jnp.int32, shape, dim)


def dot(a, b):
    return lax.dot_general(a, b, (((1,), (0,)), ((), ())), preferred_element_type=F32)


def dot_nt(a, b):
    return lax.dot_general(a, b, (((1,), (1,)), ((), ())), preferred_element_type=F32)


def onehot(mask):
    return jnp.where(mask, 1.0, 0.0).astype(BF16)


def as_column(row):
    parts = [
        jnp.transpose(jnp.broadcast_to(row[:, k : k + LANE], (LANE, LANE)))
        for k in range(0, row.shape[1], LANE)
    ]
    return jnp.concatenate(parts, axis=0)


def matches_lane(column, width):
    parts = [
        onehot(column == iota(column.shape, 1) + k)[:, : min(LANE, width - k)]
        for k in range(0, width, LANE)
    ]
    return jnp.concatenate(parts, axis=1)


def edge_rows(upper, atm_ref, ocean_ref, out_ref):
    start = 0
    for ref in (atm_ref, ocean_ref):
        rows, cols = ref.shape
        first, last = ref[0:2], ref[rows - 2 : rows]
        out_ref[:, start : start + cols] = jnp.where(upper, last, first)
        start += cols


def send_kernel(me_ref, atm_hbm, ocean_hbm, atm_ref, ocean_ref, odd_ref, sems):
    copies = [
        pltpu.make_async_copy(atm_hbm, atm_ref, sems.at[0]),
        pltpu.make_async_copy(ocean_hbm, ocean_ref, sems.at[1]),
    ]
    for copy in copies:
        copy.start()
    for copy in copies:
        copy.wait()
    edge_rows(me_ref[0] % 2 == 1, atm_ref, ocean_ref, odd_ref)


def stage_kernel(
    ntiles, main, atm_rows, atm_row_tiles, ocean_rows, row_tiles,
    me_ref, atm_ref, ocean_ref, src_hbm, own_hbm, dst_hbm, gain_hbm, coef_hbm, kappa_hbm, nu_hbm, forcing_hbm,
    pick_ref, keys_ref, slots_ref, ids_ref, field_ref, scale_ref, kappa_ref, nu_ref,
    even_ref,
    ints, gains, forcing_ref, sems,
):
    small = [
        (src_hbm, ints.at[0]), (own_hbm, ints.at[1]), (dst_hbm, ints.at[2]),
        (gain_hbm, gains.at[0]), (coef_hbm, gains.at[1]), (forcing_hbm, forcing_ref),
        (kappa_hbm, kappa_ref), (nu_hbm, nu_ref),
    ]
    copies = [pltpu.make_async_copy(a, b, sems.at[k]) for k, (a, b) in enumerate(small)]
    for copy in copies:
        copy.start()
    edge_rows(me_ref[0] % 2 == 0, atm_ref, ocean_ref, even_ref)
    for copy in copies[:3]:
        copy.wait()
    rows = main + EDGE
    per_lane = LANE // main
    source, owner, dest = ints[0], ints[1], ints[2]
    blocks = owner.shape[1]
    source = (source % atm_row_tiles) * atm_rows + source // atm_row_tiles
    row_of, col_of = dest // row_tiles, dest % row_tiles
    match = owner == iota((ntiles, blocks), 0)
    above = onehot(iota((blocks, blocks), 0) < iota((blocks, blocks), 1))
    rank = jnp.sum(
        jnp.where(match, dot(onehot(match), above), 0.0), axis=0, keepdims=True
    ).astype(jnp.int32)
    pick_ref[...] = matches_lane(as_column(source), pick_ref.shape[1])
    keys_ref[0] = source
    keys_ref[1] = owner * main + rank
    odd = owner % 2 == 1
    own_slot = owner * rows + rank
    beside = jnp.where(
        odd,
        (row_of - (ocean_rows - 1)) + jnp.where(owner < ntiles - 1, 0, 1),
        row_of + jnp.where(owner > 0, 0, 1),
    )
    side_slot = jnp.where(odd, owner + 1, owner - 1) * rows + main + col_of
    side_slot = jnp.where(beside == 0, side_slot, -1)
    for t in range(ntiles):
        slot = iota((rows, blocks), 0) + t * rows
        slots_ref[pl.ds(t * rows, rows), :] = onehot((slot == own_slot) | (slot == side_slot))
    lane_of = rank + (me_ref[0] % per_lane) * main
    place = onehot(lane_of == iota((LANE, blocks), 0))
    ids_ref[0] = dot_nt(jnp.where(match, (col_of + 1).astype(F32), 0.0).astype(BF16), place)
    ids_ref[1] = dot_nt(jnp.where(match, row_of.astype(F32), 0.0).astype(BF16), place)
    for copy in copies[3 : len(small)]:
        copy.wait()
    coef = gains[1]
    scale_ref[...] = jnp.broadcast_to(
        jnp.sum(gains[0] * coef, axis=1, keepdims=True), scale_ref.shape
    )
    field = jnp.zeros(field_ref.shape, F32)
    for k in range(forcing_ref.shape[0]):
        field = field + coef[:, k : k + 1] * forcing_ref[k].astype(F32)
    field_ref[...] = field


def spread(rows, count):
    row = iota((CHUNK, LANE), 0)
    return jnp.concatenate(
        [jnp.where(row == q, rows, 0.0) for q in range(count)], axis=1
    ).astype(BF16)


def forward_kernel(
    ntiles, main, me_ref, atm_ref, kappa_ref, even_ref, odd_ref, field_ref, scale_ref,
    pick_ref, slots_ref, ids_ref, weight_ref, next_ref, out_ref, work,
):
    atm_rows, cols = atm_ref.shape
    rows = main + EDGE
    even = me_ref[0] % 2 == 0
    ev, od = even_ref[:, :cols], odd_ref[:, :cols]
    size = 2 * atm_rows
    work[0:atm_rows] = atm_ref[...]
    work[atm_rows : 2 * atm_rows] = jnp.zeros((atm_rows, cols), F32)
    work[size - 2 : size] = jnp.where(even, od, ev)
    work[atm_rows : atm_rows + 2] = jnp.where(even, ev, od)
    x = work[...]
    kappa = kappa_ref[...]
    for _ in range(2):
        near = (
            pltpu.roll(x, 1, 0) + pltpu.roll(x, size - 1, 0)
            + pltpu.roll(x, 1, 1) + pltpu.roll(x, cols - 1, 1)
        )
        x = x + kappa * (near - 4.0 * x)
    atm = x[:atm_rows]
    next_ref[...] = atm
    field = field_ref[...] + scale_ref[:, 0:1] * atm
    tiles = jnp.concatenate(
        [field[:, c * LANE : (c + 1) * LANE] for c in range(cols // LANE)], axis=0
    ).astype(BF16)
    pieces = dot(pick_ref[...], tiles)
    blocks = pieces.shape[0]
    parts = []
    for n in range(blocks // CHUNK):
        piece = pieces[n * CHUNK : (n + 1) * CHUNK]
        rows_of = spread(piece, CHUNK)
        weight = weight_ref[pl.ds(n * CHUNK, CHUNK)].reshape(CHUNK * LANE, LANE)
        parts.append(dot(rows_of, weight))
    contribution = jnp.concatenate(parts, axis=0).astype(BF16)
    at = iota((EDGE, LANE), 0)
    for t in range(ntiles):
        sent = dot(slots_ref[pl.ds(t * rows, rows), :], contribution)
        low = sent[main:]
        low = jnp.where(at == EDGE - 4, ids_ref[0, t : t + 1, :], low)
        low = jnp.where(at == EDGE - 3, ids_ref[1, t : t + 1, :], low)
        out_ref[pl.ds(t * rows, main), :] = sent[:main].astype(BF16)
        out_ref[pl.ds(t * rows + main, EDGE), :] = low.astype(BF16)


def reverse_lanes(x):
    tiles = x.shape[1] // LANE
    back = LANE - 1 - iota((x.shape[0], LANE), 1)
    parts = [
        jnp.take_along_axis(x[:, c * LANE : (c + 1) * LANE], back, axis=1) for c in range(tiles)
    ]
    return jnp.concatenate(parts[::-1], axis=1)


def free_ocean(ntiles, me, ocean_ref, nu_ref, even_ref, odd_ref, work):
    rows, cols = ocean_ref.shape
    offset = even_ref.shape[1] - cols
    even, bottom, top = me % 2 == 0, me == 0, me == ntiles - 1
    ev, od = even_ref[:, offset:], odd_ref[:, offset:]
    size = rows + 8
    work[0:rows] = ocean_ref[...]
    work[rows:size] = jnp.zeros((8, cols), F32)
    work[size - 2 : size] = jnp.where(bottom, 0.0, jnp.where(even, od, ev))
    work[rows : rows + 2] = jnp.where(even, ev, od)
    nu = jnp.concatenate([nu_ref[c : c + 1] for c in range(cols // LANE)], axis=1)
    x = work[...]
    at = iota((size, cols), 0)
    for _ in range(2):
        folded = pltpu.roll(reverse_lanes(x[rows - 8 : rows]), 1, 0)
        tail = jnp.where(top & (iota((8, cols), 0) == 0), folded, x[rows:])
        x = jnp.concatenate([x[:rows], tail], axis=0)
        near = (
            pltpu.roll(x, 1, 0) + pltpu.roll(x, size - 1, 0)
            + pltpu.roll(x, 1, 1) + pltpu.roll(x, cols - 1, 1)
        )
        x = x + nu * (near - 4.0 * x)
        x = jnp.where(bottom & (at >= rows + 4), 0.0, x)
    return x[:rows]


def drive_kernel(ntiles, main, rows, me_ref, arrived_ref, drive_ref, side_ref, keys_ref, pair_ref):
    per_lane = LANE // main
    step = main + EDGE
    total = drive_ref.shape[0]
    row_tiles = total // rows
    drive = jnp.zeros((total, LANE), F32)
    side = jnp.zeros((EDGE, LANE), F32)
    for g in range(ntiles // per_lane):
        edge = jnp.zeros((EDGE, LANE), F32)
        values = []
        for s in range(g * per_lane, (g + 1) * per_lane):
            values.append(arrived_ref[pl.ds(s * step, main), :])
            edge = edge + arrived_ref[pl.ds(s * step + main, EDGE), :].astype(F32)
        side = side + edge
        key = (edge[EDGE - 4 : EDGE - 3] - 1.0) * rows + edge[EDGE - 3 : EDGE - 2]
        key = key.astype(jnp.int32)
        keys_ref[g : g + 1] = key
        drive = drive + dot(
            onehot(key == iota((total, LANE), 0)), jnp.concatenate(values, axis=0)
        )
    side_ref[...] = side
    drive_ref[...] = drive
    even = me_ref[0] % 2 == 0
    pair_ref[...] = jnp.where(
        even,
        drive_ref[pl.ds(rows - 1, row_tiles, stride=rows), :],
        drive_ref[pl.ds(0, row_tiles, stride=rows), :],
    )


def ocean_kernel(
    ntiles, me_ref, drive_ref, side_ref, keys_ref, ocean_ref, nu_ref, even_ref, odd_ref,
    value_ref, pick_ref, work,
):
    rows, cols = ocean_ref.shape
    free = free_ocean(ntiles, me_ref[0], ocean_ref, nu_ref, even_ref, odd_ref, work)
    row_tiles = cols // LANE
    total = rows * row_tiles
    even, top = me_ref[0] % 2 == 0, me_ref[0] == ntiles - 1
    drive, side = drive_ref[...], side_ref[...]
    tile = lambda c: drive[c * rows : (c + 1) * rows]
    spun = [pltpu.roll(tile(c), 1, 1) for c in range(row_tiles)]
    back = [pltpu.roll(tile(c), LANE - 1, 1) for c in range(row_tiles)]
    lane, at = iota((rows, LANE), 1), iota((rows, LANE), 0)
    turned = LANE - 1 - iota((8, LANE), 1)
    for c in range(row_tiles):
        d = tile(c)
        left = jnp.where(lane == 0, spun[c - 1], spun[c])
        right = jnp.where(lane == LANE - 1, back[(c + 1) % row_tiles], back[c])
        under_row = jnp.where(even, side[c : c + 1], 0.0)
        under = jnp.where(at == 0, under_row, pltpu.roll(d, 1, 0))
        fold = jnp.take_along_axis(tile(row_tiles - 1 - c)[rows - 8 :], turned, axis=1)[7:8]
        over_row = jnp.where(top, fold, jnp.where(even, 0.0, side[c : c + 1]))
        over = jnp.where(at == rows - 1, over_row, pltpu.roll(d, rows - 1, 0))
        near = under + over + left + right
        value_ref[c * rows : (c + 1) * rows] = free[:, c * LANE : (c + 1) * LANE] + (
            2.0 * d + nu_ref[c : c + 1] * (near - 4.0 * d)
        )
    for g in range(keys_ref.shape[0]):
        column = jnp.transpose(jnp.broadcast_to(keys_ref[g : g + 1], (LANE, LANE)))
        wide = jnp.concatenate([column] * -(-total // LANE), axis=1)[:, :total]
        pick_ref[pl.ds(g * LANE, LANE), :] = onehot(wide == iota((LANE, total), 1))


def return_kernel(rows, me_ref, value_ref, pick_ref, nu_ref, pair_ref, cells_ref, return_ref):
    row_tiles = nu_ref.shape[0]
    even = me_ref[0] % 2 == 0
    cells_ref[...] = value_ref[...]
    extra = nu_ref[...] * pair_ref[...]
    high, low = pl.ds(rows - 1, row_tiles, stride=rows), pl.ds(0, row_tiles, stride=rows)
    cells_ref[high, :] = cells_ref[high, :] + jnp.where(even, extra, 0.0)
    cells_ref[low, :] = cells_ref[low, :] + jnp.where(even, 0.0, extra)
    return_ref[...] = dot(pick_ref[...], cells_ref[...].astype(BF16)).astype(BF16)


def backward_kernel(
    came_ref, keys_ref, cells_ref, atm_ref, weight_ref,
    out_ref, next_hbm, atm_hbm, next_ref, out_sems,
):
    rows = next_ref.shape[0]
    for c in range(next_ref.shape[1] // LANE):
        next_ref[:, c * LANE : (c + 1) * LANE] = cells_ref[c * rows : (c + 1) * rows]
    written = [
        pltpu.make_async_copy(atm_ref, atm_hbm, out_sems.at[0]),
        pltpu.make_async_copy(next_ref, next_hbm, out_sems.at[1]),
    ]
    for copy in written:
        copy.start()
    values = dot(matches_lane(as_column(keys_ref[1]), came_ref.shape[0]), came_ref[...])
    blocks = values.shape[0]
    row = iota((CHUNK, LANE), 0)
    parts = []
    for n in range(blocks // CHUNK):
        value = values[n * CHUNK : (n + 1) * CHUNK]
        turned = jnp.concatenate(
            [jnp.transpose(weight_ref[n * CHUNK + q]) for q in range(TURNED)], axis=0
        )
        part = dot(spread(value, TURNED), turned)
        weight = weight_ref[pl.ds(n * CHUNK + TURNED, CHUNK - TURNED)]
        full = dot_nt(value.astype(BF16), weight.reshape((CHUNK - TURNED) * LANE, LANE))
        for q in range(TURNED, CHUNK):
            k = (q - TURNED) * LANE
            part = jnp.where(row == q, full[:, k : k + LANE], part)
        parts.append(part)
    result = jnp.concatenate(parts, axis=0)
    coarse = result.astype(BF16)
    fine = (result - coarse.astype(F32)).astype(BF16)
    rows = out_ref.shape[0]
    total = rows * out_ref.shape[1] // LANE
    back = onehot(keys_ref[0] == iota((total, blocks), 0))
    tiles = dot(back, coarse) + dot(back, fine)
    for c in range(out_ref.shape[1] // LANE):
        out_ref[:, c * LANE : (c + 1) * LANE] = tiles[c * rows : (c + 1) * rows]
    for copy in written:
        copy.wait()


def call(kernel, outs, specs, cost, scratch=(), limit=24 << 20, out_specs=None):
    run = pl.pallas_call(
        kernel,
        out_shape=outs,
        in_specs=specs,
        out_specs=out_specs or jax.tree.map(lambda _: VMEM, outs),
        scratch_shapes=scratch,
        compiler_params=pltpu.CompilerParams(vmem_limit_bytes=limit),
        cost_estimate=pl.CostEstimate(flops=cost, bytes_accessed=cost // 64, transcendentals=0),
    )

    def placed(*args):
        return run(
            *[
                pltpu.with_memory_space_constraint(x, pltpu.HBM) if spec is HBM else x
                for x, spec in zip(args, specs)
            ]
        )

    return placed


def per_device(
    atm_state,
    atm_kappa,
    forcing,
    flux_gain,
    remap_weight,
    remap_source,
    remap_owner,
    remap_dest,
    ocean_state,
    ocean_nu,
    flux_coef,
):
    ntiles = lax.axis_size("tiles")
    me = lax.axis_index("tiles")
    blocks = remap_source.shape[0]
    capacity = max(2, 2 * blocks // ntiles)
    main = -(-capacity // 16) * 16
    rows = main + EDGE
    atm_rows, atm_cols = atm_state.shape
    ocean_rows, ocean_cols = ocean_state.shape
    atm_tiles = atm_rows * atm_cols // LANE
    row_tiles = ocean_cols // LANE
    shape = jax.ShapeDtypeStruct
    me_arr = me.astype(jnp.int32).reshape(1)
    edges = shape((2, atm_cols + ocean_cols), F32)
    atm, ocean, to_odd = call(
        send_kernel,
        (shape(atm_state.shape, F32), shape(ocean_state.shape, F32), edges),
        [SMEM, HBM, HBM],
        1 << 34,
        [pltpu.SemaphoreType.DMA((2,))],
    )(me_arr, atm_state, ocean_state)
    pairs = [(2 * k + 1, (2 * k + 2) % ntiles) for k in range(ntiles // 2)]
    from_odd = lax.ppermute(to_odd, "tiles", pairs + [(j, i) for i, j in pairs])
    atm_row_tiles = atm_cols // LANE
    nflux = forcing.shape[0]
    pick, keys, slots, ids, field, scale, kappa, nu, to_even = call(
        functools.partial(
            stage_kernel, ntiles, main, atm_rows, atm_row_tiles, ocean_rows, row_tiles
        ),
        (
            shape((blocks, atm_tiles), BF16),
            shape((2, 1, blocks), jnp.int32),
            shape((ntiles * rows, blocks), BF16),
            shape((2, ntiles, LANE), F32),
            shape(atm_state.shape, F32),
            shape((1, LANE), F32),
            shape((1, atm_cols), F32),
            shape((row_tiles, LANE), F32),
            edges,
        ),
        [SMEM, VMEM, VMEM] + [HBM] * 8,
        1 << 20,
        [
            pltpu.VMEM((3, 1, blocks), jnp.int32),
            pltpu.VMEM((2, 1, nflux), F32),
            pltpu.VMEM(forcing.shape, BF16),
            pltpu.SemaphoreType.DMA((8,)),
        ],
    )(
        me_arr,
        atm,
        ocean,
        remap_source.reshape(1, blocks),
        remap_owner.reshape(1, blocks),
        remap_dest.reshape(1, blocks),
        flux_gain.reshape(1, nflux),
        flux_coef.reshape(1, nflux),
        atm_kappa.reshape(1, atm_cols),
        ocean_nu.reshape(row_tiles, LANE),
        forcing,
    )
    from_even = lax.ppermute(to_even, "tiles", [(i, i ^ 1) for i in range(ntiles)])
    atm_next, outgoing = call(
        functools.partial(forward_kernel, ntiles, main),
        (shape(atm_state.shape, F32), shape((ntiles * rows, LANE), BF16)),
        [SMEM] + [VMEM] * 10,
        1 << 28,
        [pltpu.VMEM((2 * atm_rows, atm_cols), F32)],
    )(me_arr, atm, kappa, from_even, from_odd, field, scale, pick, slots, ids, remap_weight)
    arrived = lax.all_to_all(outgoing, "tiles", split_axis=0, concat_axis=0, tiled=True)
    total = ocean_rows * row_tiles
    drive, side, slot_keys, to_pair = call(
        functools.partial(drive_kernel, ntiles, main, ocean_rows),
        (
            shape((total, LANE), F32),
            shape((EDGE, LANE), F32),
            shape((ntiles * main // LANE, LANE), jnp.int32),
            shape((row_tiles, LANE), F32),
        ),
        [SMEM, VMEM],
        1 << 27,
    )(me_arr, arrived)
    from_pair = lax.ppermute(to_pair, "tiles", [(i, i ^ 1) for i in range(ntiles)])
    value, take = call(
        functools.partial(ocean_kernel, ntiles),
        (shape((total, LANE), F32), shape((ntiles * main, total), BF16)),
        [SMEM] + [VMEM] * 7,
        1 << 31,
        [pltpu.VMEM((ocean_rows + 8, ocean_cols), F32)],
    )(me_arr, drive, side, slot_keys, ocean, nu, from_even, from_odd)
    cells, returned = call(
        functools.partial(return_kernel, ocean_rows),
        (shape((total, LANE), F32), shape((ntiles * main, LANE), BF16)),
        [SMEM] + [VMEM] * 4,
        1 << 27,
    )(me_arr, value, take, nu, from_pair)
    came_back = lax.all_to_all(returned, "tiles", split_axis=0, concat_axis=0, tiled=True)
    feedback, ocean_next, atm_out = call(
        backward_kernel,
        (
            shape(atm_state.shape, F32),
            shape(ocean_state.shape, F32),
            shape(atm_state.shape, F32),
        ),
        [VMEM] * 5,
        1 << 28,
        [pltpu.VMEM(ocean_state.shape, F32), pltpu.SemaphoreType.DMA((2,))],
        out_specs=(VMEM, HBM, HBM),
    )(came_back, keys, cells, atm_next, remap_weight)
    return (atm_out, ocean_next, feedback)


def solution(mesh):
    return jax.shard_map(
        per_device,
        mesh=mesh,
        in_specs=(
            P(("members", "tiles"), None),
            P(),
            P(None, ("members", "tiles"), None),
            P(),
            P("tiles", None, None),
            P("tiles"),
            P("tiles", None),
            P("tiles"),
            P(("members", "tiles"), None),
            P(),
            P(),
        ),
        out_specs=(
            P(("members", "tiles"), None),
            P(("members", "tiles"), None),
            P(("members", "tiles"), None),
        ),
        check_vma=False,
    )
```

```python
import functools

import jax
import jax.numpy as jnp
from jax import lax
from jax.experimental import pallas as pl
from jax.experimental.pallas import tpu as pltpu
from jax.sharding import PartitionSpec as P

LANE = 128
EDGE = 32
CHUNK = 8
TURNED = 6
F32 = jnp.float32
BF16 = jnp.bfloat16
VMEM = pl.BlockSpec(memory_space=pltpu.VMEM)
SMEM = pl.BlockSpec(memory_space=pltpu.SMEM)
HBM = pl.BlockSpec(memory_space=pltpu.HBM)


def iota(shape, dim):
    return lax.broadcasted_iota(jnp.int32, shape, dim)


def dot(a, b):
    return lax.dot_general(a, b, (((1,), (0,)), ((), ())), preferred_element_type=F32)


def dot_nt(a, b):
    return lax.dot_general(a, b, (((1,), (1,)), ((), ())), preferred_element_type=F32)


def onehot(mask):
    return jnp.where(mask, 1.0, 0.0).astype(BF16)


def as_column(row):
    parts = [
        jnp.transpose(jnp.broadcast_to(row[:, k : k + LANE], (LANE, LANE)))
        for k in range(0, row.shape[1], LANE)
    ]
    return jnp.concatenate(parts, axis=0)


def matches_lane(column, width):
    parts = [
        onehot(column == iota(column.shape, 1) + k)[:, : min(LANE, width - k)]
        for k in range(0, width, LANE)
    ]
    return jnp.concatenate(parts, axis=1)


def edge_rows(upper, atm_ref, ocean_ref, out_ref):
    start = 0
    for ref in (atm_ref, ocean_ref):
        rows, cols = ref.shape
        first, last = ref[0:2], ref[rows - 2 : rows]
        out_ref[:, start : start + cols] = jnp.where(upper, last, first)
        start += cols


def send_kernel(me_ref, atm_hbm, ocean_hbm, atm_ref, ocean_ref, odd_ref, sems):
    copies = [
        pltpu.make_async_copy(atm_hbm, atm_ref, sems.at[0]),
        pltpu.make_async_copy(ocean_hbm, ocean_ref, sems.at[1]),
    ]
    for copy in copies:
        copy.start()
    for copy in copies:
        copy.wait()
    edge_rows(me_ref[0] % 2 == 1, atm_ref, ocean_ref, odd_ref)


def stage_kernel(
    ntiles, main, atm_rows, atm_row_tiles, ocean_rows, row_tiles,
    me_ref, atm_ref, ocean_ref, src_hbm, own_hbm, dst_hbm, gain_hbm, coef_hbm, kappa_hbm, nu_hbm, forcing_hbm,
    pick_ref, keys_ref, slots_ref, ids_ref, field_ref, scale_ref, kappa_ref, nu_ref,
    even_ref,
    ints, gains, forcing_ref, sems,
):
    small = [
        (src_hbm, ints.at[0]), (own_hbm, ints.at[1]), (dst_hbm, ints.at[2]),
        (gain_hbm, gains.at[0]), (coef_hbm, gains.at[1]), (forcing_hbm, forcing_ref),
        (kappa_hbm, kappa_ref), (nu_hbm, nu_ref),
    ]
    copies = [pltpu.make_async_copy(a, b, sems.at[k]) for k, (a, b) in enumerate(small)]
    for copy in copies:
        copy.start()
    edge_rows(me_ref[0] % 2 == 0, atm_ref, ocean_ref, even_ref)
    for copy in copies[:3]:
        copy.wait()
    rows = main + EDGE
    per_lane = LANE // main
    source, owner, dest = ints[0], ints[1], ints[2]
    blocks = owner.shape[1]
    source = (source % atm_row_tiles) * atm_rows + source // atm_row_tiles
    row_of, col_of = dest // row_tiles, dest % row_tiles
    match = owner == iota((ntiles, blocks), 0)
    above = onehot(iota((blocks, blocks), 0) < iota((blocks, blocks), 1))
    rank = jnp.sum(
        jnp.where(match, dot(onehot(match), above), 0.0), axis=0, keepdims=True
    ).astype(jnp.int32)
    pick_ref[...] = matches_lane(as_column(source), pick_ref.shape[1])
    keys_ref[0] = source
    keys_ref[1] = owner * main + rank
    odd = owner % 2 == 1
    own_slot = owner * rows + rank
    beside = jnp.where(
        odd,
        (row_of - (ocean_rows - 1)) + jnp.where(owner < ntiles - 1, 0, 1),
        row_of + jnp.where(owner > 0, 0, 1),
    )
    side_slot = jnp.where(odd, owner + 1, owner - 1) * rows + main + col_of
    side_slot = jnp.where(beside == 0, side_slot, -1)
    for t in range(ntiles):
        slot = iota((rows, blocks), 0) + t * rows
        slots_ref[pl.ds(t * rows, rows), :] = onehot((slot == own_slot) | (slot == side_slot))
    lane_of = rank + (me_ref[0] % per_lane) * main
    place = onehot(lane_of == iota((LANE, blocks), 0))
    ids_ref[0] = dot_nt(jnp.where(match, (col_of + 1).astype(F32), 0.0).astype(BF16), place)
    ids_ref[1] = dot_nt(jnp.where(match, row_of.astype(F32), 0.0).astype(BF16), place)
    for copy in copies[3 : len(small)]:
        copy.wait()
    coef = gains[1]
    scale_ref[...] = jnp.broadcast_to(
        jnp.sum(gains[0] * coef, axis=1, keepdims=True), scale_ref.shape
    )
    field = jnp.zeros(field_ref.shape, F32)
    for k in range(forcing_ref.shape[0]):
        field = field + coef[:, k : k + 1] * forcing_ref[k].astype(F32)
    field_ref[...] = field


def spread(rows, count):
    row = iota((CHUNK, LANE), 0)
    return jnp.concatenate(
        [jnp.where(row == q, rows, 0.0) for q in range(count)], axis=1
    ).astype(BF16)


def forward_kernel(
    ntiles, main, me_ref, atm_ref, kappa_ref, even_ref, odd_ref, field_ref, scale_ref,
    pick_ref, slots_ref, ids_ref, weight_ref, next_ref, out_ref, work,
):
    atm_rows, cols = atm_ref.shape
    rows = main + EDGE
    even = me_ref[0] % 2 == 0
    ev, od = even_ref[:, :cols], odd_ref[:, :cols]
    size = 2 * atm_rows
    work[0:atm_rows] = atm_ref[...]
    work[atm_rows : 2 * atm_rows] = jnp.zeros((atm_rows, cols), F32)
    work[size - 2 : size] = jnp.where(even, od, ev)
    work[atm_rows : atm_rows + 2] = jnp.where(even, ev, od)
    x = work[...]
    kappa = kappa_ref[...]
    for _ in range(2):
        near = (
            pltpu.roll(x, 1, 0) + pltpu.roll(x, size - 1, 0)
            + pltpu.roll(x, 1, 1) + pltpu.roll(x, cols - 1, 1)
        )
        x = x + kappa * (near - 4.0 * x)
    atm = x[:atm_rows]
    next_ref[...] = atm
    field = field_ref[...] + scale_ref[:, 0:1] * atm
    tiles = jnp.concatenate(
        [field[:, c * LANE : (c + 1) * LANE] for c in range(cols // LANE)], axis=0
    ).astype(BF16)
    pieces = dot(pick_ref[...], tiles)
    blocks = pieces.shape[0]
    parts = []
    for n in range(blocks // CHUNK):
        piece = pieces[n * CHUNK : (n + 1) * CHUNK]
        rows_of = spread(piece, CHUNK)
        weight = weight_ref[pl.ds(n * CHUNK, CHUNK)].reshape(CHUNK * LANE, LANE)
        parts.append(dot(rows_of, weight))
    contribution = jnp.concatenate(parts, axis=0).astype(BF16)
    at = iota((EDGE, LANE), 0)
    for t in range(ntiles):
        sent = dot(slots_ref[pl.ds(t * rows, rows), :], contribution)
        low = sent[main:]
        low = jnp.where(at == EDGE - 4, ids_ref[0, t : t + 1, :], low)
        low = jnp.where(at == EDGE - 3, ids_ref[1, t : t + 1, :], low)
        out_ref[pl.ds(t * rows, main), :] = sent[:main].astype(BF16)
        out_ref[pl.ds(t * rows + main, EDGE), :] = low.astype(BF16)


def reverse_lanes(x):
    tiles = x.shape[1] // LANE
    back = LANE - 1 - iota((x.shape[0], LANE), 1)
    parts = [
        jnp.take_along_axis(x[:, c * LANE : (c + 1) * LANE], back, axis=1) for c in range(tiles)
    ]
    return jnp.concatenate(parts[::-1], axis=1)


def free_ocean(ntiles, me, ocean_ref, nu_ref, even_ref, odd_ref, work):
    rows, cols = ocean_ref.shape
    offset = even_ref.shape[1] - cols
    even, bottom, top = me % 2 == 0, me == 0, me == ntiles - 1
    ev, od = even_ref[:, offset:], odd_ref[:, offset:]
    size = rows + 8
    work[0:rows] = ocean_ref[...]
    work[rows:size] = jnp.zeros((8, cols), F32)
    work[size - 2 : size] = jnp.where(bottom, 0.0, jnp.where(even, od, ev))
    work[rows : rows + 2] = jnp.where(even, ev, od)
    nu = jnp.concatenate([nu_ref[c : c + 1] for c in range(cols // LANE)], axis=1)
    x = work[...]
    at = iota((size, cols), 0)
    for _ in range(2):
        folded = pltpu.roll(reverse_lanes(x[rows - 8 : rows]), 1, 0)
        tail = jnp.where(top & (iota((8, cols), 0) == 0), folded, x[rows:])
        x = jnp.concatenate([x[:rows], tail], axis=0)
        near = (
            pltpu.roll(x, 1, 0) + pltpu.roll(x, size - 1, 0)
            + pltpu.roll(x, 1, 1) + pltpu.roll(x, cols - 1, 1)
        )
        x = x + nu * (near - 4.0 * x)
        x = jnp.where(bottom & (at >= rows + 4), 0.0, x)
    return x[:rows]


def drive_kernel(ntiles, main, rows, me_ref, arrived_ref, drive_ref, side_ref, keys_ref, pair_ref):
    per_lane = LANE // main
    step = main + EDGE
    total = drive_ref.shape[0]
    row_tiles = total // rows
    drive = jnp.zeros((total, LANE), F32)
    side = jnp.zeros((EDGE, LANE), F32)
    for g in range(ntiles // per_lane):
        edge = jnp.zeros((EDGE, LANE), F32)
        values = []
        for s in range(g * per_lane, (g + 1) * per_lane):
            values.append(arrived_ref[pl.ds(s * step, main), :])
            edge = edge + arrived_ref[pl.ds(s * step + main, EDGE), :].astype(F32)
        side = side + edge
        key = (edge[EDGE - 4 : EDGE - 3] - 1.0) * rows + edge[EDGE - 3 : EDGE - 2]
        key = key.astype(jnp.int32)
        keys_ref[g : g + 1] = key
        drive = drive + dot(
            onehot(key == iota((total, LANE), 0)), jnp.concatenate(values, axis=0)
        )
    side_ref[...] = side
    drive_ref[...] = drive
    even = me_ref[0] % 2 == 0
    pair_ref[...] = jnp.where(
        even,
        drive_ref[pl.ds(rows - 1, row_tiles, stride=rows), :],
        drive_ref[pl.ds(0, row_tiles, stride=rows), :],
    )


def ocean_kernel(
    ntiles, me_ref, drive_ref, side_ref, keys_ref, ocean_ref, nu_ref, even_ref, odd_ref,
    value_ref, pick_ref, work,
):
    rows, cols = ocean_ref.shape
    free = free_ocean(ntiles, me_ref[0], ocean_ref, nu_ref, even_ref, odd_ref, work)
    row_tiles = cols // LANE
    total = rows * row_tiles
    even, top = me_ref[0] % 2 == 0, me_ref[0] == ntiles - 1
    drive, side = drive_ref[...], side_ref[...]
    tile = lambda c: drive[c * rows : (c + 1) * rows]
    spun = [pltpu.roll(tile(c), 1, 1) for c in range(row_tiles)]
    back = [pltpu.roll(tile(c), LANE - 1, 1) for c in range(row_tiles)]
    lane, at = iota((rows, LANE), 1), iota((rows, LANE), 0)
    turned = LANE - 1 - iota((8, LANE), 1)
    for c in range(row_tiles):
        d = tile(c)
        left = jnp.where(lane == 0, spun[c - 1], spun[c])
        right = jnp.where(lane == LANE - 1, back[(c + 1) % row_tiles], back[c])
        under_row = jnp.where(even, side[c : c + 1], 0.0)
        under = jnp.where(at == 0, under_row, pltpu.roll(d, 1, 0))
        fold = jnp.take_along_axis(tile(row_tiles - 1 - c)[rows - 8 :], turned, axis=1)[7:8]
        over_row = jnp.where(top, fold, jnp.where(even, 0.0, side[c : c + 1]))
        over = jnp.where(at == rows - 1, over_row, pltpu.roll(d, rows - 1, 0))
        near = under + over + left + right
        value_ref[c * rows : (c + 1) * rows] = free[:, c * LANE : (c + 1) * LANE] + (
            2.0 * d + nu_ref[c : c + 1] * (near - 4.0 * d)
        )
    for g in range(keys_ref.shape[0]):
        column = jnp.transpose(jnp.broadcast_to(keys_ref[g : g + 1], (LANE, LANE)))
        wide = jnp.concatenate([column] * -(-total // LANE), axis=1)[:, :total]
        pick_ref[pl.ds(g * LANE, LANE), :] = onehot(wide == iota((LANE, total), 1))


def return_kernel(rows, me_ref, value_ref, pick_ref, nu_ref, pair_ref, cells_ref, return_ref):
    row_tiles = nu_ref.shape[0]
    even = me_ref[0] % 2 == 0
    cells_ref[...] = value_ref[...]
    extra = nu_ref[...] * pair_ref[...]
    high, low = pl.ds(rows - 1, row_tiles, stride=rows), pl.ds(0, row_tiles, stride=rows)
    cells_ref[high, :] = cells_ref[high, :] + jnp.where(even, extra, 0.0)
    cells_ref[low, :] = cells_ref[low, :] + jnp.where(even, 0.0, extra)
    return_ref[...] = dot(pick_ref[...], cells_ref[...].astype(BF16)).astype(BF16)


def backward_kernel(
    came_ref, keys_ref, cells_ref, atm_ref, weight_ref,
    out_ref, next_hbm, atm_hbm, next_ref, out_sems,
):
    rows = next_ref.shape[0]
    for c in range(next_ref.shape[1] // LANE):
        next_ref[:, c * LANE : (c + 1) * LANE] = cells_ref[c * rows : (c + 1) * rows]
    written = [
        pltpu.make_async_copy(atm_ref, atm_hbm, out_sems.at[0]),
        pltpu.make_async_copy(next_ref, next_hbm, out_sems.at[1]),
    ]
    for copy in written:
        copy.start()
    values = dot(matches_lane(as_column(keys_ref[1]), came_ref.shape[0]), came_ref[...])
    blocks = values.shape[0]
    row = iota((CHUNK, LANE), 0)
    parts = []
    for n in range(blocks // CHUNK):
        value = values[n * CHUNK : (n + 1) * CHUNK]
        turned = jnp.concatenate(
            [jnp.transpose(weight_ref[n * CHUNK + q]) for q in range(TURNED)], axis=0
        )
        part = dot(spread(value, TURNED), turned)
        weight = weight_ref[pl.ds(n * CHUNK + TURNED, CHUNK - TURNED)]
        full = dot_nt(value.astype(BF16), weight.reshape((CHUNK - TURNED) * LANE, LANE))
        for q in range(TURNED, CHUNK):
            k = (q - TURNED) * LANE
            part = jnp.where(row == q, full[:, k : k + LANE], part)
        parts.append(part)
    result = jnp.concatenate(parts, axis=0)
    coarse = result.astype(BF16)
    fine = (result - coarse.astype(F32)).astype(BF16)
    rows = out_ref.shape[0]
    total = rows * out_ref.shape[1] // LANE
    back = onehot(keys_ref[0] == iota((total, blocks), 0))
    tiles = dot(back, coarse) + dot(back, fine)
    for c in range(out_ref.shape[1] // LANE):
        out_ref[:, c * LANE : (c + 1) * LANE] = tiles[c * rows : (c + 1) * rows]
    for copy in written:
        copy.wait()


def call(kernel, outs, specs, cost, scratch=(), limit=24 << 20, out_specs=None):
    run = pl.pallas_call(
        kernel,
        out_shape=outs,
        in_specs=specs,
        out_specs=out_specs or jax.tree.map(lambda _: VMEM, outs),
        scratch_shapes=scratch,
        compiler_params=pltpu.CompilerParams(vmem_limit_bytes=limit),
        cost_estimate=pl.CostEstimate(flops=cost, bytes_accessed=cost // 64, transcendentals=0),
    )

    def placed(*args):
        return run(
            *[
                pltpu.with_memory_space_constraint(x, pltpu.HBM) if spec is HBM else x
                for x, spec in zip(args, specs)
            ]
        )

    return placed


def per_device(
    atm_state,
    atm_kappa,
    forcing,
    flux_gain,
    remap_weight,
    remap_source,
    remap_owner,
    remap_dest,
    ocean_state,
    ocean_nu,
    flux_coef,
):
    ntiles = lax.axis_size("tiles")
    me = lax.axis_index("tiles")
    blocks = remap_source.shape[0]
    capacity = max(2, 2 * blocks // ntiles)
    main = -(-capacity // 16) * 16
    rows = main + EDGE
    atm_rows, atm_cols = atm_state.shape
    ocean_rows, ocean_cols = ocean_state.shape
    atm_tiles = atm_rows * atm_cols // LANE
    row_tiles = ocean_cols // LANE
    shape = jax.ShapeDtypeStruct
    me_arr = me.astype(jnp.int32).reshape(1)
    edges = shape((2, atm_cols + ocean_cols), F32)
    atm, ocean, to_odd = call(
        send_kernel,
        (shape(atm_state.shape, F32), shape(ocean_state.shape, F32), edges),
        [SMEM, HBM, HBM],
        1 << 34,
        [pltpu.SemaphoreType.DMA((2,))],
    )(me_arr, atm_state, ocean_state)
    pairs = [(2 * k + 1, (2 * k + 2) % ntiles) for k in range(ntiles // 2)]
    from_odd = lax.ppermute(to_odd, "tiles", pairs + [(j, i) for i, j in pairs])
    atm_row_tiles = atm_cols // LANE
    nflux = forcing.shape[0]
    pick, keys, slots, ids, field, scale, kappa, nu, to_even = call(
        functools.partial(
            stage_kernel, ntiles, main, atm_rows, atm_row_tiles, ocean_rows, row_tiles
        ),
        (
            shape((blocks, atm_tiles), BF16),
            shape((2, 1, blocks), jnp.int32),
            shape((ntiles * rows, blocks), BF16),
            shape((2, ntiles, LANE), F32),
            shape(atm_state.shape, F32),
            shape((1, LANE), F32),
            shape((1, atm_cols), F32),
            shape((row_tiles, LANE), F32),
            edges,
        ),
        [SMEM, VMEM, VMEM] + [HBM] * 8,
        1 << 20,
        [
            pltpu.VMEM((3, 1, blocks), jnp.int32),
            pltpu.VMEM((2, 1, nflux), F32),
            pltpu.VMEM(forcing.shape, BF16),
            pltpu.SemaphoreType.DMA((8,)),
        ],
    )(
        me_arr,
        atm,
        ocean,
        remap_source.reshape(1, blocks),
        remap_owner.reshape(1, blocks),
        remap_dest.reshape(1, blocks),
        flux_gain.reshape(1, nflux),
        flux_coef.reshape(1, nflux),
        atm_kappa.reshape(1, atm_cols),
        ocean_nu.reshape(row_tiles, LANE),
        forcing,
    )
    from_even = lax.ppermute(to_even, "tiles", [(i, i ^ 1) for i in range(ntiles)])
    atm_next, outgoing = call(
        functools.partial(forward_kernel, ntiles, main),
        (shape(atm_state.shape, F32), shape((ntiles * rows, LANE), BF16)),
        [SMEM] + [VMEM] * 10,
        1 << 28,
        [pltpu.VMEM((2 * atm_rows, atm_cols), F32)],
    )(me_arr, atm, kappa, from_even, from_odd, field, scale, pick, slots, ids, remap_weight)
    arrived = lax.all_to_all(outgoing, "tiles", split_axis=0, concat_axis=0, tiled=True)
    total = ocean_rows * row_tiles
    drive, side, slot_keys, to_pair = call(
        functools.partial(drive_kernel, ntiles, main, ocean_rows),
        (
            shape((total, LANE), F32),
            shape((EDGE, LANE), F32),
            shape((ntiles * main // LANE, LANE), jnp.int32),
            shape((row_tiles, LANE), F32),
        ),
        [SMEM, VMEM],
        1 << 27,
    )(me_arr, arrived)
    from_pair = lax.ppermute(to_pair, "tiles", [(i, i ^ 1) for i in range(ntiles)])
    value, take = call(
        functools.partial(ocean_kernel, ntiles),
        (shape((total, LANE), F32), shape((ntiles * main, total), BF16)),
        [SMEM] + [VMEM] * 7,
        1 << 31,
        [pltpu.VMEM((ocean_rows + 8, ocean_cols), F32)],
    )(me_arr, drive, side, slot_keys, ocean, nu, from_even, from_odd)
    cells, returned = call(
        functools.partial(return_kernel, ocean_rows),
        (shape((total, LANE), F32), shape((ntiles * main, LANE), BF16)),
        [SMEM] + [VMEM] * 4,
        1 << 27,
    )(me_arr, value, take, nu, from_pair)
    came_back = lax.all_to_all(returned, "tiles", split_axis=0, concat_axis=0, tiled=True)
    feedback, ocean_next, atm_out = call(
        backward_kernel,
        (
            shape(atm_state.shape, F32),
            shape(ocean_state.shape, F32),
            shape(atm_state.shape, F32),
        ),
        [VMEM] * 5,
        1 << 28,
        [pltpu.VMEM(ocean_state.shape, F32), pltpu.SemaphoreType.DMA((2,))],
        out_specs=(VMEM, HBM, HBM),
    )(came_back, keys, cells, atm_next, remap_weight)
    return (atm_out, ocean_next, feedback)


def solution(mesh):
    return jax.shard_map(
        per_device,
        mesh=mesh,
        in_specs=(
            P(("members", "tiles"), None),
            P(),
            P(None, ("members", "tiles"), None),
            P(),
            P("tiles", None, None),
            P("tiles"),
            P("tiles", None),
            P("tiles"),
            P(("members", "tiles"), None),
            P(),
            P(),
        ),
        out_specs=(
            P(("members", "tiles"), None),
            P(("members", "tiles"), None),
            P(("members", "tiles"), None),
        ),
        check_vma=False,
    )
```

```python
import functools

import jax
import jax.numpy as jnp
from jax import lax
from jax.experimental import pallas as pl
from jax.experimental.pallas import tpu as pltpu
from jax.sharding import PartitionSpec as P

LANE = 128
EDGE = 32
CHUNK = 16
TURNED = 12
F32 = jnp.float32
BF16 = jnp.bfloat16
VMEM = pl.BlockSpec(memory_space=pltpu.VMEM)
SMEM = pl.BlockSpec(memory_space=pltpu.SMEM)
HBM = pl.BlockSpec(memory_space=pltpu.HBM)


def iota(shape, dim):
    return lax.broadcasted_iota(jnp.int32, shape, dim)


def dot(a, b):
    return lax.dot_general(a, b, (((1,), (0,)), ((), ())), preferred_element_type=F32)


def dot_nt(a, b):
    return lax.dot_general(a, b, (((1,), (1,)), ((), ())), preferred_element_type=F32)


def onehot(mask):
    return jnp.where(mask, 1.0, 0.0).astype(BF16)


def as_column(row):
    parts = [
        jnp.transpose(jnp.broadcast_to(row[:, k : k + LANE], (LANE, LANE)))
        for k in range(0, row.shape[1], LANE)
    ]
    return jnp.concatenate(parts, axis=0)


def matches_lane(column, width):
    parts = [
        onehot(column == iota(column.shape, 1) + k)[:, : min(LANE, width - k)]
        for k in range(0, width, LANE)
    ]
    return jnp.concatenate(parts, axis=1)


def edge_rows(upper, atm_ref, ocean_ref, out_ref):
    start = 0
    for ref in (atm_ref, ocean_ref):
        rows, cols = ref.shape
        first, last = ref[0:2], ref[rows - 2 : rows]
        out_ref[:, start : start + cols] = jnp.where(upper, last, first)
        start += cols


def send_kernel(me_ref, atm_hbm, ocean_hbm, atm_ref, ocean_ref, odd_ref, sems):
    copies = [
        pltpu.make_async_copy(atm_hbm, atm_ref, sems.at[0]),
        pltpu.make_async_copy(ocean_hbm, ocean_ref, sems.at[1]),
    ]
    for copy in copies:
        copy.start()
    for copy in copies:
        copy.wait()
    edge_rows(me_ref[0] % 2 == 1, atm_ref, ocean_ref, odd_ref)


def stage_kernel(
    ntiles, main, atm_rows, atm_row_tiles, ocean_rows, row_tiles,
    me_ref, atm_ref, ocean_ref, src_hbm, own_hbm, dst_hbm, gain_hbm, coef_hbm, kappa_hbm, nu_hbm, forcing_hbm,
    pick_ref, keys_ref, slots_ref, ids_ref, field_ref, scale_ref, kappa_ref, nu_ref,
    even_ref,
    ints, gains, forcing_ref, sems,
):
    small = [
        (src_hbm, ints.at[0]), (own_hbm, ints.at[1]), (dst_hbm, ints.at[2]),
        (gain_hbm, gains.at[0]), (coef_hbm, gains.at[1]), (forcing_hbm, forcing_ref),
        (kappa_hbm, kappa_ref), (nu_hbm, nu_ref),
    ]
    copies = [pltpu.make_async_copy(a, b, sems.at[k]) for k, (a, b) in enumerate(small)]
    for copy in copies:
        copy.start()
    edge_rows(me_ref[0] % 2 == 0, atm_ref, ocean_ref, even_ref)
    for copy in copies[:3]:
        copy.wait()
    rows = main + EDGE
    per_lane = LANE // main
    source, owner, dest = ints[0], ints[1], ints[2]
    blocks = owner.shape[1]
    source = (source % atm_row_tiles) * atm_rows + source // atm_row_tiles
    row_of, col_of = dest // row_tiles, dest % row_tiles
    match = owner == iota((ntiles, blocks), 0)
    above = onehot(iota((blocks, blocks), 0) < iota((blocks, blocks), 1))
    rank = jnp.sum(
        jnp.where(match, dot(onehot(match), above), 0.0), axis=0, keepdims=True
    ).astype(jnp.int32)
    pick_ref[...] = matches_lane(as_column(source), pick_ref.shape[1])
    keys_ref[0] = source
    keys_ref[1] = owner * main + rank
    odd = owner % 2 == 1
    own_slot = owner * rows + rank
    beside = jnp.where(
        odd,
        (row_of - (ocean_rows - 1)) + jnp.where(owner < ntiles - 1, 0, 1),
        row_of + jnp.where(owner > 0, 0, 1),
    )
    side_slot = jnp.where(odd, owner + 1, owner - 1) * rows + main + col_of
    side_slot = jnp.where(beside == 0, side_slot, -1)
    for t in range(ntiles):
        slot = iota((rows, blocks), 0) + t * rows
        slots_ref[pl.ds(t * rows, rows), :] = onehot((slot == own_slot) | (slot == side_slot))
    lane_of = rank + (me_ref[0] % per_lane) * main
    place = onehot(lane_of == iota((LANE, blocks), 0))
    ids_ref[0] = dot_nt(jnp.where(match, (col_of + 1).astype(F32), 0.0).astype(BF16), place)
    ids_ref[1] = dot_nt(jnp.where(match, row_of.astype(F32), 0.0).astype(BF16), place)
    for copy in copies[3 : len(small)]:
        copy.wait()
    coef = gains[1]
    scale_ref[...] = jnp.broadcast_to(
        jnp.sum(gains[0] * coef, axis=1, keepdims=True), scale_ref.shape
    )
    field = jnp.zeros(field_ref.shape, F32)
    for k in range(forcing_ref.shape[0]):
        field = field + coef[:, k : k + 1] * forcing_ref[k].astype(F32)
    field_ref[...] = field


def spread(rows, count):
    row = iota((CHUNK, LANE), 0)
    return jnp.concatenate(
        [jnp.where(row == q, rows, 0.0) for q in range(count)], axis=1
    ).astype(BF16)


def forward_kernel(
    ntiles, main, me_ref, atm_ref, kappa_ref, even_ref, odd_ref, field_ref, scale_ref,
    pick_ref, slots_ref, ids_ref, weight_ref, next_ref, out_ref, work,
):
    atm_rows, cols = atm_ref.shape
    rows = main + EDGE
    even = me_ref[0] % 2 == 0
    ev, od = even_ref[:, :cols], odd_ref[:, :cols]
    size = 2 * atm_rows
    work[0:atm_rows] = atm_ref[...]
    work[atm_rows : 2 * atm_rows] = jnp.zeros((atm_rows, cols), F32)
    work[size - 2 : size] = jnp.where(even, od, ev)
    work[atm_rows : atm_rows + 2] = jnp.where(even, ev, od)
    x = work[...]
    kappa = kappa_ref[...]
    for _ in range(2):
        near = (
            pltpu.roll(x, 1, 0) + pltpu.roll(x, size - 1, 0)
            + pltpu.roll(x, 1, 1) + pltpu.roll(x, cols - 1, 1)
        )
        x = x + kappa * (near - 4.0 * x)
    atm = x[:atm_rows]
    next_ref[...] = atm
    field = field_ref[...] + scale_ref[:, 0:1] * atm
    tiles = jnp.concatenate(
        [field[:, c * LANE : (c + 1) * LANE] for c in range(cols // LANE)], axis=0
    ).astype(BF16)
    pieces = dot(pick_ref[...], tiles)
    blocks = pieces.shape[0]
    parts = []
    for n in range(blocks // CHUNK):
        piece = pieces[n * CHUNK : (n + 1) * CHUNK]
        rows_of = spread(piece, CHUNK)
        weight = weight_ref[pl.ds(n * CHUNK, CHUNK)].reshape(CHUNK * LANE, LANE)
        parts.append(dot(rows_of, weight))
    contribution = jnp.concatenate(parts, axis=0).astype(BF16)
    at = iota((EDGE, LANE), 0)
    for t in range(ntiles):
        sent = dot(slots_ref[pl.ds(t * rows, rows), :], contribution)
        low = sent[main:]
        low = jnp.where(at == EDGE - 4, ids_ref[0, t : t + 1, :], low)
        low = jnp.where(at == EDGE - 3, ids_ref[1, t : t + 1, :], low)
        out_ref[pl.ds(t * rows, main), :] = sent[:main].astype(BF16)
        out_ref[pl.ds(t * rows + main, EDGE), :] = low.astype(BF16)


def reverse_lanes(x):
    tiles = x.shape[1] // LANE
    back = LANE - 1 - iota((x.shape[0], LANE), 1)
    parts = [
        jnp.take_along_axis(x[:, c * LANE : (c + 1) * LANE], back, axis=1) for c in range(tiles)
    ]
    return jnp.concatenate(parts[::-1], axis=1)


def free_ocean(ntiles, me, ocean_ref, nu_ref, even_ref, odd_ref, work):
    rows, cols = ocean_ref.shape
    offset = even_ref.shape[1] - cols
    even, bottom, top = me % 2 == 0, me == 0, me == ntiles - 1
    ev, od = even_ref[:, offset:], odd_ref[:, offset:]
    size = rows + 8
    work[0:rows] = ocean_ref[...]
    work[rows:size] = jnp.zeros((8, cols), F32)
    work[size - 2 : size] = jnp.where(bottom, 0.0, jnp.where(even, od, ev))
    work[rows : rows + 2] = jnp.where(even, ev, od)
    nu = jnp.concatenate([nu_ref[c : c + 1] for c in range(cols // LANE)], axis=1)
    x = work[...]
    at = iota((size, cols), 0)
    for _ in range(2):
        folded = pltpu.roll(reverse_lanes(x[rows - 8 : rows]), 1, 0)
        tail = jnp.where(top & (iota((8, cols), 0) == 0), folded, x[rows:])
        x = jnp.concatenate([x[:rows], tail], axis=0)
        near = (
            pltpu.roll(x, 1, 0) + pltpu.roll(x, size - 1, 0)
            + pltpu.roll(x, 1, 1) + pltpu.roll(x, cols - 1, 1)
        )
        x = x + nu * (near - 4.0 * x)
        x = jnp.where(bottom & (at >= rows + 4), 0.0, x)
    return x[:rows]


def drive_kernel(ntiles, main, rows, me_ref, arrived_ref, drive_ref, side_ref, keys_ref, pair_ref):
    per_lane = LANE // main
    step = main + EDGE
    total = drive_ref.shape[0]
    row_tiles = total // rows
    drive = jnp.zeros((total, LANE), F32)
    side = jnp.zeros((EDGE, LANE), F32)
    for g in range(ntiles // per_lane):
        edge = jnp.zeros((EDGE, LANE), F32)
        values = []
        for s in range(g * per_lane, (g + 1) * per_lane):
            values.append(arrived_ref[pl.ds(s * step, main), :])
            edge = edge + arrived_ref[pl.ds(s * step + main, EDGE), :].astype(F32)
        side = side + edge
        key = (edge[EDGE - 4 : EDGE - 3] - 1.0) * rows + edge[EDGE - 3 : EDGE - 2]
        key = key.astype(jnp.int32)
        keys_ref[g : g + 1] = key
        drive = drive + dot(
            onehot(key == iota((total, LANE), 0)), jnp.concatenate(values, axis=0)
        )
    side_ref[...] = side
    drive_ref[...] = drive
    even = me_ref[0] % 2 == 0
    pair_ref[...] = jnp.where(
        even,
        drive_ref[pl.ds(rows - 1, row_tiles, stride=rows), :],
        drive_ref[pl.ds(0, row_tiles, stride=rows), :],
    )


def ocean_kernel(
    ntiles, me_ref, drive_ref, side_ref, keys_ref, ocean_ref, nu_ref, even_ref, odd_ref,
    value_ref, pick_ref, work,
):
    rows, cols = ocean_ref.shape
    free = free_ocean(ntiles, me_ref[0], ocean_ref, nu_ref, even_ref, odd_ref, work)
    row_tiles = cols // LANE
    total = rows * row_tiles
    even, top = me_ref[0] % 2 == 0, me_ref[0] == ntiles - 1
    drive, side = drive_ref[...], side_ref[...]
    tile = lambda c: drive[c * rows : (c + 1) * rows]
    spun = [pltpu.roll(tile(c), 1, 1) for c in range(row_tiles)]
    back = [pltpu.roll(tile(c), LANE - 1, 1) for c in range(row_tiles)]
    lane, at = iota((rows, LANE), 1), iota((rows, LANE), 0)
    turned = LANE - 1 - iota((8, LANE), 1)
    for c in range(row_tiles):
        d = tile(c)
        left = jnp.where(lane == 0, spun[c - 1], spun[c])
        right = jnp.where(lane == LANE - 1, back[(c + 1) % row_tiles], back[c])
        under_row = jnp.where(even, side[c : c + 1], 0.0)
        under = jnp.where(at == 0, under_row, pltpu.roll(d, 1, 0))
        fold = jnp.take_along_axis(tile(row_tiles - 1 - c)[rows - 8 :], turned, axis=1)[7:8]
        over_row = jnp.where(top, fold, jnp.where(even, 0.0, side[c : c + 1]))
        over = jnp.where(at == rows - 1, over_row, pltpu.roll(d, rows - 1, 0))
        near = under + over + left + right
        value_ref[c * rows : (c + 1) * rows] = free[:, c * LANE : (c + 1) * LANE] + (
            2.0 * d + nu_ref[c : c + 1] * (near - 4.0 * d)
        )
    for g in range(keys_ref.shape[0]):
        column = jnp.transpose(jnp.broadcast_to(keys_ref[g : g + 1], (LANE, LANE)))
        wide = jnp.concatenate([column] * -(-total // LANE), axis=1)[:, :total]
        pick_ref[pl.ds(g * LANE, LANE), :] = onehot(wide == iota((LANE, total), 1))


def return_kernel(rows, me_ref, value_ref, pick_ref, nu_ref, pair_ref, cells_ref, return_ref):
    row_tiles = nu_ref.shape[0]
    even = me_ref[0] % 2 == 0
    cells_ref[...] = value_ref[...]
    extra = nu_ref[...] * pair_ref[...]
    high, low = pl.ds(rows - 1, row_tiles, stride=rows), pl.ds(0, row_tiles, stride=rows)
    cells_ref[high, :] = cells_ref[high, :] + jnp.where(even, extra, 0.0)
    cells_ref[low, :] = cells_ref[low, :] + jnp.where(even, 0.0, extra)
    return_ref[...] = dot(pick_ref[...], cells_ref[...].astype(BF16)).astype(BF16)


def backward_kernel(
    came_ref, keys_ref, cells_ref, atm_ref, weight_ref,
    out_ref, next_hbm, atm_hbm, next_ref, out_sems,
):
    rows = next_ref.shape[0]
    for c in range(next_ref.shape[1] // LANE):
        next_ref[:, c * LANE : (c + 1) * LANE] = cells_ref[c * rows : (c + 1) * rows]
    written = [
        pltpu.make_async_copy(atm_ref, atm_hbm, out_sems.at[0]),
        pltpu.make_async_copy(next_ref, next_hbm, out_sems.at[1]),
    ]
    for copy in written:
        copy.start()
    values = dot(matches_lane(as_column(keys_ref[1]), came_ref.shape[0]), came_ref[...])
    blocks = values.shape[0]
    row = iota((CHUNK, LANE), 0)
    parts = []
    for n in range(blocks // CHUNK):
        value = values[n * CHUNK : (n + 1) * CHUNK]
        turned = jnp.concatenate(
            [jnp.transpose(weight_ref[n * CHUNK + q]) for q in range(TURNED)], axis=0
        )
        part = dot(spread(value, TURNED), turned)
        weight = weight_ref[pl.ds(n * CHUNK + TURNED, CHUNK - TURNED)]
        full = dot_nt(value.astype(BF16), weight.reshape((CHUNK - TURNED) * LANE, LANE))
        for q in range(TURNED, CHUNK):
            k = (q - TURNED) * LANE
            part = jnp.where(row == q, full[:, k : k + LANE], part)
        parts.append(part)
    result = jnp.concatenate(parts, axis=0)
    coarse = result.astype(BF16)
    fine = (result - coarse.astype(F32)).astype(BF16)
    rows = out_ref.shape[0]
    total = rows * out_ref.shape[1] // LANE
    back = onehot(keys_ref[0] == iota((total, blocks), 0))
    tiles = dot(back, coarse) + dot(back, fine)
    for c in range(out_ref.shape[1] // LANE):
        out_ref[:, c * LANE : (c + 1) * LANE] = tiles[c * rows : (c + 1) * rows]
    for copy in written:
        copy.wait()


def call(kernel, outs, specs, cost, scratch=(), limit=24 << 20, out_specs=None):
    run = pl.pallas_call(
        kernel,
        out_shape=outs,
        in_specs=specs,
        out_specs=out_specs or jax.tree.map(lambda _: VMEM, outs),
        scratch_shapes=scratch,
        compiler_params=pltpu.CompilerParams(vmem_limit_bytes=limit),
        cost_estimate=pl.CostEstimate(flops=cost, bytes_accessed=cost // 64, transcendentals=0),
    )

    def placed(*args):
        return run(
            *[
                pltpu.with_memory_space_constraint(x, pltpu.HBM) if spec is HBM else x
                for x, spec in zip(args, specs)
            ]
        )

    return placed


def per_device(
    atm_state,
    atm_kappa,
    forcing,
    flux_gain,
    remap_weight,
    remap_source,
    remap_owner,
    remap_dest,
    ocean_state,
    ocean_nu,
    flux_coef,
):
    ntiles = lax.axis_size("tiles")
    me = lax.axis_index("tiles")
    blocks = remap_source.shape[0]
    capacity = max(2, 2 * blocks // ntiles)
    main = -(-capacity // 16) * 16
    rows = main + EDGE
    atm_rows, atm_cols = atm_state.shape
    ocean_rows, ocean_cols = ocean_state.shape
    atm_tiles = atm_rows * atm_cols // LANE
    row_tiles = ocean_cols // LANE
    shape = jax.ShapeDtypeStruct
    me_arr = me.astype(jnp.int32).reshape(1)
    edges = shape((2, atm_cols + ocean_cols), F32)
    atm, ocean, to_odd = call(
        send_kernel,
        (shape(atm_state.shape, F32), shape(ocean_state.shape, F32), edges),
        [SMEM, HBM, HBM],
        1 << 34,
        [pltpu.SemaphoreType.DMA((2,))],
    )(me_arr, atm_state, ocean_state)
    pairs = [(2 * k + 1, (2 * k + 2) % ntiles) for k in range(ntiles // 2)]
    from_odd = lax.ppermute(to_odd, "tiles", pairs + [(j, i) for i, j in pairs])
    atm_row_tiles = atm_cols // LANE
    nflux = forcing.shape[0]
    pick, keys, slots, ids, field, scale, kappa, nu, to_even = call(
        functools.partial(
            stage_kernel, ntiles, main, atm_rows, atm_row_tiles, ocean_rows, row_tiles
        ),
        (
            shape((blocks, atm_tiles), BF16),
            shape((2, 1, blocks), jnp.int32),
            shape((ntiles * rows, blocks), BF16),
            shape((2, ntiles, LANE), F32),
            shape(atm_state.shape, F32),
            shape((1, LANE), F32),
            shape((1, atm_cols), F32),
            shape((row_tiles, LANE), F32),
            edges,
        ),
        [SMEM, VMEM, VMEM] + [HBM] * 8,
        1 << 20,
        [
            pltpu.VMEM((3, 1, blocks), jnp.int32),
            pltpu.VMEM((2, 1, nflux), F32),
            pltpu.VMEM(forcing.shape, BF16),
            pltpu.SemaphoreType.DMA((8,)),
        ],
    )(
        me_arr,
        atm,
        ocean,
        remap_source.reshape(1, blocks),
        remap_owner.reshape(1, blocks),
        remap_dest.reshape(1, blocks),
        flux_gain.reshape(1, nflux),
        flux_coef.reshape(1, nflux),
        atm_kappa.reshape(1, atm_cols),
        ocean_nu.reshape(row_tiles, LANE),
        forcing,
    )
    from_even = lax.ppermute(to_even, "tiles", [(i, i ^ 1) for i in range(ntiles)])
    atm_next, outgoing = call(
        functools.partial(forward_kernel, ntiles, main),
        (shape(atm_state.shape, F32), shape((ntiles * rows, LANE), BF16)),
        [SMEM] + [VMEM] * 10,
        1 << 28,
        [pltpu.VMEM((2 * atm_rows, atm_cols), F32)],
    )(me_arr, atm, kappa, from_even, from_odd, field, scale, pick, slots, ids, remap_weight)
    arrived = lax.all_to_all(outgoing, "tiles", split_axis=0, concat_axis=0, tiled=True)
    total = ocean_rows * row_tiles
    drive, side, slot_keys, to_pair = call(
        functools.partial(drive_kernel, ntiles, main, ocean_rows),
        (
            shape((total, LANE), F32),
            shape((EDGE, LANE), F32),
            shape((ntiles * main // LANE, LANE), jnp.int32),
            shape((row_tiles, LANE), F32),
        ),
        [SMEM, VMEM],
        1 << 27,
    )(me_arr, arrived)
    from_pair = lax.ppermute(to_pair, "tiles", [(i, i ^ 1) for i in range(ntiles)])
    value, take = call(
        functools.partial(ocean_kernel, ntiles),
        (shape((total, LANE), F32), shape((ntiles * main, total), BF16)),
        [SMEM] + [VMEM] * 7,
        1 << 31,
        [pltpu.VMEM((ocean_rows + 8, ocean_cols), F32)],
    )(me_arr, drive, side, slot_keys, ocean, nu, from_even, from_odd)
    cells, returned = call(
        functools.partial(return_kernel, ocean_rows),
        (shape((total, LANE), F32), shape((ntiles * main, LANE), BF16)),
        [SMEM] + [VMEM] * 4,
        1 << 27,
    )(me_arr, value, take, nu, from_pair)
    came_back = lax.all_to_all(returned, "tiles", split_axis=0, concat_axis=0, tiled=True)
    feedback, ocean_next, atm_out = call(
        backward_kernel,
        (
            shape(atm_state.shape, F32),
            shape(ocean_state.shape, F32),
            shape(atm_state.shape, F32),
        ),
        [VMEM] * 5,
        1 << 28,
        [pltpu.VMEM(ocean_state.shape, F32), pltpu.SemaphoreType.DMA((2,))],
        out_specs=(VMEM, HBM, HBM),
    )(came_back, keys, cells, atm_next, remap_weight)
    return (atm_out, ocean_next, feedback)


def solution(mesh):
    return jax.shard_map(
        per_device,
        mesh=mesh,
        in_specs=(
            P(("members", "tiles"), None),
            P(),
            P(None, ("members", "tiles"), None),
            P(),
            P("tiles", None, None),
            P("tiles"),
            P("tiles", None),
            P("tiles"),
            P(("members", "tiles"), None),
            P(),
            P(),
        ),
        out_specs=(
            P(("members", "tiles"), None),
            P(("members", "tiles"), None),
            P(("members", "tiles"), None),
        ),
        check_vma=False,
    )
```
